128 devices in a mesh: gx: 4 (over x_hi, core), gy: 8 (over x_lo, y), gz: 4 (over z).
Axes of the slice: x: 4 (x_hi: 2, x_lo: 2; x = x_hi * 2 + x_lo), y: 4, z: 4, core: 2. Of those that a mesh axis runs over, the one named last changes fastest.
Arguments:
- conc: float32 [128, 512, 1024], P('gx', 'gy', 'gz'), may hold values from 0.2 to 1
- load: float32 [128, 512, 1024], P('gx', 'gy', 'gz'), may hold values from 0 to 1
- adj_conc: float32 [128, 512, 1024], P('gx', 'gy', 'gz'), may hold values from -6 to 6
- adj_load: float32 [128, 512, 1024], P('gx', 'gy', 'gz'), may hold values from -6 to 6
- vel_x: float32 [128, 512, 1024], P('gx', 'gy', 'gz'), may hold values from -0.03 to 0.03
- vel_y: float32 [128, 512, 1024], P('gx', 'gy', 'gz'), may hold values from -0.03 to 0.03
- vel_z: float32 [128, 512, 1024], P('gx', 'gy', 'gz'), may hold values from -0.03 to 0.03
- solid: int32 [128, 512, 1024], P('gx', 'gy', 'gz'), may hold values 0 or 1
- voxel_slot: int32 [128, 512, 1024], P('gx', 'gy', 'gz'), may hold values from 0 to 4095
- slot_grain: int32 [128, 4096], P(('gx', 'gy', 'gz')), may hold values from 0 to 262143, as said below
- grain_home: int32 [262144], replicated, may hold values from 0 to 262143, as said below
- rates: float32 [262144], P(('gx', 'gy', 'gz')), may hold values from 0.01 to 0.2
Outputs:
- adj_conc_start: float32 [128, 512, 1024], P('gx', 'gy', 'gz')
- adj_load_start: float32 [128, 512, 1024], P('gx', 'gy', 'gz')
- rate_grad: float32 [262144], P(('gx', 'gy', 'gz'))
The draws below stay inside these ranges and needn't reach their ends.
Inputs may be any that keep to these rules, and one draw needn't show every extreme that they name: `slot_grain`: device block t's slots name grains t * 2048 to t * 2048 + 2 * 2048 - 1, taken modulo 262144, so a grain appears in the tables of neighbouring blocks. `grain_home`: A permutation of the 262144 places.
All inputs are finite; a program needn't handle non-finite values. No bound on the sum of `solid` on one device may be relied on, other than what follows from the above.
Results may differ from the reference program's by a relative error of at most 0.00013.
Values sent between devices are 32-bit elements; how exact they have to be, the bound alone decides.
A program may use at most 256 MiB of HBM per device.

```python
import math
import jax
import jax.numpy as jnp

CX = 32
CY = 64
CZ = 256
GPD = 2048
SLOTS = 4096
GRAINS = 262144
NX = 128
NY = 512
NZ = 1024
N_GY = 8
N_GZ = 4


def draw_slot_grain(key, part):
    key = jax.random.fold_in(key, 3)
    blocks = GRAINS // GPD
    offsets = jax.random.randint(key, (blocks, SLOTS), 0, 2 * GPD)
    offsets = offsets.at[:, 0].set(2 * GPD - 1)
    offsets = offsets.at[:, 1].set(GPD)
    starts = (jnp.arange(blocks) * GPD)[:, None]
    return ((starts + offsets) % GRAINS).astype(jnp.int32)


def draw_grain_home(key, part):
    key = jax.random.fold_in(key, 7)
    return jax.random.permutation(key, GRAINS).astype(jnp.int32)


def plant(entries, own_key, low, high):
    index_at = [jax.random.randint(jax.random.fold_in(own_key, axis), (), 0, length) for axis, length in enumerate(entries.shape)]
    main_axis = entries.shape.index(max(entries.shape))
    beside = index_at[:main_axis] + [(index_at[main_axis] + 1) % entries.shape[main_axis]] + index_at[main_axis + 1:]
    return entries.at[tuple(index_at)].set(low).at[tuple(beside)].set(high)


def level_of(rng, extent, shards, low, top_value):
    def one(dim, blocks):
        steps = jax.random.uniform(jax.random.fold_in(jax.random.fold_in(rng, 6), dim), (blocks,), jnp.float32, low / len(shards), top_value / len(shards))
        return jnp.repeat(jnp.exp(steps), extent[dim] // blocks).reshape((-1,) + (1,) * (len(extent) - dim - 1))

    gain = one(*shards[0])
    for cut in shards[1:]:
        gain = gain * one(*cut)
    return gain


def normal_values(own_key, shape, width, most, split=(), kind=jnp.bfloat16):
    values = jax.random.normal(own_key, shape, jnp.float32) * width
    if len(split) > 0:
        values = level_of(own_key, shape, split, -0.22, 0.18) * values
    return jnp.clip(values, min=-most, max=most).astype(kind)


def setup_inputs(seed: int = 0) -> dict:
    keys = jax.random.split(jax.random.key(seed), 13)
    return {
        "conc": jnp.clip(0.2 + 0.8 * jax.random.uniform(keys[0], (NX, NY, NZ), jnp.float32) ** level_of(keys[0], (NX, NY, NZ), ((0, 4), (1, 8), (2, 4)), -0.2, 0.2), 0.2, 1.0),
        "load": jnp.clip(1.0 * jax.random.uniform(keys[1], (NX, NY, NZ), jnp.float32) ** level_of(keys[1], (NX, NY, NZ), ((0, 4), (1, 8), (2, 4)), -0.2, 0.2), 0.0, 1.0),
        "adj_conc": normal_values(keys[2], (NX, NY, NZ), 1.0, 6.0, ((0, 4), (1, 8), (2, 4)), jnp.float32),
        "adj_load": normal_values(keys[3], (NX, NY, NZ), 1.0, 6.0, ((0, 4), (1, 8), (2, 4)), jnp.float32),
        "vel_x": jnp.clip(jax.random.uniform(keys[4], (NX, NY, NZ), jnp.float32, -0.03, 0.03) * level_of(keys[4], (NX, NY, NZ), ((0, 4), (1, 8), (2, 4)), -0.4, 0.0), -0.03, 0.03),
        "vel_y": jnp.clip(jax.random.uniform(keys[5], (NX, NY, NZ), jnp.float32, -0.03, 0.03) * level_of(keys[5], (NX, NY, NZ), ((0, 4), (1, 8), (2, 4)), -0.4, 0.0), -0.03, 0.03),
        "vel_z": jnp.clip(jax.random.uniform(keys[6], (NX, NY, NZ), jnp.float32, -0.03, 0.03) * level_of(keys[6], (NX, NY, NZ), ((0, 4), (1, 8), (2, 4)), -0.4, 0.0), -0.03, 0.03),
        "solid": plant((jax.random.randint(keys[7], (NX, NY, NZ), 0, 5) < 2).astype(jnp.int32), jax.random.fold_in(keys[7], 1), 0, 1),
        "voxel_slot": plant(jax.random.randint(keys[8], (NX, NY, NZ), 0, SLOTS), jax.random.fold_in(keys[8], 1), 0, SLOTS - 1).astype(jnp.int32),
        "slot_grain": draw_slot_grain(jax.random.fold_in(keys[12], 71), 0),
        "grain_home": draw_grain_home(jax.random.fold_in(keys[12], 71), 0),
        "rates": jnp.clip(jnp.exp(math.log(0.2) - 2.9957323 * jax.random.uniform(keys[11], (GRAINS,), jnp.float32) ** level_of(keys[11], (GRAINS,), ((0, 128),), -0.2, 0.2)), 0.01, 0.2),
    }


dispersion = 0.06


def neighbour(values, dimension, offset):
    spans = [slice(1, -1), slice(1, -1), slice(1, -1)]
    length = values.shape[dimension]
    spans[dimension] = slice(1 + offset, length - 1 + offset)
    return values[tuple(spans)]


def forward(conc_ext, load, weight_ext, speeds, kvox):
    centre = neighbour(conc_ext, 0, 0)
    weight = neighbour(weight_ext, 0, 0)
    spread = jnp.zeros_like(centre)
    transport = jnp.zeros_like(centre)
    for dimension in range(3):
        speed_ext = speeds[dimension]
        spread = spread + weight * neighbour(weight_ext, dimension, 1) * (neighbour(conc_ext, dimension, 1) - centre)
        spread = spread + weight * neighbour(weight_ext, dimension, -1) * (neighbour(conc_ext, dimension, -1) - centre)
        speed = neighbour(speed_ext, 0, 0)
        before = neighbour(speed_ext, dimension, -1)
        upper = jnp.maximum(speed, 0.0) * centre + jnp.minimum(speed, 0.0) * neighbour(conc_ext, dimension, 1)
        lower = jnp.maximum(before, 0.0) * neighbour(conc_ext, dimension, -1) + jnp.minimum(before, 0.0) * centre
        transport = transport + (lower - upper)
    uptake = kvox * (centre / (1.0 + centre) - load)
    return centre + dispersion * spread + transport - uptake, load + uptake


def adjoint(adj_ext, adj_load, conc, load, weight_ext, speeds, kvox):
    centre = neighbour(adj_ext, 0, 0)
    weight = neighbour(weight_ext, 0, 0)
    spread = jnp.zeros_like(centre)
    transport = jnp.zeros_like(centre)
    for dimension in range(3):
        speed_ext = speeds[dimension]
        spread = spread + weight * neighbour(weight_ext, dimension, 1) * (neighbour(adj_ext, dimension, 1) - centre)
        spread = spread + weight * neighbour(weight_ext, dimension, -1) * (neighbour(adj_ext, dimension, -1) - centre)
        speed = neighbour(speed_ext, 0, 0)
        before = neighbour(speed_ext, dimension, -1)
        transport = transport + jnp.maximum(speed, 0.0) * (neighbour(adj_ext, dimension, 1) - centre)
        transport = transport + jnp.minimum(before, 0.0) * (centre - neighbour(adj_ext, dimension, -1))
    differ = adj_load - centre
    denom = 1.0 + conc
    new_conc = centre + dispersion * spread + transport + kvox * differ / (denom * denom)
    new_load = adj_load - kvox * differ
    terms = (conc / denom - load) * differ
    return new_conc, new_load, terms


def reference(conc, load, adj_conc, adj_load, vel_x, vel_y, vel_z, solid, voxel_slot, slot_grain, grain_home, rates):
    def padded(values):
        return jnp.pad(values, 1)

    index_x = (jnp.arange(NX) // CX).astype(jnp.int32)[:, None, None]
    index_y = (jnp.arange(NY) // CY).astype(jnp.int32)[None, :, None]
    index_z = (jnp.arange(NZ) // CZ).astype(jnp.int32)[None, None, :]
    tile_index = (index_x * (N_GY * N_GZ) + index_y * N_GZ + index_z).astype(jnp.int32)
    tile_index = jnp.broadcast_to(tile_index, voxel_slot.shape)
    grain_label = slot_grain[tile_index, voxel_slot]
    places = grain_home[grain_label]
    solid_float = solid.astype(jnp.float32)
    weight = 1.0 - 0.7 * solid_float
    kvox = solid_float * rates[places]
    speeds = (padded(vel_x), padded(vel_y), padded(vel_z))
    weight_ext = padded(weight)
    conc_one, load_one = forward(padded(conc), load, weight_ext, speeds, kvox)
    adj_one, adj_load_one, late = adjoint(padded(adj_conc), adj_load, conc_one, load_one, weight_ext, speeds, kvox)
    adj_start, adj_load_start, early = adjoint(padded(adj_one), adj_load_one, conc, load, weight_ext, speeds, kvox)
    voxel_terms = solid_float * (early + late)
    rate_grad = jax.ops.segment_sum(voxel_terms.reshape(-1), places.reshape(-1), num_segments=GRAINS)
    return adj_start, adj_load_start, rate_grad
```

```python
import functools

import jax
import jax.numpy as jnp
from jax import lax
from jax.experimental import pallas as pl
from jax.experimental.pallas import tpu as pltpu
from jax.sharding import PartitionSpec as P

f32, bf16, i32 = jnp.float32, jnp.bfloat16, jnp.int32
MESH = pl.DeviceIdType.MESH
ANY = pl.BlockSpec(memory_space=pl.ANY)
dispersion = 0.06
rate_step = 0.2 / 65535.0
CX, CY, CZ = 32, 64, 256


def greet():
    barrier = pltpu.get_barrier_semaphore()
    for axis, count in (("gx", 4), ("gy", 8), ("gz", 4)):
        me = lax.axis_index(axis)
        for o in range(1, count):
            pl.semaphore_signal(
                barrier, inc=1, device_id={axis: lax.rem(me + o, count)}, device_id_type=MESH
            )
    pl.semaphore_wait(barrier, 13)


def gather_faces(
    conc, adj, vx, vy, vz, solid, rates,
    xlo, xlo_s, xhi, xhi_s, ylo, yhi, zlo, zhi, yown, zown, rall,
    ybuf, ysol, zbuf, zsol, yfwd, ybwd, zfwd, zbwd, lsem, rsem, osem, ssem, dsem,
):
    gx, gy, gz = (lax.axis_index(a) for a in ("gx", "gy", "gz"))
    xh, core = gx // 2, lax.rem(gx, 2)
    local = []
    pairs = ((conc, CY - 8), (adj, CY - 8), (vy, CY - 8), (conc, 0), (adj, 0))
    for k, (ref, start) in enumerate(pairs):
        local.append(pltpu.make_async_copy(ref.at[:, start:start + 8, :], ybuf.at[k], lsem.at[k]))
    for k, start in enumerate((CY - 8, 0)):
        local.append(pltpu.make_async_copy(solid.at[:, start:start + 8, :], ysol.at[k], lsem.at[5 + k]))
    pairs = ((conc, CZ - 128), (adj, CZ - 128), (vz, CZ - 128), (conc, 0), (adj, 0))
    for k, (ref, start) in enumerate(pairs):
        local.append(pltpu.make_async_copy(ref.at[:, :, start:start + 128], zbuf.at[k], lsem.at[7 + k]))
    for k, start in enumerate((CZ - 128, 0)):
        local.append(pltpu.make_async_copy(solid.at[:, :, start:start + 128], zsol.at[k], lsem.at[12 + k]))
    for copy in local:
        copy.start()
    mine = pltpu.make_async_copy(rates, rall.at[xh, core, gy, gz], osem.at[0])
    mine.start()
    greet()

    started = []

    def send(src, dst, where):
        k = len(started)
        copy = pltpu.make_async_remote_copy(
            src_ref=src, dst_ref=dst, send_sem=ssem.at[k], recv_sem=rsem.at[k],
            device_id=where, device_id_type=MESH,
        )
        copy.start()
        started.append(copy)
        return copy

    first = send(rates, rall.at[xh, core, gy, gz], {"gx": gx + 2 - 4 * xh})
    right, left = {"gx": lax.rem(gx + 1, 4)}, {"gx": lax.rem(gx + 3, 4)}
    faces = []
    for k, ref in enumerate((conc, adj, vx)):
        faces.append(send(ref.at[CX - 1], xlo.at[k], right))
    faces.append(send(solid.at[CX - 1], xlo_s, right))
    for k, ref in enumerate((conc, adj)):
        faces.append(send(ref.at[0], xhi.at[k], left))
    faces.append(send(solid.at[0], xhi_s, left))

    for copy in local[:7]:
        copy.wait()

    def rows(x, carry):
        at = pl.ds(x, 1)
        for k in range(3):
            yfwd[k, at, :] = ybuf[k, x, 7:8, :]
        yfwd[3, at, :] = 1.0 - 0.7 * ysol[0, x, 7:8, :].astype(f32)
        for k in range(2):
            ybwd[k, at, :] = ybuf[3 + k, x, 0:1, :]
        ybwd[2, at, :] = 1.0 - 0.7 * ysol[1, x, 0:1, :].astype(f32)
        return carry

    lax.fori_loop(0, CX, rows, 0)
    faces.append(send(yfwd, ylo, {"gy": lax.rem(gy + 1, 8)}))
    faces.append(send(ybwd, yhi, {"gy": lax.rem(gy + 7, 8)}))
    keep_y = pltpu.make_async_copy(ybwd, yown, osem.at[1])
    keep_y.start()

    mine.wait()
    first.wait_recv()
    second = [
        send(rall.at[:, core, gy, gz], rall.at[:, core, gy, gz], {"gz": lax.rem(gz + o, 4)})
        for o in range(1, 4)
    ]

    for copy in local[7:]:
        copy.wait()
    lane = lax.broadcasted_iota(i32, (CY, 128), 1)

    def columns(x, carry):
        fwd, bwd = carry
        for k in range(3):
            fwd = jnp.where(lane == x + 32 * k, zbuf[k, x][:, 127:128], fwd)
        fwd = jnp.where(lane == x + 96, 1.0 - 0.7 * zsol[0, x][:, 127:128].astype(f32), fwd)
        for k in range(2):
            bwd = jnp.where(lane == x + 32 * k, zbuf[3 + k, x][:, 0:1], bwd)
        bwd = jnp.where(lane == x + 64, 1.0 - 0.7 * zsol[1, x][:, 0:1].astype(f32), bwd)
        return fwd, bwd

    zero = jnp.zeros((CY, 128), f32)
    fwd, bwd = lax.fori_loop(0, CX, columns, (zero, zero))
    zfwd[...] = fwd
    zbwd[...] = bwd
    faces.append(send(zfwd, zlo, {"gz": lax.rem(gz + 1, 4)}))
    faces.append(send(zbwd, zhi, {"gz": lax.rem(gz + 3, 4)}))
    keep_z = pltpu.make_async_copy(zbwd, zown, osem.at[2])
    keep_z.start()

    for copy in second:
        copy.wait_recv()
    third = [
        send(rall.at[:, core, gy], rall.at[:, core, gy], {"gy": lax.rem(gy + o, 8)})
        for o in range(1, 8)
    ]
    for copy in third:
        copy.wait_recv()
    last = send(rall.at[:, core], rall.at[:, core], {"gx": gx + 1 - 2 * core})
    last.wait_recv()
    for copy in faces:
        copy.wait_recv()
    for copy in started:
        copy.wait_send()
    keep_y.wait()
    keep_z.wait()


def call_faces(conc, adj, vx, vy, vz, solid, rates):
    face = lambda *s: jax.ShapeDtypeStruct(s, f32)
    outs = (
        face(3, CY, CZ), jax.ShapeDtypeStruct((CY, CZ), i32),
        face(2, CY, CZ), jax.ShapeDtypeStruct((CY, CZ), i32),
        face(4, CX, CZ), face(3, CX, CZ),
        face(CY, 128), face(CY, 128), face(3, CX, CZ), face(CY, 128),
        face(2, 2, 8, 4, 16, 128),
    )
    return pl.pallas_call(
        gather_faces,
        out_shape=outs,
        in_specs=[ANY] * 7,
        out_specs=[ANY] * len(outs),
        scratch_shapes=[
            pltpu.VMEM((5, CX, 8, CZ), f32), pltpu.VMEM((2, CX, 8, CZ), i32),
            pltpu.VMEM((5, CX, CY, 128), f32), pltpu.VMEM((2, CX, CY, 128), i32),
            pltpu.VMEM((4, CX, CZ), f32), pltpu.VMEM((3, CX, CZ), f32),
            pltpu.VMEM((CY, 128), f32), pltpu.VMEM((CY, 128), f32),
            pltpu.SemaphoreType.DMA((14,)), pltpu.SemaphoreType.DMA((24,)),
            pltpu.SemaphoreType.DMA((3,)), pltpu.SemaphoreType.DMA((24,)),
            pltpu.SemaphoreType.DMA((1,)),
        ],
        compiler_params=pltpu.CompilerParams(
            collective_id=0, has_side_effects=True, vmem_limit_bytes=40 << 20
        ),
    )(conc, adj, vx, vy, vz, solid, rates)


def roll_tile(tile, shift):
    return pltpu.roll(tile, shift, 1)


def main_kernel(
    block_ref,
    conc_ref, conc_next, adj_ref, adj_next, solid_ref, solid_next, load_ref, adjload_ref,
    vx_ref, vy_ref, vz_ref, slot_ref,
    xlo, xlo_s, xhi, xhi_s, ylo, yhi, zlo, zhi, yown, zown, rall, home0, home1, slot_grain,
    fin_ref, mstart_ref, dense_ref, lx_ref, ly_ref, lz_ref, cx_ref, cy_ref, cz_ref,
    packed, places_ref, table, hx, qx, hy, qy, hz, gp, lp, bxp, axp, qpp,
    hi_f, lo_f, term_f, hot_lo, hot_hi, total,
):
    i = pl.program_id(0)
    gx, gy, gz = (lax.axis_index(a) for a in ("gx", "gy", "gz"))
    has = lambda cond: jnp.where(cond, 1.0, 0.0).astype(f32)
    lo_x, hi_x = has(gx > 0), has(gx < 3)
    lo_y, hi_y = has(gy > 0), has(gy < 7)
    lo_z, hi_z = has(gz > 0), has(gz < 3)
    lane1 = lax.broadcasted_iota(i32, (CY, 128), 1)
    weight_of = lambda s: 1.0 - 0.7 * s.astype(f32)

    def pair(w0, w1, v):
        k = (dispersion * w0) * w1
        return k - jnp.minimum(v, 0.0), k + jnp.maximum(v, 0.0)

    @pl.when(i == 0)
    def _():
        total[...] = jnp.zeros_like(total)
        def pack(r, carry):
            at = pl.ds(pl.multiple_of(r * 64, 64), 64)
            up = pl.ds(pl.multiple_of(r * 64 + 1024, 64), 64)
            low = (rall[at, :] * (1.0 / rate_step) + 0.5).astype(i32)
            high = (rall[up, :] * (1.0 / rate_step) + 0.5).astype(i32)
            packed[at, :] = low + (high << 16)
            return carry

        lax.fori_loop(0, 16, pack, 0)
        base = (slot_grain[...] - block_ref[0] * 2048) & 262143
        lanes = [base[8 * j:8 * j + 8] & 127 for j in range(4)]
        rows = [base[8 * j:8 * j + 8] >> 7 for j in range(4)]
        found = [jnp.zeros((8, 128), i32)] * 4
        for r in range(32):
            src = home0 if r < 16 else home1
            row = jnp.broadcast_to(src[0, r % 16:r % 16 + 1, :], (8, 128))
            for j in range(4):
                found[j] = jnp.where(
                    rows[j] == r, jnp.take_along_axis(row, lanes[j], axis=1), found[j]
                )
        for j in range(4):
            places_ref[8 * j:8 * j + 8, :] = found[j]
        lanes = [f & 127 for f in found]
        rows = [(f >> 7) & 1023 for f in found]

        def look(r8, acc):
            acc = list(acc)
            for u in range(8):
                r = r8 * 8 + u
                row = jnp.broadcast_to(packed[pl.ds(r, 1), :], (8, 128))
                for j in range(4):
                    acc[j] = jnp.where(
                        rows[j] == r, jnp.take_along_axis(row, lanes[j], axis=1), acc[j]
                    )
            return tuple(acc)

        got = lax.fori_loop(0, 128, look, tuple(jnp.zeros((8, 128), i32) for _ in range(4)))
        got = [
            jnp.where(found[j] >= 131072, lax.shift_right_logical(got[j], 16), got[j] & 65535)
            for j in range(4)
        ]
        table[0:8, :] = got[0] + (got[2] << 16)
        table[8:16, :] = got[1] + (got[3] << 16)

        a, b = pair(weight_of(xlo_s[...]) * lo_x, weight_of(solid_ref[0]), xlo[2] * lo_x)
        hx[...] = a * conc_ref[0] - b * (xlo[0] * lo_x)
        qx[...] = a * (adj_ref[0] - xlo[1] * lo_x)
        cx_ref[0] = a
        a, b = pair(ylo[3] * lo_y, yown[2], ylo[2] * lo_y)
        hy[...] = a * yown[0] - b * (ylo[0] * lo_y)
        qy[...] = a * (yown[1] - ylo[1] * lo_y)
        cy_ref[0] = a
        low = zlo[...] * lo_z
        own = zown[...]
        own_w = roll_tile(own, 64)
        a, b = pair(roll_tile(low, 32), own_w, roll_tile(low, 64))
        flux_c = a * own - b * low
        flux_l = a * (roll_tile(own, 96) - roll_tile(low, 96))
        hz[...] = jnp.where(lane1 < 32, flux_c, roll_tile(jnp.where(lane1 < 32, flux_l, 0.0), 32))
        cz_ref[...] = jnp.where(lane1 < 32, a, 0.0)
        lz_ref[...] = jnp.zeros_like(lz_ref)

    ri = lax.broadcasted_iota(i32, (CY, CZ), 0)
    li = lax.broadcasted_iota(i32, (CY, CZ), 1)
    at = pl.ds(i, 1)
    two = lambda tile: jnp.concatenate([tile, tile], axis=1)
    lane_first = lambda tile, k: two(roll_tile(tile, lax.rem(256 - i - 32 * k, 128)))
    lane_last = lambda tile, k: two(roll_tile(tile, lax.rem(255 - i - 32 * k, 128)))

    def up_y(v, row):
        return jnp.where(ri == CY - 1, row, pltpu.roll(v, CY - 1, 0))

    def down_y(v, row):
        return jnp.where(ri == 0, row, pltpu.roll(v, 1, 0))

    def up_z(v, tile):
        return jnp.where(li == CZ - 1, tile, pltpu.roll(v, CZ - 1, 1))

    def down_z(v, tile):
        return jnp.where(li == 0, tile, pltpu.roll(v, 1, 1))

    c, l = conc_ref[0], adj_ref[0]
    sol = solid_ref[0].astype(f32)
    w = 1.0 - 0.7 * sol
    end = i == CX - 1
    w1 = jnp.where(end, weight_of(xhi_s[...]) * hi_x, weight_of(solid_next[0]))
    c1 = jnp.where(end, xhi[0] * hi_x, conc_next[0])
    l1 = jnp.where(end, xhi[1] * hi_x, adj_next[0])
    ax, bx = pair(w, w1, vx_ref[0])
    flux = ax * c1 - bx * c
    div = flux - hx[...]
    hx[...] = flux
    d = l1 - l
    q = ax * d
    lap = bx * d - qx[...]
    qx[...] = q
    ay, by = pair(w, up_y(w, yhi[2, at, :] * hi_y), vy_ref[0])
    flux = ay * up_y(c, yhi[0, at, :] * hi_y) - by * c
    div = div + flux - down_y(flux, hy[at, :])
    d = up_y(l, yhi[1, at, :] * hi_y) - l
    q = ay * d
    lap = lap + by * d - down_y(q, qy[at, :])
    high = zhi[...] * hi_z
    az, bz = pair(w, up_z(w, lane_last(high, 2)), vz_ref[0])
    flux = az * up_z(c, lane_last(high, 0)) - bz * c
    div = div + flux - down_z(flux, lane_first(hz[...], 0))
    d = up_z(l, lane_last(high, 1)) - l
    q = az * d
    lap = lap + bz * d - down_z(q, lane_first(hz[...], 1))

    lookups = []
    for g in range(CY // 8):
        halves = []
        for h in range(2):
            s = slot_ref[0, 8 * g:8 * g + 8, 128 * h:128 * h + 128]
            lo, hi = s & 127, s >> 7
            level = [
                jnp.take_along_axis(jnp.broadcast_to(table[r:r + 1, :], (8, 128)), lo, axis=1)
                for r in range(16)
            ]
            for bit in range(4):
                mask = (hi & (1 << bit)) != 0
                level = [
                    jnp.where(mask, level[2 * j + 1], level[2 * j]) for j in range(len(level) // 2)
                ]
            p = level[0]
            value = jnp.where((hi & 16) != 0, lax.shift_right_logical(p, 16), p & 65535)
            halves.append(value.astype(f32) * rate_step)
        lookups.append(jnp.concatenate(halves, axis=1))
    kv = sol * jnp.concatenate(lookups, axis=0)

    def inverse(v):
        r = pl.reciprocal(v, approx=True)
        return r * (2.0 - v * r)

    m = adjload_ref[0]
    u0 = inverse(1.0 + c)
    e0 = c * u0 - load_ref[0]
    r = kv * e0
    conc1 = c + div - r
    load1 = load_ref[0] + r
    d1 = m - l
    u1 = inverse(1.0 + conc1)
    kd = kv * d1
    adj1 = l + lap + kd * (u1 * u1)
    m1 = m - kd
    d0 = m1 - adj1
    kd = kv * d0
    mstart_ref[0] = m1 - kd
    term_f[...] = sol * ((conc1 * u1 - load1) * d1 + e0 * d0)
    base = adj1 + kd * (u0 * u0)

    d = up_y(adj1, 0.0) - adj1
    base = base + by * d - down_y(ay * d, cy_ref[0, at, :] * adj1[0:1, :])
    d = up_z(adj1, 0.0) - adj1
    first_col = lane_first(cz_ref[...], 0) * adj1
    base = base + bz * d - down_z(az * d, first_col)

    @pl.when(i == 0)
    def _():
        qpp[...] = cx_ref[0] * adj1
        lx_ref[0] = adj1

    @pl.when(i > 0)
    def _():
        dx = adj1 - lp[...]
        fin_ref[i - 1] = gp[...] + bxp[...] * dx - qpp[...]
        qpp[...] = axp[...] * dx

    @pl.when(end)
    def _():
        fin_ref[CX - 1] = base - bx * adj1 - qpp[...]
        lx_ref[1] = adj1
        cx_ref[1] = bx

    gp[...] = base
    lp[...] = adj1
    bxp[...] = bx
    axp[...] = ax
    ly_ref[0, at, :] = adj1[0:1, :]
    ly_ref[1, at, :] = adj1[CY - 1:CY, :]
    cy_ref[1, at, :] = by[CY - 1:CY, :]
    packed_l = jnp.where(lane1 == i, adj1[:, 0:1], lz_ref[...])
    lz_ref[...] = jnp.where(lane1 == i + 32, adj1[:, CZ - 1:CZ], packed_l)
    cz_ref[...] = jnp.where(lane1 == i + 32, bz[:, CZ - 1:CZ], cz_ref[...])

    slots = slot_ref[0]
    hi_f[...] = (slots >> 7).astype(f32)
    lo_f[...] = (slots & 127).astype(f32)
    ids = lax.broadcasted_iota(i32, (128, CZ), 0).astype(f32).astype(bf16)
    zero, one = jnp.zeros((16, CZ), bf16), jnp.ones((16, CZ), bf16)
    row = lambda ref, y: jnp.broadcast_to(ref[y:y + 1, :], (16, CZ))
    acc = total[...]
    for chunk in range(8):
        slot = chunk % 4
        for y8 in range(8):
            y = chunk * 8 + y8
            span = slice(y8 * CZ, y8 * CZ + CZ)
            h, o = row(hi_f, y).astype(bf16), row(lo_f, y).astype(bf16)
            t = row(term_f, y)
            t_high = t.astype(bf16)
            t_low = (t - t_high.astype(f32)).astype(bf16)
            for j in range(2):
                mask = ids[16 * j:16 * j + 16] == h
                hot_hi[slot, 16 * j:16 * j + 16, span] = jnp.where(mask, t_high, zero)
                hot_hi[slot, 32 + 16 * j:48 + 16 * j, span] = jnp.where(mask, t_low, zero)
            for j in range(8):
                hot_lo[slot, 16 * j:16 * j + 16, span] = jnp.where(
                    ids[16 * j:16 * j + 16] == o, one, zero
                )
        acc = acc + lax.dot_general(
            hot_lo[slot], hot_hi[slot], (((1,), (1,)), ((), ())), preferred_element_type=f32
        )
    total[...] = acc

    @pl.when(end)
    def _():
        by_lane = total[...].T
        sums = by_lane[0:32] + by_lane[32:64]
        places = places_ref[...]
        high = sums.astype(bf16)
        high_f = high.astype(f32)
        low_f = sums - high_f
        place_lane = (places & 127).astype(f32)
        place_row = places >> 7
        lane_ids = lax.broadcasted_iota(i32, (128, 128), 0).astype(f32)

        row_ids = lax.broadcasted_iota(i32, (256, 128), 0)

        hots = []
        values = []
        for s in range(32):
            match = lane_ids == place_lane[s:s + 1, :]
            values.append(
                jnp.concatenate(
                    [
                        jnp.where(match, high_f[s:s + 1, :], 0.0).astype(bf16),
                        jnp.where(match, low_f[s:s + 1, :], 0.0).astype(bf16),
                    ],
                    axis=0,
                )
            )
        value = jnp.concatenate(values, axis=1)

        def spread(n, carry):
            hot = jnp.concatenate(
                [
                    jnp.where(row_ids + n * 256 == place_row[s:s + 1, :], 1.0, 0.0).astype(bf16)
                    for s in range(32)
                ],
                axis=1,
            )
            got = lax.dot_general(
                hot, value, (((1,), (1,)), ((), ())), preferred_element_type=f32
            )
            dense_ref[pl.ds(pl.multiple_of(n * 256, 256), 256), :] = got[:, 0:128] + got[:, 128:256]
            return carry

        lax.fori_loop(0, 8, spread, 0)


def call_main(block, arrays, faces, home, slot_grain):
    conc, load, adj, adj_load, vx, vy, vz, solid, slot = arrays
    plane = pl.BlockSpec((1, CY, CZ), lambda i, b: (i, 0, 0))
    after = pl.BlockSpec((1, CY, CZ), lambda i, b: (jnp.minimum(i + 1, CX - 1), 0, 0))

    def whole(shape):
        return pl.BlockSpec(shape, lambda i, b: (0,) * len(shape))

    face_shapes = [
        (3, CY, CZ), (CY, CZ), (2, CY, CZ), (CY, CZ), (4, CX, CZ), (3, CX, CZ),
        (CY, 128), (CY, 128), (3, CX, CZ), (CY, 128), (2048, 128),
    ]
    out_shapes = [
        (CX, CY, CZ), (CX, CY, CZ), (2048, 128), (2, CY, CZ), (2, CX, CZ), (CY, 128),
        (2, CY, CZ), (2, CX, CZ), (CY, 128),
    ]
    plane_scratch = pltpu.VMEM((CY, CZ), f32)
    row_scratch = pltpu.VMEM((CX, CZ), f32)
    return pl.pallas_call(
        main_kernel,
        out_shape=[jax.ShapeDtypeStruct(s, f32) for s in out_shapes],
        grid_spec=pltpu.PrefetchScalarGridSpec(
            num_scalar_prefetch=1,
            grid=(CX,),
            in_specs=[plane, after, plane, after, plane, after, plane, plane, plane, plane, plane, plane]
            + [whole(s) for s in face_shapes]
            + [
                pl.BlockSpec((1, 16, 128), lambda i, b: (b[0], 0, 0)),
                pl.BlockSpec((1, 16, 128), lambda i, b: (lax.rem(b[0] + 1, 128), 0, 0)),
                whole((32, 128)),
            ],
            out_specs=[whole(out_shapes[0]), plane] + [whole(s) for s in out_shapes[2:]],
            scratch_shapes=[
                pltpu.VMEM((1024, 128), i32), pltpu.VMEM((32, 128), i32), pltpu.VMEM((16, 128), i32),
                plane_scratch, plane_scratch, row_scratch, row_scratch, pltpu.VMEM((CY, 128), f32),
                plane_scratch, plane_scratch, plane_scratch, plane_scratch, plane_scratch,
                plane_scratch, plane_scratch, plane_scratch,
                pltpu.VMEM((4, 128, 2048), bf16), pltpu.VMEM((4, 64, 2048), bf16),
                pltpu.VMEM((128, 64), f32),
            ],
        ),
        compiler_params=pltpu.CompilerParams(
            dimension_semantics=("arbitrary",), vmem_limit_bytes=50 << 20
        ),
        cost_estimate=pl.CostEstimate(flops=10 ** 9, bytes_accessed=25 << 20, transcendentals=0),
    )(
        block, conc, conc, adj, adj, solid, solid, load, adj_load, vx, vy, vz, slot,
        *faces[:10], faces[10].reshape(2048, 128), home, home, slot_grain,
    )


def finish_kernel(
    fin, dense, lx, ly, lz, cx, cy, cz,
    out, grad,
    fbuf, xlo, xhi, ylo, yhi, zlo, zhi, d1, r1, r2, s2, r3, s3, r4, lsem, ssem, rsem,
):
    gx, gy, gz = (lax.axis_index(a) for a in ("gx", "gy", "gz"))
    xh, core = gx // 2, lax.rem(gx, 2)
    has = lambda cond: jnp.where(cond, 1.0, 0.0).astype(f32)
    hi_x, hi_y, hi_z = has(gx < 3), has(gy < 7), has(gz < 3)
    keep = pltpu.make_async_copy(dense.at[:, core], d1, lsem.at[0])
    keep.start()
    body = pltpu.make_async_copy(fin, fbuf, lsem.at[1])
    body.start()
    greet()
    started = []

    def send(src, dst, where):
        k = len(started)
        copy = pltpu.make_async_remote_copy(
            src_ref=src, dst_ref=dst, send_sem=ssem.at[k], recv_sem=rsem.at[k],
            device_id=where, device_id_type=MESH,
        )
        copy.start()
        started.append(copy)
        return copy

    first = send(dense.at[:, 1 - core], r1, {"gx": gx + 1 - 2 * core})
    faces = [
        send(lx.at[1], xlo, {"gx": lax.rem(gx + 1, 4)}),
        send(lx.at[0], xhi, {"gx": lax.rem(gx + 3, 4)}),
        send(ly.at[1], ylo, {"gy": lax.rem(gy + 1, 8)}),
        send(ly.at[0], yhi, {"gy": lax.rem(gy + 7, 8)}),
        send(lz, zlo, {"gz": lax.rem(gz + 1, 4)}),
        send(lz, zhi, {"gz": lax.rem(gz + 3, 4)}),
    ]
    keep.wait()
    first.wait_recv()

    def add_first(h, carry):
        for x in range(2):
            d1[x, h] = d1[x, h] + r1[x, h]
        return carry

    lax.fori_loop(0, 8, add_first, 0)
    second = [
        send(d1.at[:, lax.rem(gy + o, 8)], r2.at[o - 1], {"gy": lax.rem(gy + o, 8)})
        for o in range(1, 8)
    ]
    body.wait()
    for copy in faces:
        copy.wait_recv()
    fbuf[0] = fbuf[0] + cx[0] * xlo[...]
    fbuf[CX - 1] = fbuf[CX - 1] + cx[1] * (xhi[...] * hi_x)
    lane = lax.broadcasted_iota(i32, (CY, 128), 1)
    cols = cz[...] * jnp.where(
        lane < 32, pltpu.roll(zlo[...], 96, 1), pltpu.roll(zhi[...] * hi_z, 32, 1)
    )

    def fix(x, carry):
        at = pl.ds(x, 1)
        fbuf[x, 0:1, :] = fbuf[x, 0:1, :] + cy[0, at, :] * ylo[at, :]
        fbuf[x, CY - 1:CY, :] = fbuf[x, CY - 1:CY, :] + cy[1, at, :] * (yhi[at, :] * hi_y)
        low = pltpu.roll(cols, lax.rem(128 - x, 128), 1)
        high = pltpu.roll(cols, 95 - x, 1)
        fbuf[x, :, 0:128] = fbuf[x, :, 0:128] + jnp.where(lane == 0, low, 0.0)
        fbuf[x, :, 128:256] = fbuf[x, :, 128:256] + jnp.where(lane == 127, high, 0.0)
        return carry

    lax.fori_loop(0, CX, fix, 0)
    store = pltpu.make_async_copy(fbuf, out, lsem.at[2])
    store.start()
    for copy in second:
        copy.wait_recv()
    for x in range(2):
        acc = d1[x, gy]
        for o in range(7):
            acc = acc + r2[o, x]
        s2[x] = acc
    third = [
        send(s2.at[:, lax.rem(gz + o, 4)], r3.at[o - 1], {"gz": lax.rem(gz + o, 4)})
        for o in range(1, 4)
    ]
    for copy in third:
        copy.wait_recv()
    for x in range(2):
        s3[x] = s2[x, gz] + r3[0, x] + r3[1, x] + r3[2, x]
    last = send(s3.at[1 - xh], r4, {"gx": gx + 2 - 4 * xh})
    last.wait_recv()
    grad[...] = s3[xh] + r4[...]
    for copy in started:
        copy.wait_send()
    store.wait()


def call_finish(fin, dense, lx, ly, lz, cx, cy, cz):
    vmem = pl.BlockSpec(memory_space=pltpu.VMEM)
    return pl.pallas_call(
        finish_kernel,
        out_shape=(
            jax.ShapeDtypeStruct((CX, CY, CZ), f32), jax.ShapeDtypeStruct((16, 128), f32)
        ),
        in_specs=[ANY] * 5 + [vmem] * 3,
        out_specs=(ANY, vmem),
        scratch_shapes=[
            pltpu.VMEM((CX, CY, CZ), f32),
            pltpu.VMEM((CY, CZ), f32), pltpu.VMEM((CY, CZ), f32),
            pltpu.VMEM((CX, CZ), f32), pltpu.VMEM((CX, CZ), f32),
            pltpu.VMEM((CY, 128), f32), pltpu.VMEM((CY, 128), f32),
            pltpu.VMEM((2, 8, 4, 16, 128), f32), pltpu.VMEM((2, 8, 4, 16, 128), f32),
            pltpu.VMEM((7, 2, 4, 16, 128), f32), pltpu.VMEM((2, 4, 16, 128), f32),
            pltpu.VMEM((3, 2, 16, 128), f32), pltpu.VMEM((2, 16, 128), f32),
            pltpu.VMEM((16, 128), f32),
            pltpu.SemaphoreType.DMA((3,)), pltpu.SemaphoreType.DMA((18,)),
            pltpu.SemaphoreType.DMA((18,)),
        ],
        compiler_params=pltpu.CompilerParams(
            collective_id=1, has_side_effects=True, vmem_limit_bytes=40 << 20
        ),
    )(fin, dense, lx, ly, lz, cx, cy, cz)


def per_device(
    conc, load, adj_conc, adj_load, vel_x, vel_y, vel_z, solid, voxel_slot, slot_grain, grain_home, rates
):
    block = (lax.axis_index("gx") * 32 + lax.axis_index("gy") * 4 + lax.axis_index("gz")).astype(i32)
    faces = call_faces(conc, adj_conc, vel_x, vel_y, vel_z, solid, rates.reshape(16, 128))
    arrays = (conc, load, adj_conc, adj_load, vel_x, vel_y, vel_z, solid, voxel_slot)
    fin, load_start, dense, lx, ly, lz, cx, cy, cz = call_main(
        block.reshape(1), arrays, faces, grain_home.reshape(128, 16, 128), slot_grain.reshape(32, 128)
    )
    start, grad = call_finish(
        fin, dense.reshape(2, 2, 8, 4, 16, 128), lx, ly, lz, cx, cy, cz
    )
    return start, load_start, grad.reshape(2048)


def solution(mesh):
    cells = P("gx", "gy", "gz")
    every = P(("gx", "gy", "gz"))
    return jax.shard_map(
        per_device,
        mesh=mesh,
        in_specs=(cells,) * 9 + (P(("gx", "gy", "gz"), None), P(), every),
        out_specs=(cells, cells, every),
        check_vma=False,
    )
```

```python
import functools

import jax
import jax.numpy as jnp
from jax import lax
from jax.experimental import pallas as pl
from jax.experimental.pallas import tpu as pltpu
from jax.sharding import PartitionSpec as P

f32, bf16, i32, f8 = jnp.float32, jnp.bfloat16, jnp.int32, jnp.float8_e4m3fn
DIGITS = 4
CHUNKS = 4
MESH = pl.DeviceIdType.MESH
ANY = pl.BlockSpec(memory_space=pl.ANY)
dispersion = 0.06
rate_step = 0.2 / 65535.0
CX, CY, CZ = 32, 64, 256


def greet():
    barrier = pltpu.get_barrier_semaphore()
    for axis, count in (("gx", 4), ("gy", 8), ("gz", 4)):
        me = lax.axis_index(axis)
        for o in range(1, count):
            pl.semaphore_signal(
                barrier, inc=1, device_id={axis: lax.rem(me + o, count)}, device_id_type=MESH
            )
    pl.semaphore_wait(barrier, 13)


def gather_faces(
    conc, adj, vx, vy, vz, solid, rates,
    xlo, xlo_s, xhi, xhi_s, ylo, yhi, zlo, zhi, yown, zown, rall,
    ybuf, ysol, zbuf, zsol, yfwd, ybwd, zfwd, zbwd, lsem, rsem, osem, ssem, dsem,
):
    gx, gy, gz = (lax.axis_index(a) for a in ("gx", "gy", "gz"))
    xh, core = gx // 2, lax.rem(gx, 2)
    local = []
    pairs = ((conc, CY - 8), (adj, CY - 8), (vy, CY - 8), (conc, 0), (adj, 0))
    for k, (ref, start) in enumerate(pairs):
        local.append(pltpu.make_async_copy(ref.at[:, start:start + 8, :], ybuf.at[k], lsem.at[k]))
    for k, start in enumerate((CY - 8, 0)):
        local.append(pltpu.make_async_copy(solid.at[:, start:start + 8, :], ysol.at[k], lsem.at[5 + k]))
    pairs = ((conc, CZ - 128), (adj, CZ - 128), (vz, CZ - 128), (conc, 0), (adj, 0))
    for k, (ref, start) in enumerate(pairs):
        local.append(pltpu.make_async_copy(ref.at[:, :, start:start + 128], zbuf.at[k], lsem.at[7 + k]))
    for k, start in enumerate((CZ - 128, 0)):
        local.append(pltpu.make_async_copy(solid.at[:, :, start:start + 128], zsol.at[k], lsem.at[12 + k]))
    for copy in local:
        copy.start()
    mine = pltpu.make_async_copy(rates, rall.at[xh, core, gy, gz], osem.at[0])
    mine.start()
    greet()

    started = []

    def send(src, dst, where):
        k = len(started)
        copy = pltpu.make_async_remote_copy(
            src_ref=src, dst_ref=dst, send_sem=ssem.at[k], recv_sem=rsem.at[k],
            device_id=where, device_id_type=MESH,
        )
        copy.start()
        started.append(copy)
        return copy

    first = send(rates, rall.at[xh, core, gy, gz], {"gx": gx + 2 - 4 * xh})
    right, left = {"gx": lax.rem(gx + 1, 4)}, {"gx": lax.rem(gx + 3, 4)}
    faces = []
    for k, ref in enumerate((conc, adj, vx)):
        faces.append(send(ref.at[CX - 1], xlo.at[k], right))
    faces.append(send(solid.at[CX - 1], xlo_s, right))
    for k, ref in enumerate((conc, adj)):
        faces.append(send(ref.at[0], xhi.at[k], left))
    faces.append(send(solid.at[0], xhi_s, left))

    for copy in local[:7]:
        copy.wait()

    def rows(x, carry):
        at = pl.ds(x, 1)
        for k in range(3):
            yfwd[k, at, :] = ybuf[k, x, 7:8, :]
        yfwd[3, at, :] = 1.0 - 0.7 * ysol[0, x, 7:8, :].astype(f32)
        for k in range(2):
            ybwd[k, at, :] = ybuf[3 + k, x, 0:1, :]
        ybwd[2, at, :] = 1.0 - 0.7 * ysol[1, x, 0:1, :].astype(f32)
        return carry

    lax.fori_loop(0, CX, rows, 0)
    faces.append(send(yfwd, ylo, {"gy": lax.rem(gy + 1, 8)}))
    faces.append(send(ybwd, yhi, {"gy": lax.rem(gy + 7, 8)}))
    keep_y = pltpu.make_async_copy(ybwd, yown, osem.at[1])
    keep_y.start()

    mine.wait()
    first.wait_recv()
    second = [
        send(rall.at[:, core, gy, gz], rall.at[:, core, gy, gz], {"gz": lax.rem(gz + o, 4)})
        for o in range(1, 4)
    ]

    for copy in local[7:]:
        copy.wait()
    lane = lax.broadcasted_iota(i32, (CY, 128), 1)

    def columns(x, carry):
        fwd, bwd = carry
        for k in range(3):
            fwd = jnp.where(lane == x + 32 * k, zbuf[k, x][:, 127:128], fwd)
        fwd = jnp.where(lane == x + 96, 1.0 - 0.7 * zsol[0, x][:, 127:128].astype(f32), fwd)
        for k in range(2):
            bwd = jnp.where(lane == x + 32 * k, zbuf[3 + k, x][:, 0:1], bwd)
        bwd = jnp.where(lane == x + 64, 1.0 - 0.7 * zsol[1, x][:, 0:1].astype(f32), bwd)
        return fwd, bwd

    zero = jnp.zeros((CY, 128), f32)
    fwd, bwd = lax.fori_loop(0, CX, columns, (zero, zero))
    zfwd[...] = fwd
    zbwd[...] = bwd
    faces.append(send(zfwd, zlo, {"gz": lax.rem(gz + 1, 4)}))
    faces.append(send(zbwd, zhi, {"gz": lax.rem(gz + 3, 4)}))
    keep_z = pltpu.make_async_copy(zbwd, zown, osem.at[2])
    keep_z.start()

    for copy in second:
        copy.wait_recv()
    third = [
        send(rall.at[:, core, gy], rall.at[:, core, gy], {"gy": lax.rem(gy + o, 8)})
        for o in range(1, 8)
    ]
    for copy in third:
        copy.wait_recv()
    last = send(rall.at[:, core], rall.at[:, core], {"gx": gx + 1 - 2 * core})
    last.wait_recv()
    for copy in faces:
        copy.wait_recv()
    for copy in started:
        copy.wait_send()
    keep_y.wait()
    keep_z.wait()


def call_faces(conc, adj, vx, vy, vz, solid, rates):
    face = lambda *s: jax.ShapeDtypeStruct(s, f32)
    outs = (
        face(3, CY, CZ), jax.ShapeDtypeStruct((CY, CZ), i32),
        face(2, CY, CZ), jax.ShapeDtypeStruct((CY, CZ), i32),
        face(4, CX, CZ), face(3, CX, CZ),
        face(CY, 128), face(CY, 128), face(3, CX, CZ), face(CY, 128),
        face(2, 2, 8, 4, 16, 128),
    )
    return pl.pallas_call(
        gather_faces,
        out_shape=outs,
        in_specs=[ANY] * 7,
        out_specs=[ANY] * len(outs),
        scratch_shapes=[
            pltpu.VMEM((5, CX, 8, CZ), f32), pltpu.VMEM((2, CX, 8, CZ), i32),
            pltpu.VMEM((5, CX, CY, 128), f32), pltpu.VMEM((2, CX, CY, 128), i32),
            pltpu.VMEM((4, CX, CZ), f32), pltpu.VMEM((3, CX, CZ), f32),
            pltpu.VMEM((CY, 128), f32), pltpu.VMEM((CY, 128), f32),
            pltpu.SemaphoreType.DMA((14,)), pltpu.SemaphoreType.DMA((24,)),
            pltpu.SemaphoreType.DMA((3,)), pltpu.SemaphoreType.DMA((24,)),
            pltpu.SemaphoreType.DMA((1,)),
        ],
        compiler_params=pltpu.CompilerParams(
            collective_id=0, has_side_effects=True, vmem_limit_bytes=62 << 20
        ),
    )(conc, adj, vx, vy, vz, solid, rates)


def roll_tile(tile, shift):
    return pltpu.roll(tile, shift, 1)


def main_kernel(
    block_ref,
    conc_ref, conc_next, adj_ref, adj_next, solid_ref, solid_next, load_ref, adjload_ref,
    vx_ref, vy_ref, vz_ref, slot_ref,
    xlo, xlo_s, xhi, xhi_s, ylo, yhi, zlo, zhi, yown, zown, rall, home0, home1, slot_grain,
    fin_ref, mstart_ref, dense_ref, lx_ref, ly_ref, lz_ref, cx_ref, cy_ref, cz_ref,
    packed, places_ref, table, hx, qx, hy, qy, hz, gp, lp, bxp, axp, qpp,
    hi_f, lo_f, term_f, hot_lo, hot_hi, total, got_ref, look_ref
):
    i = pl.program_id(0)
    gx, gy, gz = (lax.axis_index(a) for a in ("gx", "gy", "gz"))
    has = lambda cond: jnp.where(cond, 1.0, 0.0).astype(f32)
    lo_x, hi_x = has(gx > 0), has(gx < 3)
    lo_y, hi_y = has(gy > 0), has(gy < 7)
    lo_z, hi_z = has(gz > 0), has(gz < 3)
    lane1 = lax.broadcasted_iota(i32, (CY, 128), 1)
    weight_of = lambda s: 1.0 - 0.7 * s.astype(f32)

    def pair(w0, w1, v):
        k = (dispersion * w0) * w1
        return k - jnp.minimum(v, 0.0), k + jnp.maximum(v, 0.0)

    @pl.when(i == 0)
    def _():
        total[...] = jnp.zeros_like(total)
        hot_lo[...] = jnp.zeros_like(hot_lo)
        hot_hi[...] = jnp.zeros_like(hot_hi)
        def pack(r, carry):
            at = pl.ds(pl.multiple_of(r * 128, 128), 128)
            packed[at, :] = (rall[at, :] * (1.0 / rate_step) + 0.5).astype(i32)
            return carry

        lax.fori_loop(0, 16, pack, 0)
        base = (slot_grain[...] - block_ref[0] * 2048) & 262143
        lanes = [base[8 * j:8 * j + 8] & 127 for j in range(4)]
        rows = [base[8 * j:8 * j + 8] >> 7 for j in range(4)]
        found = [jnp.zeros((8, 128), i32)] * 4
        for r in range(32):
            src = home0 if r < 16 else home1
            row = jnp.broadcast_to(src[0, r % 16:r % 16 + 1, :], (8, 128))
            for j in range(4):
                found[j] = jnp.where(
                    rows[j] == r, jnp.take_along_axis(row, lanes[j], axis=1), found[j]
                )
        for j in range(4):
            places_ref[8 * j:8 * j + 8, :] = found[j]
        lanes = [f & 127 for f in found]
        rows = [(f >> 7) & 1023 for f in found]


        sub_ids = lax.broadcasted_iota(i32, (256, 128), 0).astype(f32).astype(bf16)
        ones, zeros = jnp.ones((256, 128), bf16), jnp.zeros((256, 128), bf16)

        def look(n, acc):
            at = pl.ds(pl.multiple_of(n * 256, 256), 256)
            q = packed[at, :]
            digits = jnp.concatenate([(q & 255).astype(f32).astype(bf16), ((q >> 8) & 255).astype(f32).astype(bf16)], axis=1)
            first = (n * 256).astype(f32)
            hot = jnp.concatenate(
                [
                    jnp.where(
                        sub_ids == jnp.broadcast_to((found[s // 8] >> 7).astype(f32)[s % 8:s % 8 + 1, :] - first, (256, 128)).astype(bf16),
                        ones, zeros,
                    )
                    for s in range(32)
                ],
                axis=1,
            )
            got_ref[...] = got_ref[...] + lax.dot_general(digits, hot, (((0,), (0,)), ((), ())), preferred_element_type=f32)
            return acc
        got_ref[...] = jnp.zeros_like(got_ref)
        lax.fori_loop(0, 8, look, 0)
        lids = lax.broadcasted_iota(i32, (128, 128), 0)
        for s in range(32):
            m = lids == (found[s // 8] & 127)[s % 8:s % 8 + 1, :]
            sp = slice(128 * s, 128 * s + 128)
            v = got_ref[0:128, sp] + 256.0 * got_ref[128:256, sp]
            look_ref[s:s + 1, :] = jnp.sum(jnp.where(m, v, 0.0), axis=0, keepdims=True)
        got = [look_ref[8 * j:8 * j + 8, :].astype(i32) for j in range(4)]
        table[0:8, :] = got[0] + (got[2] << 16)
        table[8:16, :] = got[1] + (got[3] << 16)

        a, b = pair(weight_of(xlo_s[...]) * lo_x, weight_of(solid_ref[0]), xlo[2] * lo_x)
        hx[...] = a * conc_ref[0] - b * (xlo[0] * lo_x)
        qx[...] = a * (adj_ref[0] - xlo[1] * lo_x)
        cx_ref[0] = a
        a, b = pair(ylo[3] * lo_y, yown[2], ylo[2] * lo_y)
        hy[...] = a * yown[0] - b * (ylo[0] * lo_y)
        qy[...] = a * (yown[1] - ylo[1] * lo_y)
        cy_ref[0] = a
        low = zlo[...] * lo_z
        own = zown[...]
        own_w = roll_tile(own, 64)
        a, b = pair(roll_tile(low, 32), own_w, roll_tile(low, 64))
        flux_c = a * own - b * low
        flux_l = a * (roll_tile(own, 96) - roll_tile(low, 96))
        hz[...] = jnp.where(lane1 < 32, flux_c, roll_tile(jnp.where(lane1 < 32, flux_l, 0.0), 32))
        cz_ref[...] = jnp.where(lane1 < 32, a, 0.0)
        lz_ref[...] = jnp.zeros_like(lz_ref)

    def products():
        acc = None
        for chunk in range(CHUNKS):
            span = slice(chunk * (CY * CZ // CHUNKS), (chunk + 1) * (CY * CZ // CHUNKS))
            got = lax.dot_general(
                hot_lo[:, span], hot_hi[:, span], (((1,), (1,)), ((), ())), preferred_element_type=f32
            )
            acc = got if acc is None else acc + got
        return acc

    total[...] = total[...] + products()
    ri = lax.broadcasted_iota(i32, (CY, CZ), 0)
    li = lax.broadcasted_iota(i32, (CY, CZ), 1)
    at = pl.ds(i, 1)
    two = lambda tile: jnp.concatenate([tile, tile], axis=1)
    lane_first = lambda tile, k: two(roll_tile(tile, lax.rem(256 - i - 32 * k, 128)))
    lane_last = lambda tile, k: two(roll_tile(tile, lax.rem(255 - i - 32 * k, 128)))

    def up_y(v, row):
        return jnp.where(ri == CY - 1, row, pltpu.roll(v, CY - 1, 0))

    def down_y(v, row):
        return jnp.where(ri == 0, row, pltpu.roll(v, 1, 0))

    def up_z(v, tile):
        return jnp.where(li == CZ - 1, tile, pltpu.roll(v, CZ - 1, 1))

    def down_z(v, tile):
        return jnp.where(li == 0, tile, pltpu.roll(v, 1, 1))

    c, l = conc_ref[0], adj_ref[0]
    sol = solid_ref[0].astype(f32)
    w = 1.0 - 0.7 * sol
    end = i == CX - 1
    w1 = jnp.where(end, weight_of(xhi_s[...]) * hi_x, weight_of(solid_next[0]))
    c1 = jnp.where(end, xhi[0] * hi_x, conc_next[0])
    l1 = jnp.where(end, xhi[1] * hi_x, adj_next[0])
    ax, bx = pair(w, w1, vx_ref[0])
    flux = ax * c1 - bx * c
    div = flux - hx[...]
    hx[...] = flux
    d = l1 - l
    q = ax * d
    lap = bx * d - qx[...]
    qx[...] = q
    ay, by = pair(w, up_y(w, yhi[2, at, :] * hi_y), vy_ref[0])
    flux = ay * up_y(c, yhi[0, at, :] * hi_y) - by * c
    div = div + flux - down_y(flux, hy[at, :])
    d = up_y(l, yhi[1, at, :] * hi_y) - l
    q = ay * d
    lap = lap + by * d - down_y(q, qy[at, :])
    high = zhi[...] * hi_z
    az, bz = pair(w, up_z(w, lane_last(high, 2)), vz_ref[0])
    flux = az * up_z(c, lane_last(high, 0)) - bz * c
    div = div + flux - down_z(flux, lane_first(hz[...], 0))
    d = up_z(l, lane_last(high, 1)) - l
    q = az * d
    lap = lap + bz * d - down_z(q, lane_first(hz[...], 1))

    lookups = []
    for g in range(CY // 8):
        halves = []
        for h in range(2):
            s = slot_ref[0, 8 * g:8 * g + 8, 128 * h:128 * h + 128]
            lo, hi = s & 127, s >> 7
            level = [
                jnp.take_along_axis(jnp.broadcast_to(table[r:r + 1, :], (8, 128)), lo, axis=1)
                for r in range(16)
            ]
            for bit in range(4):
                mask = (hi & (1 << bit)) != 0
                level = [
                    jnp.where(mask, level[2 * j + 1], level[2 * j]) for j in range(len(level) // 2)
                ]
            p = level[0]
            value = jnp.where((hi & 16) != 0, lax.shift_right_logical(p, 16), p & 65535)
            halves.append(value.astype(f32) * rate_step)
        lookups.append(jnp.concatenate(halves, axis=1))
    kv = sol * jnp.concatenate(lookups, axis=0)

    def inverse(v):
        r = pl.reciprocal(v, approx=True)
        return r * (2.0 - v * r)

    m = adjload_ref[0]
    u0 = inverse(1.0 + c)
    e0 = c * u0 - load_ref[0]
    r = kv * e0
    conc1 = c + div - r
    load1 = load_ref[0] + r
    d1 = m - l
    u1 = inverse(1.0 + conc1)
    kd = kv * d1
    adj1 = l + lap + kd * (u1 * u1)
    m1 = m - kd
    d0 = m1 - adj1
    kd = kv * d0
    mstart_ref[0] = m1 - kd
    term_f[...] = sol * ((conc1 * u1 - load1) * d1 + e0 * d0)
    base = adj1 + kd * (u0 * u0)

    d = up_y(adj1, 0.0) - adj1
    base = base + by * d - down_y(ay * d, cy_ref[0, at, :] * adj1[0:1, :])
    d = up_z(adj1, 0.0) - adj1
    first_col = lane_first(cz_ref[...], 0) * adj1
    base = base + bz * d - down_z(az * d, first_col)

    @pl.when(i == 0)
    def _():
        qpp[...] = cx_ref[0] * adj1
        lx_ref[0] = adj1

    @pl.when(i > 0)
    def _():
        dx = adj1 - lp[...]
        fin_ref[i - 1] = gp[...] + bxp[...] * dx - qpp[...]
        qpp[...] = axp[...] * dx

    @pl.when(end)
    def _():
        fin_ref[CX - 1] = base - bx * adj1 - qpp[...]
        lx_ref[1] = adj1
        cx_ref[1] = bx

    gp[...] = base
    lp[...] = adj1
    bxp[...] = bx
    axp[...] = ax
    ly_ref[0, at, :] = adj1[0:1, :]
    ly_ref[1, at, :] = adj1[CY - 1:CY, :]
    cy_ref[1, at, :] = by[CY - 1:CY, :]
    packed_l = jnp.where(lane1 == i, adj1[:, 0:1], lz_ref[...])
    lz_ref[...] = jnp.where(lane1 == i + 32, adj1[:, CZ - 1:CZ], packed_l)
    cz_ref[...] = jnp.where(lane1 == i + 32, bz[:, CZ - 1:CZ], cz_ref[...])

    slots = slot_ref[0]
    hi_f[...] = (slots >> 7).astype(f32)
    lo_f[...] = (slots & 127).astype(f32)
    ids = lax.broadcasted_iota(i32, (128, CZ), 0).astype(f32).astype(bf16)
    zero, one = jnp.zeros((32, CZ), bf16), jnp.ones((32, CZ), bf16)
    row = lambda ref, y: jnp.broadcast_to(ref[y:y + 1, :], (32, CZ))
    for y in range(CY):
        span = slice(y * CZ, y * CZ + CZ)
        rest = row(term_f, y)
        mask = ids[0:32] == row(hi_f, y).astype(bf16)
        for k in range(DIGITS):
            digit = rest.astype(f8).astype(f32)
            hot_hi[32 * k:32 * k + 32, span] = jnp.where(mask, digit.astype(bf16), zero).astype(f8)
            if k < DIGITS - 1:
                rest = (rest - digit) * 16.0
        low = row(lo_f, y).astype(bf16)
        for j in range(4):
            at_j = slice(32 * j, 32 * j + 32)
            hot_lo[at_j, span] = jnp.where(ids[at_j] == low, one, zero).astype(f8)

    @pl.when(end)
    def _():
        total[...] = total[...] + products()
        by_lane = total[...].T
        sums = by_lane[32 * DIGITS - 32:32 * DIGITS]
        for k in range(DIGITS - 2, -1, -1):
            sums = by_lane[32 * k:32 * k + 32] + sums * (1.0 / 16.0)
        places = places_ref[...]
        high = sums.astype(bf16)
        high_f = high.astype(f32)
        low_f = sums - high_f
        place_lane = (places & 127).astype(f32)
        place_row = places >> 7
        lane_ids = lax.broadcasted_iota(i32, (128, 128), 0).astype(f32)

        row_ids = lax.broadcasted_iota(i32, (256, 128), 0).astype(f32).astype(bf16)
        row_f = place_row.astype(f32)
        ones, zeros = jnp.ones((256, 128), bf16), jnp.zeros((256, 128), bf16)

        values = []
        for s in range(32):
            match = lane_ids == place_lane[s:s + 1, :]
            values.append(
                jnp.concatenate(
                    [
                        jnp.where(match, high_f[s:s + 1, :], 0.0).astype(bf16),
                        jnp.where(match, low_f[s:s + 1, :], 0.0).astype(bf16),
                    ],
                    axis=0,
                )
            )
        value = jnp.concatenate(values, axis=1)

        def spread(n, carry):
            first = (n * 256).astype(f32)
            hot = jnp.concatenate(
                [
                    jnp.where(
                        row_ids == jnp.broadcast_to(row_f[s:s + 1, :] - first, (256, 128)).astype(bf16),
                        ones, zeros,
                    )
                    for s in range(32)
                ],
                axis=1,
            )
            got = lax.dot_general(
                hot, value, (((1,), (1,)), ((), ())), preferred_element_type=f32
            )
            dense_ref[pl.ds(pl.multiple_of(n * 256, 256), 256), :] = got[:, 0:128] + got[:, 128:256]
            return carry

        lax.fori_loop(0, 8, spread, 0)


def call_main(block, arrays, faces, home, slot_grain):
    conc, load, adj, adj_load, vx, vy, vz, solid, slot = arrays
    plane = pl.BlockSpec((1, CY, CZ), lambda i, b: (i, 0, 0))
    after = pl.BlockSpec((1, CY, CZ), lambda i, b: (jnp.minimum(i + 1, CX - 1), 0, 0))

    def whole(shape):
        return pl.BlockSpec(shape, lambda i, b: (0,) * len(shape))

    face_shapes = [
        (3, CY, CZ), (CY, CZ), (2, CY, CZ), (CY, CZ), (4, CX, CZ), (3, CX, CZ),
        (CY, 128), (CY, 128), (3, CX, CZ), (CY, 128), (2048, 128),
    ]
    out_shapes = [
        (CX, CY, CZ), (CX, CY, CZ), (2048, 128), (2, CY, CZ), (2, CX, CZ), (CY, 128),
        (2, CY, CZ), (2, CX, CZ), (CY, 128),
    ]
    plane_scratch = pltpu.VMEM((CY, CZ), f32)
    row_scratch = pltpu.VMEM((CX, CZ), f32)
    return pl.pallas_call(
        main_kernel,
        out_shape=[jax.ShapeDtypeStruct(s, f32) for s in out_shapes],
        grid_spec=pltpu.PrefetchScalarGridSpec(
            num_scalar_prefetch=1,
            grid=(CX,),
            in_specs=[plane, after, plane, after, plane, after, plane, plane, plane, plane, plane, plane]
            + [whole(s) for s in face_shapes]
            + [
                pl.BlockSpec((1, 16, 128), lambda i, b: (b[0], 0, 0)),
                pl.BlockSpec((1, 16, 128), lambda i, b: (lax.rem(b[0] + 1, 128), 0, 0)),
                whole((32, 128)),
            ],
            out_specs=[whole(out_shapes[0]), plane] + [whole(s) for s in out_shapes[2:]],
            scratch_shapes=[
                pltpu.VMEM((2048, 128), i32), pltpu.VMEM((32, 128), i32), pltpu.VMEM((16, 128), i32),
                plane_scratch, plane_scratch, row_scratch, row_scratch, pltpu.VMEM((CY, 128), f32),
                plane_scratch, plane_scratch, plane_scratch, plane_scratch, plane_scratch,
                plane_scratch, plane_scratch, plane_scratch,
                pltpu.VMEM((128, CY * CZ), f8), pltpu.VMEM((32 * DIGITS, CY * CZ), f8),
                pltpu.VMEM((128, 32 * DIGITS), f32), pltpu.VMEM((256, 4096), f32), pltpu.VMEM((32, 128), f32),
            ],
        ),
        compiler_params=pltpu.CompilerParams(
            dimension_semantics=("arbitrary",), vmem_limit_bytes=58 << 20
        ),
        cost_estimate=pl.CostEstimate(flops=10 ** 9, bytes_accessed=25 << 20, transcendentals=0),
    )(
        block, conc, conc, adj, adj, solid, solid, load, adj_load, vx, vy, vz, slot,
        *faces[:10], faces[10].reshape(2048, 128), home, home, slot_grain,
    )


def finish_kernel(
    fin, dense, lx, ly, lz, cx, cy, cz,
    out, grad,
    fbuf, xlo, xhi, ylo, yhi, zlo, zhi, d1, r1, r2, s2, r3, s3, r4, lsem, ssem, rsem,
):
    gx, gy, gz = (lax.axis_index(a) for a in ("gx", "gy", "gz"))
    xh, core = gx // 2, lax.rem(gx, 2)
    has = lambda cond: jnp.where(cond, 1.0, 0.0).astype(f32)
    hi_x, hi_y, hi_z = has(gx < 3), has(gy < 7), has(gz < 3)
    keep = pltpu.make_async_copy(dense.at[:, core], d1, lsem.at[0])
    keep.start()
    body = pltpu.make_async_copy(fin, fbuf, lsem.at[1])
    body.start()
    greet()
    started = []

    def send(src, dst, where):
        k = len(started)
        copy = pltpu.make_async_remote_copy(
            src_ref=src, dst_ref=dst, send_sem=ssem.at[k], recv_sem=rsem.at[k],
            device_id=where, device_id_type=MESH,
        )
        copy.start()
        started.append(copy)
        return copy

    first = send(dense.at[:, 1 - core], r1, {"gx": gx + 1 - 2 * core})
    faces = [
        send(lx.at[1], xlo, {"gx": lax.rem(gx + 1, 4)}),
        send(lx.at[0], xhi, {"gx": lax.rem(gx + 3, 4)}),
        send(ly.at[1], ylo, {"gy": lax.rem(gy + 1, 8)}),
        send(ly.at[0], yhi, {"gy": lax.rem(gy + 7, 8)}),
        send(lz, zlo, {"gz": lax.rem(gz + 1, 4)}),
        send(lz, zhi, {"gz": lax.rem(gz + 3, 4)}),
    ]
    keep.wait()
    first.wait_recv()

    def add_first(h, carry):
        for x in range(2):
            d1[x, h] = d1[x, h] + r1[x, h]
        return carry

    lax.fori_loop(0, 8, add_first, 0)
    second = [
        send(d1.at[:, lax.rem(gy + o, 8)], r2.at[o - 1], {"gy": lax.rem(gy + o, 8)})
        for o in range(1, 8)
    ]
    body.wait()
    for copy in faces:
        copy.wait_recv()
    fbuf[0] = fbuf[0] + cx[0] * xlo[...]
    fbuf[CX - 1] = fbuf[CX - 1] + cx[1] * (xhi[...] * hi_x)
    lane = lax.broadcasted_iota(i32, (CY, 128), 1)
    cols = cz[...] * jnp.where(
        lane < 32, pltpu.roll(zlo[...], 96, 1), pltpu.roll(zhi[...] * hi_z, 32, 1)
    )

    def fix(x, carry):
        at = pl.ds(x, 1)
        fbuf[x, 0:1, :] = fbuf[x, 0:1, :] + cy[0, at, :] * ylo[at, :]
        fbuf[x, CY - 1:CY, :] = fbuf[x, CY - 1:CY, :] + cy[1, at, :] * (yhi[at, :] * hi_y)
        low = pltpu.roll(cols, lax.rem(128 - x, 128), 1)
        high = pltpu.roll(cols, 95 - x, 1)
        fbuf[x, :, 0:128] = fbuf[x, :, 0:128] + jnp.where(lane == 0, low, 0.0)
        fbuf[x, :, 128:256] = fbuf[x, :, 128:256] + jnp.where(lane == 127, high, 0.0)
        return carry

    lax.fori_loop(0, CX, fix, 0)
    store = pltpu.make_async_copy(fbuf, out, lsem.at[2])
    store.start()
    for copy in second:
        copy.wait_recv()
    for x in range(2):
        acc = d1[x, gy]
        for o in range(7):
            acc = acc + r2[o, x]
        s2[x] = acc
    third = [
        send(s2.at[:, lax.rem(gz + o, 4)], r3.at[o - 1], {"gz": lax.rem(gz + o, 4)})
        for o in range(1, 4)
    ]
    for copy in third:
        copy.wait_recv()
    for x in range(2):
        s3[x] = s2[x, gz] + r3[0, x] + r3[1, x] + r3[2, x]
    last = send(s3.at[1 - xh], r4, {"gx": gx + 2 - 4 * xh})
    last.wait_recv()
    grad[...] = s3[xh] + r4[...]
    for copy in started:
        copy.wait_send()
    store.wait()


def call_finish(fin, dense, lx, ly, lz, cx, cy, cz):
    vmem = pl.BlockSpec(memory_space=pltpu.VMEM)
    return pl.pallas_call(
        finish_kernel,
        out_shape=(
            jax.ShapeDtypeStruct((CX, CY, CZ), f32), jax.ShapeDtypeStruct((16, 128), f32)
        ),
        in_specs=[ANY] * 5 + [vmem] * 3,
        out_specs=(ANY, vmem),
        scratch_shapes=[
            pltpu.VMEM((CX, CY, CZ), f32),
            pltpu.VMEM((CY, CZ), f32), pltpu.VMEM((CY, CZ), f32),
            pltpu.VMEM((CX, CZ), f32), pltpu.VMEM((CX, CZ), f32),
            pltpu.VMEM((CY, 128), f32), pltpu.VMEM((CY, 128), f32),
            pltpu.VMEM((2, 8, 4, 16, 128), f32), pltpu.VMEM((2, 8, 4, 16, 128), f32),
            pltpu.VMEM((7, 2, 4, 16, 128), f32), pltpu.VMEM((2, 4, 16, 128), f32),
            pltpu.VMEM((3, 2, 16, 128), f32), pltpu.VMEM((2, 16, 128), f32),
            pltpu.VMEM((16, 128), f32),
            pltpu.SemaphoreType.DMA((3,)), pltpu.SemaphoreType.DMA((18,)),
            pltpu.SemaphoreType.DMA((18,)),
        ],
        compiler_params=pltpu.CompilerParams(
            collective_id=1, has_side_effects=True, vmem_limit_bytes=62 << 20
        ),
    )(fin, dense, lx, ly, lz, cx, cy, cz)


def per_device(
    conc, load, adj_conc, adj_load, vel_x, vel_y, vel_z, solid, voxel_slot, slot_grain, grain_home, rates
):
    block = (lax.axis_index("gx") * 32 + lax.axis_index("gy") * 4 + lax.axis_index("gz")).astype(i32)
    faces = call_faces(conc, adj_conc, vel_x, vel_y, vel_z, solid, rates.reshape(16, 128))
    arrays = (conc, load, adj_conc, adj_load, vel_x, vel_y, vel_z, solid, voxel_slot)
    fin, load_start, dense, lx, ly, lz, cx, cy, cz = call_main(
        block.reshape(1), arrays, faces, grain_home.reshape(128, 16, 128), slot_grain.reshape(32, 128)
    )
    start, grad = call_finish(
        fin, dense.reshape(2, 2, 8, 4, 16, 128), lx, ly, lz, cx, cy, cz
    )
    return start, load_start, grad.reshape(2048)


def solution(mesh):
    cells = P("gx", "gy", "gz")
    every = P(("gx", "gy", "gz"))
    return jax.shard_map(
        per_device,
        mesh=mesh,
        in_specs=(cells,) * 9 + (P(("gx", "gy", "gz"), None), P(), every),
        out_specs=(cells, cells, every),
        check_vma=False,
    )
```

```python
import functools

import jax
import jax.numpy as jnp
from jax import lax
from jax.experimental import pallas as pl
from jax.experimental.pallas import tpu as pltpu
from jax.sharding import PartitionSpec as P

f32, bf16, i32, f8 = jnp.float32, jnp.bfloat16, jnp.int32, jnp.float8_e4m3fn
DIGITS = 3
CHUNKS = 4
MESH = pl.DeviceIdType.MESH
ANY = pl.BlockSpec(memory_space=pl.ANY)
dispersion = 0.06
rate_step = 0.2 / 65535.0
CX, CY, CZ = 32, 64, 256


def greet():
    barrier = pltpu.get_barrier_semaphore()
    for axis, count in (("gx", 4), ("gy", 8), ("gz", 4)):
        me = lax.axis_index(axis)
        for o in range(1, count):
            pl.semaphore_signal(
                barrier, inc=1, device_id={axis: lax.rem(me + o, count)}, device_id_type=MESH
            )
    pl.semaphore_wait(barrier, 13)


def weight_of(s):
    return 1.0 - 0.7 * s.astype(f32)


def pair(w0, w1, v):
    k = (dispersion * w0) * w1
    return k - jnp.minimum(v, 0.0), k + jnp.maximum(v, 0.0)


def plane_iotas():
    return (
        lax.broadcasted_iota(i32, (CY, CZ), 0),
        lax.broadcasted_iota(i32, (CY, CZ), 1),
        lax.broadcasted_iota(i32, (CY, 128), 1),
    )


def shifts(ri, li):
    return (
        lambda v: jnp.where(ri == CY - 1, 0.0, pltpu.roll(v, CY - 1, 0)),
        lambda v: jnp.where(ri == 0, 0.0, pltpu.roll(v, 1, 0)),
        lambda v: jnp.where(li == CZ - 1, 0.0, pltpu.roll(v, CZ - 1, 1)),
        lambda v: jnp.where(li == 0, 0.0, pltpu.roll(v, 1, 1)),
    )


def sender(started, ssem, rsem):
    def send(src, dst, where):
        k = len(started)
        copy = pltpu.make_async_remote_copy(
            src_ref=src, dst_ref=dst, send_sem=ssem.at[k], recv_sem=rsem.at[k],
            device_id=where, device_id_type=MESH,
        )
        copy.start()
        started.append(copy)
        return copy

    return send


def gather_faces(
    conc, adj, vx, vy, vz, solid, rates,
    xlo, xlo_s, xhi, xhi_s, ylo, yhi, zlo, zhi, yown, zown, yend, zend, rall, s1_out, s2_out,
    cb, lb, vxb, vyb, vzb, sb, s1, s2, hx, qx, yfwd, ybwd, zfwd, zbwd, lsem, rsem, osem, ssem,
):
    gx, gy, gz = (lax.axis_index(a) for a in ("gx", "gy", "gz"))
    xh, core = gx // 2, lax.rem(gx, 2)
    local = []
    for q in range(4):
        at = pl.ds(8 * q, 8)
        local.append([
            pltpu.make_async_copy(ref.at[at], buf.at[at], lsem.at[6 * q + k])
            for k, (ref, buf) in enumerate(
                ((conc, cb), (adj, lb), (solid, sb), (vx, vxb), (vy, vyb), (vz, vzb))
            )
        ])
        for copy in local[q]:
            copy.start()
    mine = pltpu.make_async_copy(rates, rall.at[xh, core, gy, gz], osem.at[0])
    mine.start()
    greet()

    started = []
    send = sender(started, ssem, rsem)
    first = send(rates, rall.at[xh, core, gy, gz], {"gx": gx + 2 - 4 * xh})
    right, left = {"gx": lax.rem(gx + 1, 4)}, {"gx": lax.rem(gx + 3, 4)}
    faces = []
    for k, ref in enumerate((conc, adj, vx)):
        faces.append(send(ref.at[CX - 1], xlo.at[k], right))
    faces.append(send(solid.at[CX - 1], xlo_s, right))
    for k, ref in enumerate((conc, adj)):
        faces.append(send(ref.at[0], xhi.at[k], left))
    faces.append(send(solid.at[0], xhi_s, left))

    hx[...] = jnp.zeros_like(hx)
    qx[...] = jnp.zeros_like(qx)
    zfwd[...] = jnp.zeros_like(zfwd)
    zbwd[...] = jnp.zeros_like(zbwd)

    def plane(x, carry):
        ri, li, lane = plane_iotas()
        up_y, down_y, up_z, down_z = shifts(ri, li)
        at = pl.ds(x, 1)
        nx = jnp.minimum(x + 1, CX - 1)
        inside = jnp.where(x < CX - 1, 1.0, 0.0).astype(f32)
        c, l, w = cb[x], lb[x], weight_of(sb[x])
        v_x, v_y, v_z = vxb[x], vyb[x], vzb[x]
        a, b = pair(w, weight_of(sb[nx]) * inside, v_x)
        flux = a * (cb[nx] * inside) - b * c
        div = c + flux - hx[...]
        hx[...] = flux
        d = lb[nx] * inside - l
        lap = l + b * d - qx[...]
        qx[...] = a * d
        a, b = pair(w, up_y(w), v_y)
        flux = a * up_y(c) - b * c
        div = div + flux - down_y(flux)
        d = up_y(l) - l
        lap = lap + b * d - down_y(a * d)
        a, b = pair(w, up_z(w), v_z)
        flux = a * up_z(c) - b * c
        s1[x] = div + flux - down_z(flux)
        d = up_z(l) - l
        s2[x] = lap + b * d - down_z(a * d)
        for k, v in enumerate((c, l, v_y, w)):
            yfwd[k, at, :] = v[CY - 1:CY, :]
        for k, v in enumerate((c, l, w)):
            ybwd[k, at, :] = v[0:1, :]
        pack = zfwd[...]
        for k, v in enumerate((c, l, v_z, w)):
            pack = jnp.where(lane == x + 32 * k, v[:, CZ - 1:CZ], pack)
        zfwd[...] = pack
        pack = zbwd[...]
        for k, v in enumerate((c, l, w)):
            pack = jnp.where(lane == x + 32 * k, v[:, 0:1], pack)
        zbwd[...] = pack
        return carry

    def arrived(q):
        for copy in local[q]:
            copy.wait()

    mine.wait()
    first.wait_recv()
    second = [
        send(rall.at[:, core, gy, gz], rall.at[:, core, gy, gz], {"gz": lax.rem(gz + o, 4)})
        for o in range(1, 4)
    ]
    arrived(0)
    arrived(1)
    lax.fori_loop(0, 5, plane, 0)
    for copy in second:
        copy.wait_recv()
    third = [
        send(rall.at[:, core, gy], rall.at[:, core, gy], {"gy": lax.rem(gy + o, 8)})
        for o in range(1, 8)
    ]
    arrived(2)
    arrived(3)
    lax.fori_loop(5, 24, plane, 0)
    for copy in third:
        copy.wait_recv()
    last = send(rall.at[:, core], rall.at[:, core], {"gx": gx + 1 - 2 * core})
    outs = [
        pltpu.make_async_copy(s1.at[0:24], s1_out.at[0:24], osem.at[1]),
        pltpu.make_async_copy(s2.at[0:24], s2_out.at[0:24], osem.at[2]),
    ]
    for copy in outs:
        copy.start()
    lax.fori_loop(24, CX, plane, 0)
    faces.append(send(yfwd, ylo, {"gy": lax.rem(gy + 1, 8)}))
    faces.append(send(ybwd, yhi, {"gy": lax.rem(gy + 7, 8)}))
    faces.append(send(zfwd, zlo, {"gz": lax.rem(gz + 1, 4)}))
    faces.append(send(zbwd, zhi, {"gz": lax.rem(gz + 3, 4)}))
    keep = [
        pltpu.make_async_copy(s1.at[24:32], s1_out.at[24:32], osem.at[3]),
        pltpu.make_async_copy(s2.at[24:32], s2_out.at[24:32], osem.at[4]),
        pltpu.make_async_copy(yfwd, yend, osem.at[5]),
        pltpu.make_async_copy(ybwd, yown, osem.at[6]),
        pltpu.make_async_copy(zfwd, zend, osem.at[7]),
        pltpu.make_async_copy(zbwd, zown, osem.at[8]),
    ]
    for copy in keep:
        copy.start()
    last.wait_recv()
    for copy in faces:
        copy.wait_recv()
    for copy in started:
        copy.wait_send()
    for copy in outs + keep:
        copy.wait()


def call_faces(conc, adj, vx, vy, vz, solid, rates):
    face = lambda *s: jax.ShapeDtypeStruct(s, f32)
    outs = (
        face(3, CY, CZ), jax.ShapeDtypeStruct((CY, CZ), i32),
        face(2, CY, CZ), jax.ShapeDtypeStruct((CY, CZ), i32),
        face(4, CX, CZ), face(3, CX, CZ),
        face(CY, 128), face(CY, 128), face(3, CX, CZ), face(CY, 128),
        face(4, CX, CZ), face(CY, 128),
        face(2, 2, 8, 4, 16, 128), face(CX, CY, CZ), face(CX, CY, CZ),
    )
    whole = pltpu.VMEM((CX, CY, CZ), f32)
    return pl.pallas_call(
        gather_faces,
        out_shape=outs,
        in_specs=[ANY] * 7,
        out_specs=[ANY] * len(outs),
        scratch_shapes=[
            whole, whole, whole, whole, whole, pltpu.VMEM((CX, CY, CZ), i32), whole, whole,
            pltpu.VMEM((CY, CZ), f32), pltpu.VMEM((CY, CZ), f32),
            pltpu.VMEM((4, CX, CZ), f32), pltpu.VMEM((3, CX, CZ), f32),
            pltpu.VMEM((CY, 128), f32), pltpu.VMEM((CY, 128), f32),
            pltpu.SemaphoreType.DMA((24,)), pltpu.SemaphoreType.DMA((23,)),
            pltpu.SemaphoreType.DMA((9,)), pltpu.SemaphoreType.DMA((23,)),
        ],
        compiler_params=pltpu.CompilerParams(
            collective_id=0, has_side_effects=True, vmem_limit_bytes=62 << 20
        ),
    )(conc, adj, vx, vy, vz, solid, rates)


def roll_tile(tile, shift):
    return pltpu.roll(tile, shift, 1)


def main_kernel(
    block_ref,
    s1_ref, s2_ref, conc_ref, adj_ref, solid_ref, load_ref, adjload_ref, slot_ref, vend_ref,
    xlo, xlo_s, xhi, xhi_s, ylo, yhi, zlo, zhi, yown, zown, yend, zend, rall, home0, home1, slot_grain,
    adj1_ref, base_ref, mstart_ref, dense_ref, ly_ref, lz_ref, cx_ref, cy_ref, cz_ref,
    packed, places_ref, table, xc, yc, zc,
    hi_f, lo_f, term_f, hot_lo, hot_hi, total, got_ref, look_ref,
):
    i = pl.program_id(0)
    gx, gy, gz = (lax.axis_index(a) for a in ("gx", "gy", "gz"))
    has = lambda cond: jnp.where(cond, 1.0, 0.0).astype(f32)
    lo_x, hi_x = has(gx > 0), has(gx < 3)
    lo_y, hi_y = has(gy > 0), has(gy < 7)
    lo_z, hi_z = has(gz > 0), has(gz < 3)
    lane1 = lax.broadcasted_iota(i32, (CY, 128), 1)
    @pl.when(i == 0)
    def _():
        total[...] = jnp.zeros_like(total)
        hot_lo[...] = jnp.zeros_like(hot_lo)
        hot_hi[...] = jnp.zeros_like(hot_hi)
        def pack(r, carry):
            at = pl.ds(pl.multiple_of(r * 128, 128), 128)
            packed[at, :] = (rall[at, :] * (1.0 / rate_step) + 0.5).astype(i32)
            return carry

        lax.fori_loop(0, 16, pack, 0)
        base = (slot_grain[...] - block_ref[0] * 2048) & 262143
        lanes = [base[8 * j:8 * j + 8] & 127 for j in range(4)]
        rows = [base[8 * j:8 * j + 8] >> 7 for j in range(4)]
        found = [jnp.zeros((8, 128), i32)] * 4
        for r in range(32):
            src = home0 if r < 16 else home1
            row = jnp.broadcast_to(src[0, r % 16:r % 16 + 1, :], (8, 128))
            for j in range(4):
                found[j] = jnp.where(
                    rows[j] == r, jnp.take_along_axis(row, lanes[j], axis=1), found[j]
                )
        for j in range(4):
            places_ref[8 * j:8 * j + 8, :] = found[j]
        lanes = [f & 127 for f in found]
        rows = [(f >> 7) & 1023 for f in found]


        sub_ids = lax.broadcasted_iota(i32, (256, 128), 0).astype(f32).astype(bf16)
        ones, zeros = jnp.ones((256, 128), bf16), jnp.zeros((256, 128), bf16)

        def look(n, acc):
            at = pl.ds(pl.multiple_of(n * 256, 256), 256)
            q = packed[at, :]
            digits = jnp.concatenate([(q & 255).astype(f32).astype(bf16), ((q >> 8) & 255).astype(f32).astype(bf16)], axis=1)
            first = (n * 256).astype(f32)
            hot = jnp.concatenate(
                [
                    jnp.where(
                        sub_ids == jnp.broadcast_to((found[s // 8] >> 7).astype(f32)[s % 8:s % 8 + 1, :] - first, (256, 128)).astype(bf16),
                        ones, zeros,
                    )
                    for s in range(32)
                ],
                axis=1,
            )
            got_ref[...] = got_ref[...] + lax.dot_general(digits, hot, (((0,), (0,)), ((), ())), preferred_element_type=f32)
            return acc
        got_ref[...] = jnp.zeros_like(got_ref)
        lax.fori_loop(0, 8, look, 0)
        lids = lax.broadcasted_iota(i32, (128, 128), 0)
        for s in range(32):
            m = lids == (found[s // 8] & 127)[s % 8:s % 8 + 1, :]
            sp = slice(128 * s, 128 * s + 128)
            v = got_ref[0:128, sp] + 256.0 * got_ref[128:256, sp]
            look_ref[s:s + 1, :] = jnp.sum(jnp.where(m, v, 0.0), axis=0, keepdims=True)
        got = [look_ref[8 * j:8 * j + 8, :].astype(i32) for j in range(4)]
        table[0:8, :] = got[0] + (got[2] << 16)
        table[8:16, :] = got[1] + (got[3] << 16)

        a, b = pair(weight_of(xlo_s[...]) * lo_x, weight_of(solid_ref[0]), xlo[2] * lo_x)
        xc[0] = b * (xlo[0] * lo_x) - a * conc_ref[0]
        xc[1] = a * (xlo[1] * lo_x - adj_ref[0])
        cx_ref[0] = a
        a, b = pair(ylo[3] * lo_y, yown[2], ylo[2] * lo_y)
        yc[0] = b * (ylo[0] * lo_y) - a * yown[0]
        yc[1] = a * (ylo[1] * lo_y - yown[1])
        cy_ref[0] = a
        k = (dispersion * yend[3]) * (yhi[2] * hi_y)
        a, b = k - jnp.minimum(yend[2], 0.0), k + jnp.maximum(yend[2], 0.0)
        yc[2] = a * (yhi[0] * hi_y) - k * yend[0]
        yc[3] = b * (yhi[1] * hi_y) - k * yend[1]
        cy_ref[1] = b
        cy_ref[2] = k
        low, own = zlo[...] * lo_z, zown[...]
        a, b = pair(roll_tile(low, 32), roll_tile(own, 64), roll_tile(low, 64))
        low_c = b * low - a * own
        low_l = a * (roll_tile(low, 96) - roll_tile(own, 96))
        coef = jnp.where(lane1 < 32, a, 0.0)
        high, own = zhi[...] * hi_z, zend[...]
        k = (dispersion * roll_tile(own, 32)) * roll_tile(high, 64)
        v = roll_tile(own, 64)
        a, b = k - jnp.minimum(v, 0.0), k + jnp.maximum(v, 0.0)
        high_c = a * high - k * own
        high_l = b * roll_tile(high, 96) - k * roll_tile(own, 96)

        def lay(parts):
            out = parts[0]
            for n in range(1, 4):
                out = jnp.where(lane1 >= 32 * n, roll_tile(parts[n], 32 * n), out)
            return out

        zc[...] = lay([low_c, low_l, high_c, high_l])
        cz_ref[...] = lay([coef, b, k, jnp.zeros_like(k)])
        lz_ref[...] = jnp.zeros_like(lz_ref)

    @pl.when(i == CX - 1)
    def _():
        k = (dispersion * weight_of(solid_ref[0])) * (weight_of(xhi_s[...]) * hi_x)
        v = vend_ref[0]
        a, b = k - jnp.minimum(v, 0.0), k + jnp.maximum(v, 0.0)
        xc[0] = a * (xhi[0] * hi_x) - k * conc_ref[0]
        xc[1] = b * (xhi[1] * hi_x) - k * adj_ref[0]
        cx_ref[1] = b
        cx_ref[2] = k

    def products():
        acc = None
        for chunk in range(CHUNKS):
            span = slice(chunk * (CY * CZ // CHUNKS), (chunk + 1) * (CY * CZ // CHUNKS))
            got = lax.dot_general(
                hot_lo[:, span], hot_hi[:, span], (((1,), (1,)), ((), ())), preferred_element_type=f32
            )
            acc = got if acc is None else acc + got
        return acc

    total[...] = total[...] + products()
    at = pl.ds(i, 1)
    end = i == CX - 1
    ri = lax.broadcasted_iota(i32, (8, CZ), 0)
    edge = jnp.where((i == 0) | end, 1.0, 0.0).astype(f32)

    def with_faces(v, n):
        v = v + edge * xc[n]
        low = roll_tile(zc[...], lax.rem(256 - i - 32 * n, 128))
        high = roll_tile(zc[...], lax.rem(319 - i - 32 * n, 128))
        v = v + jnp.concatenate(
            [jnp.where(lane1 == 0, low, 0.0), jnp.where(lane1 == 127, high, 0.0)], axis=1
        )
        first = v[0:8, :] + jnp.where(ri == 0, yc[n, at, :], 0.0)
        final = v[CY - 8:CY, :] + jnp.where(ri == 7, yc[2 + n, at, :], 0.0)
        return jnp.concatenate([first, v[8:CY - 8, :], final], axis=0)

    c, l = conc_ref[0], adj_ref[0]
    sol = solid_ref[0].astype(f32)

    lookups = []
    for g in range(CY // 8):
        halves = []
        for h in range(2):
            s = slot_ref[0, 8 * g:8 * g + 8, 128 * h:128 * h + 128]
            lo, hi = s & 127, s >> 7
            level = [
                jnp.take_along_axis(jnp.broadcast_to(table[r:r + 1, :], (8, 128)), lo, axis=1)
                for r in range(16)
            ]
            for bit in range(4):
                mask = (hi & (1 << bit)) != 0
                level = [
                    jnp.where(mask, level[2 * j + 1], level[2 * j]) for j in range(len(level) // 2)
                ]
            p = level[0]
            value = jnp.where((hi & 16) != 0, lax.shift_right_logical(p, 16), p & 65535)
            halves.append(value.astype(f32) * rate_step)
        lookups.append(jnp.concatenate(halves, axis=1))
    kv = sol * jnp.concatenate(lookups, axis=0)

    def inverse(v):
        r = pl.reciprocal(v, approx=True)
        return r * (2.0 - v * r)

    m = adjload_ref[0]
    u0 = inverse(1.0 + c)
    e0 = c * u0 - load_ref[0]
    r = kv * e0
    conc1 = with_faces(s1_ref[0], 0) - r
    load1 = load_ref[0] + r
    d1 = m - l
    u1 = inverse(1.0 + conc1)
    kd = kv * d1
    adj1 = with_faces(s2_ref[0], 1) + kd * (u1 * u1)
    m1 = m - kd
    d0 = m1 - adj1
    kd = kv * d0
    mstart_ref[0] = m1 - kd
    term_f[...] = sol * ((conc1 * u1 - load1) * d1 + e0 * d0)
    base_ref[0] = adj1 + kd * (u0 * u0)
    adj1_ref[0] = adj1
    ly_ref[0, at, :] = adj1[0:1, :]
    ly_ref[1, at, :] = adj1[CY - 1:CY, :]
    packed_l = jnp.where(lane1 == i, adj1[:, 0:1], lz_ref[...])
    lz_ref[...] = jnp.where(lane1 == i + 32, adj1[:, CZ - 1:CZ], packed_l)

    slots = slot_ref[0]
    hi_f[...] = (slots >> 7).astype(f32)
    lo_f[...] = (slots & 127).astype(f32)
    ids = lax.broadcasted_iota(i32, (128, CZ), 0).astype(f32).astype(bf16)
    zero, one = jnp.zeros((32, CZ), bf16), jnp.ones((32, CZ), bf16)
    row = lambda ref, y: jnp.broadcast_to(ref[y:y + 1, :], (32, CZ))
    for y in range(CY):
        span = slice(y * CZ, y * CZ + CZ)
        rest = row(term_f, y)
        mask = ids[0:32] == row(hi_f, y).astype(bf16)
        for k in range(DIGITS):
            digit = rest.astype(f8).astype(f32)
            hot_hi[32 * k:32 * k + 32, span] = jnp.where(mask, digit.astype(bf16), zero).astype(f8)
            if k < DIGITS - 1:
                rest = (rest - digit) * 16.0
        low = row(lo_f, y).astype(bf16)
        for j in range(4):
            at_j = slice(32 * j, 32 * j + 32)
            hot_lo[at_j, span] = jnp.where(ids[at_j] == low, one, zero).astype(f8)

    @pl.when(end)
    def _():
        total[...] = total[...] + products()
        by_lane = total[...].T
        sums = by_lane[32 * DIGITS - 32:32 * DIGITS]
        for k in range(DIGITS - 2, -1, -1):
            sums = by_lane[32 * k:32 * k + 32] + sums * (1.0 / 16.0)
        places = places_ref[...]
        high = sums.astype(bf16)
        high_f = high.astype(f32)
        low_f = sums - high_f
        place_lane = (places & 127).astype(f32)
        place_row = places >> 7
        lane_ids = lax.broadcasted_iota(i32, (128, 128), 0).astype(f32)

        row_ids = lax.broadcasted_iota(i32, (256, 128), 0).astype(f32).astype(bf16)
        row_f = place_row.astype(f32)
        ones, zeros = jnp.ones((256, 128), bf16), jnp.zeros((256, 128), bf16)

        values = []
        for s in range(32):
            match = lane_ids == place_lane[s:s + 1, :]
            values.append(
                jnp.concatenate(
                    [
                        jnp.where(match, high_f[s:s + 1, :], 0.0).astype(bf16),
                        jnp.where(match, low_f[s:s + 1, :], 0.0).astype(bf16),
                    ],
                    axis=0,
                )
            )
        value = jnp.concatenate(values, axis=1)

        def spread(n, carry):
            first = (n * 256).astype(f32)
            hot = jnp.concatenate(
                [
                    jnp.where(
                        row_ids == jnp.broadcast_to(row_f[s:s + 1, :] - first, (256, 128)).astype(bf16),
                        ones, zeros,
                    )
                    for s in range(32)
                ],
                axis=1,
            )
            got = lax.dot_general(
                hot, value, (((1,), (1,)), ((), ())), preferred_element_type=f32
            )
            dense_ref[pl.ds(pl.multiple_of(n * 256, 256), 256), :] = got[:, 0:128] + got[:, 128:256]
            return carry

        lax.fori_loop(0, 8, spread, 0)


def call_main(block, arrays, faces, home, slot_grain):
    conc, load, adj, adj_load, vx, solid, slot = arrays
    plane = pl.BlockSpec((1, CY, CZ), lambda i, b: (i, 0, 0))

    def whole(shape):
        return pl.BlockSpec(shape, lambda i, b: (0,) * len(shape))

    face_shapes = [
        (3, CY, CZ), (CY, CZ), (2, CY, CZ), (CY, CZ), (4, CX, CZ), (3, CX, CZ),
        (CY, 128), (CY, 128), (3, CX, CZ), (CY, 128), (4, CX, CZ), (CY, 128), (2048, 128),
    ]
    block_shape = (CX, CY, CZ)
    out_shapes = [
        block_shape, block_shape, block_shape, (2048, 128), (2, CX, CZ), (CY, 128),
        (3, CY, CZ), (3, CX, CZ), (CY, 128),
    ]
    plane_scratch = pltpu.VMEM((CY, CZ), f32)
    return pl.pallas_call(
        main_kernel,
        out_shape=[jax.ShapeDtypeStruct(s, f32) for s in out_shapes],
        grid_spec=pltpu.PrefetchScalarGridSpec(
            num_scalar_prefetch=1,
            grid=(CX,),
            in_specs=[plane] * 8
            + [pl.BlockSpec((1, CY, CZ), lambda i, b: (CX - 1, 0, 0))]
            + [whole(s) for s in face_shapes]
            + [
                pl.BlockSpec((1, 16, 128), lambda i, b: (b[0], 0, 0)),
                pl.BlockSpec((1, 16, 128), lambda i, b: (lax.rem(b[0] + 1, 128), 0, 0)),
                whole((32, 128)),
            ],
            out_specs=[plane] * 3 + [whole(s) for s in out_shapes[3:]],
            scratch_shapes=[
                pltpu.VMEM((2048, 128), i32), pltpu.VMEM((32, 128), i32), pltpu.VMEM((16, 128), i32),
                pltpu.VMEM((2, CY, CZ), f32), pltpu.VMEM((4, CX, CZ), f32), pltpu.VMEM((CY, 128), f32),
                plane_scratch, plane_scratch, plane_scratch,
                pltpu.VMEM((128, CY * CZ), f8), pltpu.VMEM((32 * DIGITS, CY * CZ), f8),
                pltpu.VMEM((128, 32 * DIGITS), f32), pltpu.VMEM((256, 4096), f32), pltpu.VMEM((32, 128), f32),
            ],
        ),
        compiler_params=pltpu.CompilerParams(
            dimension_semantics=("arbitrary",), vmem_limit_bytes=58 << 20
        ),
        cost_estimate=pl.CostEstimate(flops=10 ** 9, bytes_accessed=25 << 20, transcendentals=0),
    )(
        block, faces[13], faces[14], conc, adj, solid, load, adj_load, slot, vx,
        *faces[:12], faces[12].reshape(2048, 128), home, home, slot_grain,
    )


def finish_kernel(
    adj1, base, solid, vx, vy, vz, dense, ly, lz, cx, cy, cz,
    out, grad,
    lb, fb, sb, vxb, vyb, vzb, qx, yc, zc,
    xlo, xhi, ylo, yhi, zlo, zhi, d1, r1, r2, s2, r3, s3, r4, lsem, ssem, rsem,
):
    gx, gy, gz = (lax.axis_index(a) for a in ("gx", "gy", "gz"))
    xh, core = gx // 2, lax.rem(gx, 2)
    has = lambda cond: jnp.where(cond, 1.0, 0.0).astype(f32)
    hi_x, hi_y, hi_z = has(gx < 3), has(gy < 7), has(gz < 3)
    keep = pltpu.make_async_copy(dense.at[:, core], d1, lsem.at[0])
    keep.start()
    loads = [
        pltpu.make_async_copy(ref, buf, lsem.at[1 + k])
        for k, (ref, buf) in enumerate(
            ((adj1, lb), (base, fb), (solid, sb), (vx, vxb), (vy, vyb), (vz, vzb))
        )
    ]
    for copy in loads:
        copy.start()
    greet()
    started = []
    send = sender(started, ssem, rsem)
    first = send(dense.at[:, 1 - core], r1, {"gx": gx + 1 - 2 * core})
    faces = [
        send(adj1.at[CX - 1], xlo, {"gx": lax.rem(gx + 1, 4)}),
        send(adj1.at[0], xhi, {"gx": lax.rem(gx + 3, 4)}),
        send(ly.at[1], ylo, {"gy": lax.rem(gy + 1, 8)}),
        send(ly.at[0], yhi, {"gy": lax.rem(gy + 7, 8)}),
        send(lz, zlo, {"gz": lax.rem(gz + 1, 4)}),
        send(lz, zhi, {"gz": lax.rem(gz + 3, 4)}),
    ]
    keep.wait()
    first.wait_recv()

    def add_first(h, carry):
        for x in range(2):
            d1[x, h] = d1[x, h] + r1[x, h]
        return carry

    lax.fori_loop(0, 8, add_first, 0)
    second = [
        send(d1.at[:, lax.rem(gy + o, 8)], r2.at[o - 1], {"gy": lax.rem(gy + o, 8)})
        for o in range(1, 8)
    ]
    for copy in loads:
        copy.wait()
    for copy in faces:
        copy.wait_recv()
    fb[0] = fb[0] + cx[0] * (xlo[...] - lb[0])
    fb[CX - 1] = fb[CX - 1] + cx[1] * (xhi[...] * hi_x) - cx[2] * lb[CX - 1]
    yc[0] = cy[0] * (ylo[...] - ly[0])
    yc[1] = cy[1] * (yhi[...] * hi_y) - cy[2] * ly[1]
    lane1 = lax.broadcasted_iota(i32, (CY, 128), 1)
    own, coef = lz[...], cz[...]
    zc[...] = jnp.where(
        lane1 < 32,
        coef * (pltpu.roll(zlo[...], 96, 1) - own),
        coef * (pltpu.roll(zhi[...], 32, 1) * hi_z) - pltpu.roll(coef, 96, 1) * own,
    )
    qx[...] = jnp.zeros_like(qx)

    def plane(x, carry):
        ri, li, lane = plane_iotas()
        up_y, down_y, up_z, down_z = shifts(ri, li)
        at = pl.ds(x, 1)
        nx = jnp.minimum(x + 1, CX - 1)
        inside = jnp.where(x < CX - 1, 1.0, 0.0).astype(f32)
        l, w = lb[x], weight_of(sb[x])
        a, b = pair(w, weight_of(sb[nx]) * inside, vxb[x])
        d = lb[nx] * inside - l
        lap = fb[x] + b * d - qx[...]
        qx[...] = a * d
        a, b = pair(w, up_y(w), vyb[x])
        d = up_y(l) - l
        lap = lap + b * d - down_y(a * d)
        a, b = pair(w, up_z(w), vzb[x])
        d = up_z(l) - l
        lap = lap + b * d - down_z(a * d)
        cols = zc[...]
        low = pltpu.roll(cols, lax.rem(128 - x, 128), 1)
        high = pltpu.roll(cols, 95 - x, 1)
        lap = lap + jnp.concatenate(
            [jnp.where(lane == 0, low, 0.0), jnp.where(lane == 127, high, 0.0)], axis=1
        )
        fb[x] = lap
        fb[x, 0:1, :] = lap[0:1, :] + yc[0, at, :]
        fb[x, CY - 1:CY, :] = lap[CY - 1:CY, :] + yc[1, at, :]
        return carry

    lax.fori_loop(0, 16, plane, 0)
    store = [pltpu.make_async_copy(fb.at[0:16], out.at[0:16], lsem.at[7])]
    store[0].start()
    for copy in second:
        copy.wait_recv()
    for x in range(2):
        acc = d1[x, gy]
        for o in range(7):
            acc = acc + r2[o, x]
        s2[x] = acc
    third = [
        send(s2.at[:, lax.rem(gz + o, 4)], r3.at[o - 1], {"gz": lax.rem(gz + o, 4)})
        for o in range(1, 4)
    ]
    lax.fori_loop(16, 24, plane, 0)
    for copy in third:
        copy.wait_recv()
    for x in range(2):
        s3[x] = s2[x, gz] + r3[0, x] + r3[1, x] + r3[2, x]
    last = send(s3.at[1 - xh], r4, {"gx": gx + 2 - 4 * xh})
    lax.fori_loop(24, CX, plane, 0)
    store.append(pltpu.make_async_copy(fb.at[16:32], out.at[16:32], lsem.at[8]))
    store[1].start()
    last.wait_recv()
    grad[...] = s3[xh] + r4[...]
    for copy in started:
        copy.wait_send()
    for copy in store:
        copy.wait()


def call_finish(adj1, base, solid, vx, vy, vz, dense, ly, lz, cx, cy, cz):
    vmem = pl.BlockSpec(memory_space=pltpu.VMEM)
    whole = pltpu.VMEM((CX, CY, CZ), f32)
    return pl.pallas_call(
        finish_kernel,
        out_shape=(
            jax.ShapeDtypeStruct((CX, CY, CZ), f32), jax.ShapeDtypeStruct((16, 128), f32)
        ),
        in_specs=[ANY] * 7 + [vmem] * 5,
        out_specs=(ANY, vmem),
        scratch_shapes=[
            whole, whole, pltpu.VMEM((CX, CY, CZ), i32), whole, whole, whole,
            pltpu.VMEM((CY, CZ), f32), pltpu.VMEM((2, CX, CZ), f32), pltpu.VMEM((CY, 128), f32),
            pltpu.VMEM((CY, CZ), f32), pltpu.VMEM((CY, CZ), f32),
            pltpu.VMEM((CX, CZ), f32), pltpu.VMEM((CX, CZ), f32),
            pltpu.VMEM((CY, 128), f32), pltpu.VMEM((CY, 128), f32),
            pltpu.VMEM((2, 8, 4, 16, 128), f32), pltpu.VMEM((2, 8, 4, 16, 128), f32),
            pltpu.VMEM((7, 2, 4, 16, 128), f32), pltpu.VMEM((2, 4, 16, 128), f32),
            pltpu.VMEM((3, 2, 16, 128), f32), pltpu.VMEM((2, 16, 128), f32),
            pltpu.VMEM((16, 128), f32),
            pltpu.SemaphoreType.DMA((9,)), pltpu.SemaphoreType.DMA((18,)),
            pltpu.SemaphoreType.DMA((18,)),
        ],
        compiler_params=pltpu.CompilerParams(
            collective_id=1, has_side_effects=True, vmem_limit_bytes=62 << 20
        ),
    )(adj1, base, solid, vx, vy, vz, dense, ly, lz, cx, cy, cz)


def per_device(
    conc, load, adj_conc, adj_load, vel_x, vel_y, vel_z, solid, voxel_slot, slot_grain, grain_home, rates
):
    block = (lax.axis_index("gx") * 32 + lax.axis_index("gy") * 4 + lax.axis_index("gz")).astype(i32)
    faces = call_faces(conc, adj_conc, vel_x, vel_y, vel_z, solid, rates.reshape(16, 128))
    arrays = (conc, load, adj_conc, adj_load, vel_x, solid, voxel_slot)
    adj1, base, load_start, dense, ly, lz, cx, cy, cz = call_main(
        block.reshape(1), arrays, faces, grain_home.reshape(128, 16, 128), slot_grain.reshape(32, 128)
    )
    start, grad = call_finish(
        adj1, base, solid, vel_x, vel_y, vel_z, dense.reshape(2, 2, 8, 4, 16, 128), ly, lz, cx, cy, cz
    )
    return start, load_start, grad.reshape(2048)


def solution(mesh):
    cells = P("gx", "gy", "gz")
    every = P(("gx", "gy", "gz"))
    return jax.shard_map(
        per_device,
        mesh=mesh,
        in_specs=(cells,) * 9 + (P(("gx", "gy", "gz"), None), P(), every),
        out_specs=(cells, cells, every),
        check_vma=False,
    )
```

```python
import functools

import jax
import jax.numpy as jnp
from jax import lax
from jax.experimental import pallas as pl
from jax.experimental.pallas import tpu as pltpu
from jax.sharding import PartitionSpec as P

f32, bf16, i32, f8 = jnp.float32, jnp.bfloat16, jnp.int32, jnp.float8_e4m3fn
DIGITS = 3
CHUNKS = 4
PLANES = 2
MESH = pl.DeviceIdType.MESH
ANY = pl.BlockSpec(memory_space=pl.ANY)
dispersion = 0.06
rate_step = 0.2 / 65535.0
CX, CY, CZ = 32, 64, 256


def greet():
    barrier = pltpu.get_barrier_semaphore()
    for axis, count in (("gx", 4), ("gy", 8), ("gz", 4)):
        me = lax.axis_index(axis)
        for o in range(1, count):
            pl.semaphore_signal(
                barrier, inc=1, device_id={axis: lax.rem(me + o, count)}, device_id_type=MESH
            )
    pl.semaphore_wait(barrier, 13)


def weight_of(s):
    return 1.0 - 0.7 * s.astype(f32)


def pair(w0, w1, v):
    k = (dispersion * w0) * w1
    return k - jnp.minimum(v, 0.0), k + jnp.maximum(v, 0.0)


def plane_iotas():
    return (
        lax.broadcasted_iota(i32, (CY, CZ), 0),
        lax.broadcasted_iota(i32, (CY, CZ), 1),
        lax.broadcasted_iota(i32, (CY, 128), 1),
    )


def shifts(ri, li):
    return (
        lambda v: jnp.where(ri == CY - 1, 0.0, pltpu.roll(v, CY - 1, 0)),
        lambda v: jnp.where(ri == 0, 0.0, pltpu.roll(v, 1, 0)),
        lambda v: jnp.where(li == CZ - 1, 0.0, pltpu.roll(v, CZ - 1, 1)),
        lambda v: jnp.where(li == 0, 0.0, pltpu.roll(v, 1, 1)),
    )


def sender(started, ssem, rsem):
    def send(src, dst, where, slot=None):
        k = len(started) if slot is None else slot
        copy = pltpu.make_async_remote_copy(
            src_ref=src, dst_ref=dst, send_sem=ssem.at[k], recv_sem=rsem.at[k],
            device_id=where, device_id_type=MESH,
        )
        if slot is None:
            copy.start()
            started.append(copy)
        return copy

    return send


def each(copies, what):
    for copy in copies:
        getattr(copy, what)()


def gather_faces(
    conc, adj, vx, vy, vz, solid, rates,
    xlo, xlo_s, xhi, xhi_s, ylo, yhi, zlo, zhi, yown, zown, yend, zend, rall, s1_out, s2_out,
    cb, lb, vxb, vyb, vzb, sb, s1, s2, hx, qx, yfwd, ybwd, zfwd, zbwd, lsem, rsem, osem, ssem,
):
    gx, gy, gz = (lax.axis_index(a) for a in ("gx", "gy", "gz"))
    xh, core = gx // 2, lax.rem(gx, 2)
    local = []
    for q in range(4):
        at = pl.ds(8 * q, 8)
        local.append([
            pltpu.make_async_copy(ref.at[at], buf.at[at], lsem.at[6 * q + k])
            for k, (ref, buf) in enumerate(
                ((conc, cb), (adj, lb), (solid, sb), (vx, vxb), (vy, vyb), (vz, vzb))
            )
        ])
        for copy in local[q]:
            copy.start()
    mine = pltpu.make_async_copy(rates, rall.at[xh, core, gy, gz], osem.at[0])
    mine.start()
    greet()

    started = []
    send = sender(started, ssem, rsem)
    first = send(rates, rall.at[xh, core, gy, gz], {"gx": gx + 2 - 4 * xh})
    right, left = {"gx": lax.rem(gx + 1, 4)}, {"gx": lax.rem(gx + 3, 4)}
    faces = []
    for k, ref in enumerate((conc, adj, vx)):
        faces.append(send(ref.at[CX - 1], xlo.at[k], right))
    faces.append(send(solid.at[CX - 1], xlo_s, right))
    for k, ref in enumerate((conc, adj)):
        faces.append(send(ref.at[0], xhi.at[k], left))
    faces.append(send(solid.at[0], xhi_s, left))

    hx[...] = jnp.zeros_like(hx)
    qx[...] = jnp.zeros_like(qx)
    zfwd[...] = jnp.zeros_like(zfwd)
    zbwd[...] = jnp.zeros_like(zbwd)

    def plane(x, carry):
        ri, li, lane = plane_iotas()
        up_y, down_y, up_z, down_z = shifts(ri, li)
        at = pl.ds(x, 1)
        nx = jnp.minimum(x + 1, CX - 1)
        inside = jnp.where(x < CX - 1, 1.0, 0.0).astype(f32)
        c, l, w = cb[x], lb[x], weight_of(sb[x])
        v_x, v_y, v_z = vxb[x], vyb[x], vzb[x]
        a, b = pair(w, weight_of(sb[nx]) * inside, v_x)
        flux = a * (cb[nx] * inside) - b * c
        div = c + flux - hx[...]
        hx[...] = flux
        d = lb[nx] * inside - l
        lap = l + b * d - qx[...]
        qx[...] = a * d
        a, b = pair(w, up_y(w), v_y)
        flux = a * up_y(c) - b * c
        div = div + flux - down_y(flux)
        d = up_y(l) - l
        lap = lap + b * d - down_y(a * d)
        a, b = pair(w, up_z(w), v_z)
        flux = a * up_z(c) - b * c
        s1[x] = div + flux - down_z(flux)
        d = up_z(l) - l
        s2[x] = lap + b * d - down_z(a * d)
        for k, v in enumerate((c, l, v_y, w)):
            yfwd[k, at, :] = v[CY - 1:CY, :]
        for k, v in enumerate((c, l, w)):
            ybwd[k, at, :] = v[0:1, :]
        pack = zfwd[...]
        for k, v in enumerate((c, l, v_z, w)):
            pack = jnp.where(lane == x + 32 * k, v[:, CZ - 1:CZ], pack)
        zfwd[...] = pack
        pack = zbwd[...]
        for k, v in enumerate((c, l, w)):
            pack = jnp.where(lane == x + 32 * k, v[:, 0:1], pack)
        zbwd[...] = pack
        return carry

    def arrived(q):
        for copy in local[q]:
            copy.wait()

    mine.wait()
    first.wait_recv()
    one, row_y, row_z = rall.at[:, core, gy, gz], rall.at[:, core, gy], rall.at[:, core, :, gz]
    to_z = [{"gz": lax.rem(gz + o, 4)} for o in range(1, 4)]
    to_y = [{"gy": lax.rem(gy + o, 8)} for o in range(1, 8)]
    second = (
        [send(one, one, where, 13 + n) for n, where in enumerate(to_z)],
        [send(one, one, where, 16 + n) for n, where in enumerate(to_y)],
    )
    third = (
        [send(row_y, row_y, where, 23 + n) for n, where in enumerate(to_y)],
        [send(row_z, row_z, where, 30 + n) for n, where in enumerate(to_z)],
    )
    for way in range(2):
        @pl.when(core == way)
        def _():
            each(second[way], "start")

    arrived(0)
    arrived(1)
    lax.fori_loop(0, 5, plane, 0)
    for way in range(2):
        @pl.when(core == way)
        def _():
            each(second[way], "wait_recv")
            each(third[way], "start")

    arrived(2)
    arrived(3)
    lax.fori_loop(5, 24, plane, 0)
    for way in range(2):
        @pl.when(core == way)
        def _():
            each(third[way], "wait_recv")
            each(second[way], "wait_send")
            each(third[way], "wait_send")

    last = send(rall.at[:, core], rall.at[:, core], {"gx": gx + 1 - 2 * core})
    outs = [
        pltpu.make_async_copy(s1.at[0:24], s1_out.at[0:24], osem.at[1]),
        pltpu.make_async_copy(s2.at[0:24], s2_out.at[0:24], osem.at[2]),
    ]
    for copy in outs:
        copy.start()
    lax.fori_loop(24, CX, plane, 0)
    faces.append(send(yfwd, ylo, {"gy": lax.rem(gy + 1, 8)}))
    faces.append(send(ybwd, yhi, {"gy": lax.rem(gy + 7, 8)}))
    faces.append(send(zfwd, zlo, {"gz": lax.rem(gz + 1, 4)}))
    faces.append(send(zbwd, zhi, {"gz": lax.rem(gz + 3, 4)}))
    keep = [
        pltpu.make_async_copy(s1.at[24:32], s1_out.at[24:32], osem.at[3]),
        pltpu.make_async_copy(s2.at[24:32], s2_out.at[24:32], osem.at[4]),
        pltpu.make_async_copy(yfwd, yend, osem.at[5]),
        pltpu.make_async_copy(ybwd, yown, osem.at[6]),
        pltpu.make_async_copy(zfwd, zend, osem.at[7]),
        pltpu.make_async_copy(zbwd, zown, osem.at[8]),
    ]
    for copy in keep:
        copy.start()
    last.wait_recv()
    for copy in faces:
        copy.wait_recv()
    for copy in started:
        copy.wait_send()
    for copy in outs + keep:
        copy.wait()


def call_faces(conc, adj, vx, vy, vz, solid, rates):
    face = lambda *s: jax.ShapeDtypeStruct(s, f32)
    outs = (
        face(3, CY, CZ), jax.ShapeDtypeStruct((CY, CZ), i32),
        face(2, CY, CZ), jax.ShapeDtypeStruct((CY, CZ), i32),
        face(4, CX, CZ), face(3, CX, CZ),
        face(CY, 128), face(CY, 128), face(3, CX, CZ), face(CY, 128),
        face(4, CX, CZ), face(CY, 128),
        face(2, 2, 8, 4, 16, 128), face(CX, CY, CZ), face(CX, CY, CZ),
    )
    whole = pltpu.VMEM((CX, CY, CZ), f32)
    return pl.pallas_call(
        gather_faces,
        out_shape=outs,
        in_specs=[ANY] * 7,
        out_specs=[ANY] * len(outs),
        scratch_shapes=[
            whole, whole, whole, whole, whole, pltpu.VMEM((CX, CY, CZ), i32), whole, whole,
            pltpu.VMEM((CY, CZ), f32), pltpu.VMEM((CY, CZ), f32),
            pltpu.VMEM((4, CX, CZ), f32), pltpu.VMEM((3, CX, CZ), f32),
            pltpu.VMEM((CY, 128), f32), pltpu.VMEM((CY, 128), f32),
            pltpu.SemaphoreType.DMA((24,)), pltpu.SemaphoreType.DMA((33,)),
            pltpu.SemaphoreType.DMA((9,)), pltpu.SemaphoreType.DMA((33,)),
        ],
        compiler_params=pltpu.CompilerParams(
            collective_id=0, has_side_effects=True, vmem_limit_bytes=62 << 20
        ),
    )(conc, adj, vx, vy, vz, solid, rates)


def roll_tile(tile, shift):
    return pltpu.roll(tile, shift, 1)


def main_kernel(
    block_ref,
    s1_ref, s2_ref, conc_ref, adj_ref, solid_ref, load_ref, adjload_ref, slot_ref, vend_ref,
    xlo, xlo_s, xhi, xhi_s, ylo, yhi, zlo, zhi, yown, zown, yend, zend, rall, home0, home1, slot_grain,
    adj1_ref, base_ref, mstart_ref, dense_ref, ly_ref, lz_ref, cx_ref, cy_ref, cz_ref,
    packed, places_ref, table, xc, yc, zc,
    hi_f, lo_f, term_f, hot_lo, hot_hi, total, got_ref, look_ref,
):
    step = pl.program_id(0)
    gx, gy, gz = (lax.axis_index(a) for a in ("gx", "gy", "gz"))
    has = lambda cond: jnp.where(cond, 1.0, 0.0).astype(f32)
    lo_x, hi_x = has(gx > 0), has(gx < 3)
    lo_y, hi_y = has(gy > 0), has(gy < 7)
    lo_z, hi_z = has(gz > 0), has(gz < 3)
    lane1 = lax.broadcasted_iota(i32, (CY, 128), 1)
    @pl.when(step == 0)
    def _():
        total[...] = jnp.zeros_like(total)
        hot_lo[...] = jnp.zeros_like(hot_lo)
        term_f[...] = jnp.zeros_like(term_f)
        hi_f[...] = jnp.zeros_like(hi_f)
        lo_f[...] = jnp.zeros_like(lo_f)
        hot_hi[...] = jnp.zeros_like(hot_hi)
        def pack(r, carry):
            at = pl.ds(pl.multiple_of(r * 128, 128), 128)
            packed[at, :] = (rall[at, :] * (1.0 / rate_step) + 0.5).astype(i32)
            return carry

        lax.fori_loop(0, 16, pack, 0)
        base = (slot_grain[...] - block_ref[0] * 2048) & 262143
        lanes = [base[8 * j:8 * j + 8] & 127 for j in range(4)]
        rows = [base[8 * j:8 * j + 8] >> 7 for j in range(4)]
        found = [jnp.zeros((8, 128), i32)] * 4
        for r in range(32):
            src = home0 if r < 16 else home1
            row = jnp.broadcast_to(src[0, r % 16:r % 16 + 1, :], (8, 128))
            for j in range(4):
                found[j] = jnp.where(
                    rows[j] == r, jnp.take_along_axis(row, lanes[j], axis=1), found[j]
                )
        for j in range(4):
            places_ref[8 * j:8 * j + 8, :] = found[j]
        lanes = [f & 127 for f in found]
        rows = [(f >> 7) & 1023 for f in found]


        sub_ids = lax.broadcasted_iota(i32, (256, 128), 0).astype(f32).astype(bf16)
        ones, zeros = jnp.ones((256, 128), bf16), jnp.zeros((256, 128), bf16)

        def look(n, acc):
            at = pl.ds(pl.multiple_of(n * 256, 256), 256)
            q = packed[at, :]
            digits = jnp.concatenate([(q & 255).astype(f32).astype(bf16), ((q >> 8) & 255).astype(f32).astype(bf16)], axis=1)
            first = (n * 256).astype(f32)
            hot = jnp.concatenate(
                [
                    jnp.where(
                        sub_ids == jnp.broadcast_to((found[s // 8] >> 7).astype(f32)[s % 8:s % 8 + 1, :] - first, (256, 128)).astype(bf16),
                        ones, zeros,
                    )
                    for s in range(32)
                ],
                axis=1,
            )
            got_ref[...] = got_ref[...] + lax.dot_general(digits, hot, (((0,), (0,)), ((), ())), preferred_element_type=f32)
            return acc
        got_ref[...] = jnp.zeros_like(got_ref)
        lax.fori_loop(0, 8, look, 0)
        lids = lax.broadcasted_iota(i32, (128, 128), 0)
        for s in range(32):
            m = lids == (found[s // 8] & 127)[s % 8:s % 8 + 1, :]
            sp = slice(128 * s, 128 * s + 128)
            v = got_ref[0:128, sp] + 256.0 * got_ref[128:256, sp]
            look_ref[s:s + 1, :] = jnp.sum(jnp.where(m, v, 0.0), axis=0, keepdims=True)
        got = [look_ref[8 * j:8 * j + 8, :].astype(i32) for j in range(4)]
        table[0:8, :] = got[0] + (got[2] << 16)
        table[8:16, :] = got[1] + (got[3] << 16)

        a, b = pair(weight_of(xlo_s[...]) * lo_x, weight_of(solid_ref[0]), xlo[2] * lo_x)
        xc[0] = b * (xlo[0] * lo_x) - a * conc_ref[0]
        xc[1] = a * (xlo[1] * lo_x - adj_ref[0])
        xc[2] = xc[0]
        xc[3] = xc[1]
        cx_ref[0] = a
        a, b = pair(ylo[3] * lo_y, yown[2], ylo[2] * lo_y)
        yc[0] = b * (ylo[0] * lo_y) - a * yown[0]
        yc[1] = a * (ylo[1] * lo_y - yown[1])
        cy_ref[0] = a
        k = (dispersion * yend[3]) * (yhi[2] * hi_y)
        a, b = k - jnp.minimum(yend[2], 0.0), k + jnp.maximum(yend[2], 0.0)
        yc[2] = a * (yhi[0] * hi_y) - k * yend[0]
        yc[3] = b * (yhi[1] * hi_y) - k * yend[1]
        cy_ref[1] = b
        cy_ref[2] = k
        low, own = zlo[...] * lo_z, zown[...]
        a, b = pair(roll_tile(low, 32), roll_tile(own, 64), roll_tile(low, 64))
        low_c = b * low - a * own
        low_l = a * (roll_tile(low, 96) - roll_tile(own, 96))
        coef = jnp.where(lane1 < 32, a, 0.0)
        high, own = zhi[...] * hi_z, zend[...]
        k = (dispersion * roll_tile(own, 32)) * roll_tile(high, 64)
        v = roll_tile(own, 64)
        a, b = k - jnp.minimum(v, 0.0), k + jnp.maximum(v, 0.0)
        high_c = a * high - k * own
        high_l = b * roll_tile(high, 96) - k * roll_tile(own, 96)

        def lay(parts):
            out = parts[0]
            for n in range(1, 4):
                out = jnp.where(lane1 >= 32 * n, roll_tile(parts[n], 32 * n), out)
            return out

        zc[...] = lay([low_c, low_l, high_c, high_l])
        cz_ref[...] = lay([coef, b, k, jnp.zeros_like(k)])
        lz_ref[...] = jnp.zeros_like(lz_ref)

    @pl.when(step == CX // PLANES - 1)
    def _():
        k = (dispersion * weight_of(solid_ref[PLANES - 1])) * (weight_of(xhi_s[...]) * hi_x)
        v = vend_ref[0]
        a, b = k - jnp.minimum(v, 0.0), k + jnp.maximum(v, 0.0)
        xc[2] = a * (xhi[0] * hi_x) - k * conc_ref[PLANES - 1]
        xc[3] = b * (xhi[1] * hi_x) - k * adj_ref[PLANES - 1]
        cx_ref[1] = b
        cx_ref[2] = k

    ids = lax.broadcasted_iota(i32, (128, CZ), 0).astype(f32).astype(bf16)
    zero, one = jnp.zeros((32, CZ), bf16), jnp.ones((32, CZ), bf16)
    rows_of = CY // CHUNKS
    width = rows_of * CZ

    def product(g):
        span = slice(g * width, (g + 1) * width)
        return lax.dot_general(
            hot_lo[:, span], hot_hi[:, span], (((1,), (1,)), ((), ())), preferred_element_type=f32
        )

    def make_hot(g):
        def row(plane):
            half = jnp.broadcast_to(plane, (16, CZ)).astype(bf16)
            return jnp.concatenate([half, half], axis=0)

        for y in range(g * rows_of, (g + 1) * rows_of):
            span = slice(y * CZ, y * CZ + CZ)
            mask = ids[0:32] == row(hi_f[y:y + 1, :])
            for k in range(DIGITS):
                hot_hi[32 * k:32 * k + 32, span] = jnp.where(mask, row(term_f[k, y:y + 1, :]), zero).astype(f8)
            low = row(lo_f[y:y + 1, :])
            for j in range(4):
                at_j = slice(32 * j, 32 * j + 32)
                hot_lo[at_j, span] = jnp.where(ids[at_j] == low, one, zero).astype(f8)

    def rate_of(p, g):
        halves = []
        for h in range(2):
            s = slot_ref[p, 8 * g:8 * g + 8, 128 * h:128 * h + 128]
            lo, hi = s & 127, s >> 7
            level = [
                jnp.take_along_axis(jnp.broadcast_to(table[r:r + 1, :], (8, 128)), lo, axis=1)
                for r in range(16)
            ]
            for bit in range(4):
                mask = (hi & (1 << bit)) != 0
                level = [
                    jnp.where(mask, level[2 * j + 1], level[2 * j]) for j in range(len(level) // 2)
                ]
            both = level[0]
            value = jnp.where((hi & 16) != 0, lax.shift_right_logical(both, 16), both & 65535)
            halves.append(value.astype(f32) * rate_step)
        return jnp.concatenate(halves, axis=1)

    def one_plane(p):
        i = step * PLANES + p
        acc = total[...]
        lookups = []
        per = CY // 8 // CHUNKS
        for g in range(CHUNKS):
            acc = acc + product(g)
            for n in range(per):
                lookups.append(rate_of(p, g * per + n))
            make_hot(g)
        total[...] = acc
        at = pl.ds(i, 1)
        end = i == CX - 1
        ri = lax.broadcasted_iota(i32, (8, CZ), 0)
        edge = jnp.where((i == 0) | end, 1.0, 0.0).astype(f32)
        edge_at = 0 if p == 0 else 2

        def with_faces(v, n):
            v = v + edge * xc[edge_at + n]
            low = roll_tile(zc[...], lax.rem(256 - i - 32 * n, 128))
            high = roll_tile(zc[...], lax.rem(319 - i - 32 * n, 128))
            v = v + jnp.concatenate(
                [jnp.where(lane1 == 0, low, 0.0), jnp.where(lane1 == 127, high, 0.0)], axis=1
            )
            first = v[0:8, :] + jnp.where(ri == 0, yc[n, at, :], 0.0)
            final = v[CY - 8:CY, :] + jnp.where(ri == 7, yc[2 + n, at, :], 0.0)
            return jnp.concatenate([first, v[8:CY - 8, :], final], axis=0)

        c, l = conc_ref[p], adj_ref[p]
        sol = solid_ref[p].astype(f32)

        kv = sol * jnp.concatenate(lookups, axis=0)

        def inverse(v):
            r = pl.reciprocal(v, approx=True)
            return r * (2.0 - v * r)

        m = adjload_ref[p]
        u0 = inverse(1.0 + c)
        e0 = c * u0 - load_ref[p]
        r = kv * e0
        conc1 = with_faces(s1_ref[p], 0) - r
        load1 = load_ref[p] + r
        d1 = m - l
        u1 = inverse(1.0 + conc1)
        kd = kv * d1
        adj1 = with_faces(s2_ref[p], 1) + kd * (u1 * u1)
        m1 = m - kd
        d0 = m1 - adj1
        kd = kv * d0
        mstart_ref[p] = m1 - kd
        rest = sol * ((conc1 * u1 - load1) * d1 + e0 * d0)
        for k in range(DIGITS):
            digit = rest.astype(f8).astype(f32)
            term_f[k] = digit
            rest = (rest - digit) * 16.0
        base_ref[p] = adj1 + kd * (u0 * u0)
        adj1_ref[p] = adj1
        ly_ref[0, at, :] = adj1[0:1, :]
        ly_ref[1, at, :] = adj1[CY - 1:CY, :]
        packed_l = jnp.where(lane1 == i, adj1[:, 0:1], lz_ref[...])
        lz_ref[...] = jnp.where(lane1 == i + 32, adj1[:, CZ - 1:CZ], packed_l)

        slots = slot_ref[p]
        hi_f[...] = (slots >> 7).astype(f32)
        lo_f[...] = (slots & 127).astype(f32)

    for p in range(PLANES):
        one_plane(p)

    @pl.when(step == CX // PLANES - 1)
    def _():
        for g in range(CHUNKS):
            total[...] = total[...] + product(g)
            make_hot(g)
        for g in range(CHUNKS):
            total[...] = total[...] + product(g)
        by_lane = total[...].T
        sums = by_lane[32 * DIGITS - 32:32 * DIGITS]
        for k in range(DIGITS - 2, -1, -1):
            sums = by_lane[32 * k:32 * k + 32] + sums * (1.0 / 16.0)
        places = places_ref[...]
        high = sums.astype(bf16)
        high_f = high.astype(f32)
        low_f = sums - high_f
        place_lane = (places & 127).astype(f32)
        place_row = places >> 7
        lane_ids = lax.broadcasted_iota(i32, (128, 128), 0).astype(f32)

        row_ids = lax.broadcasted_iota(i32, (256, 128), 0).astype(f32).astype(bf16)
        row_f = place_row.astype(f32)
        ones, zeros = jnp.ones((256, 128), bf16), jnp.zeros((256, 128), bf16)

        values = []
        for s in range(32):
            match = lane_ids == place_lane[s:s + 1, :]
            values.append(
                jnp.concatenate(
                    [
                        jnp.where(match, high_f[s:s + 1, :], 0.0).astype(bf16),
                        jnp.where(match, low_f[s:s + 1, :], 0.0).astype(bf16),
                    ],
                    axis=0,
                )
            )
        value = jnp.concatenate(values, axis=1)

        def spread(n, carry):
            first = (n * 256).astype(f32)
            hot = jnp.concatenate(
                [
                    jnp.where(
                        row_ids == jnp.broadcast_to(row_f[s:s + 1, :] - first, (256, 128)).astype(bf16),
                        ones, zeros,
                    )
                    for s in range(32)
                ],
                axis=1,
            )
            got = lax.dot_general(
                hot, value, (((1,), (1,)), ((), ())), preferred_element_type=f32
            )
            dense_ref[pl.ds(pl.multiple_of(n * 256, 256), 256), :] = got[:, 0:128] + got[:, 128:256]
            return carry

        lax.fori_loop(0, 8, spread, 0)


def call_main(block, arrays, faces, home, slot_grain):
    conc, load, adj, adj_load, vx, solid, slot = arrays
    plane = pl.BlockSpec((PLANES, CY, CZ), lambda i, b: (i, 0, 0))

    def whole(shape):
        return pl.BlockSpec(shape, lambda i, b: (0,) * len(shape))

    face_shapes = [
        (3, CY, CZ), (CY, CZ), (2, CY, CZ), (CY, CZ), (4, CX, CZ), (3, CX, CZ),
        (CY, 128), (CY, 128), (3, CX, CZ), (CY, 128), (4, CX, CZ), (CY, 128), (2048, 128),
    ]
    block_shape = (CX, CY, CZ)
    out_shapes = [
        block_shape, block_shape, block_shape, (2048, 128), (2, CX, CZ), (CY, 128),
        (3, CY, CZ), (3, CX, CZ), (CY, 128),
    ]
    plane_scratch = pltpu.VMEM((CY, CZ), f32)
    return pl.pallas_call(
        main_kernel,
        out_shape=[jax.ShapeDtypeStruct(s, f32) for s in out_shapes],
        grid_spec=pltpu.PrefetchScalarGridSpec(
            num_scalar_prefetch=1,
            grid=(CX // PLANES,),
            in_specs=[plane] * 8
            + [pl.BlockSpec((1, CY, CZ), lambda i, b: (CX - 1, 0, 0))]
            + [whole(s) for s in face_shapes]
            + [
                pl.BlockSpec((1, 16, 128), lambda i, b: (b[0], 0, 0)),
                pl.BlockSpec((1, 16, 128), lambda i, b: (lax.rem(b[0] + 1, 128), 0, 0)),
                whole((32, 128)),
            ],
            out_specs=[plane] * 3 + [whole(s) for s in out_shapes[3:]],
            scratch_shapes=[
                pltpu.VMEM((2048, 128), i32), pltpu.VMEM((32, 128), i32), pltpu.VMEM((16, 128), i32),
                pltpu.VMEM((4, CY, CZ), f32), pltpu.VMEM((4, CX, CZ), f32), pltpu.VMEM((CY, 128), f32),
                plane_scratch, plane_scratch, pltpu.VMEM((DIGITS, CY, CZ), f32),
                pltpu.VMEM((128, CY * CZ), f8), pltpu.VMEM((32 * DIGITS, CY * CZ), f8),
                pltpu.VMEM((128, 32 * DIGITS), f32), pltpu.VMEM((256, 4096), f32), pltpu.VMEM((32, 128), f32),
            ],
        ),
        compiler_params=pltpu.CompilerParams(
            dimension_semantics=("arbitrary",), vmem_limit_bytes=58 << 20
        ),
        cost_estimate=pl.CostEstimate(flops=10 ** 9, bytes_accessed=25 << 20, transcendentals=0),
    )(
        block, faces[13], faces[14], conc, adj, solid, load, adj_load, slot, vx,
        *faces[:12], faces[12].reshape(2048, 128), home, home, slot_grain,
    )


def finish_kernel(
    adj1, base, solid, vx, vy, vz, dense, ly, lz, cx, cy, cz,
    out, grad,
    lb, fb, sb, vxb, vyb, vzb, qx, yc, zc,
    xlo, xhi, ylo, yhi, zlo, zhi, d1, r1, r2y, r2z, s2y, s2z, r3z, r3y, s3, r4,
    lsem, ssem, rsem,
):
    gx, gy, gz = (lax.axis_index(a) for a in ("gx", "gy", "gz"))
    xh, core = gx // 2, lax.rem(gx, 2)
    has = lambda cond: jnp.where(cond, 1.0, 0.0).astype(f32)
    hi_x, hi_y, hi_z = has(gx < 3), has(gy < 7), has(gz < 3)
    keep = pltpu.make_async_copy(dense.at[:, core], d1, lsem.at[0])
    keep.start()
    loads = [
        pltpu.make_async_copy(ref, buf, lsem.at[1 + k])
        for k, (ref, buf) in enumerate(
            ((adj1, lb), (base, fb), (solid, sb), (vx, vxb), (vy, vyb), (vz, vzb))
        )
    ]
    for copy in loads:
        copy.start()
    greet()
    started = []
    send = sender(started, ssem, rsem)
    first = send(dense.at[:, 1 - core], r1, {"gx": gx + 1 - 2 * core})
    faces = [
        send(adj1.at[CX - 1], xlo, {"gx": lax.rem(gx + 1, 4)}),
        send(adj1.at[0], xhi, {"gx": lax.rem(gx + 3, 4)}),
        send(ly.at[1], ylo, {"gy": lax.rem(gy + 1, 8)}),
        send(ly.at[0], yhi, {"gy": lax.rem(gy + 7, 8)}),
        send(lz, zlo, {"gz": lax.rem(gz + 1, 4)}),
        send(lz, zhi, {"gz": lax.rem(gz + 3, 4)}),
    ]
    keep.wait()
    first.wait_recv()

    def add_first(h, carry):
        for x in range(2):
            d1[x, h] = d1[x, h] + r1[x, h]
        return carry

    lax.fori_loop(0, 8, add_first, 0)
    ys = [lax.rem(gy + o, 8) for o in range(1, 8)]
    zs = [lax.rem(gz + o, 4) for o in range(1, 4)]
    second = (
        [send(d1.at[:, y], r2y.at[n], {"gy": y}, 8 + n) for n, y in enumerate(ys)],
        [send(d1.at[:, :, z], r2z.at[n], {"gz": z}, 15 + n) for n, z in enumerate(zs)],
    )
    third = (
        [send(s2y.at[:, z], r3z.at[n], {"gz": z}, 18 + n) for n, z in enumerate(zs)],
        [send(s2z.at[:, y], r3y.at[n], {"gy": y}, 21 + n) for n, y in enumerate(ys)],
    )
    for way in range(2):
        @pl.when(core == way)
        def _():
            each(second[way], "start")

    for copy in loads:
        copy.wait()
    for copy in faces:
        copy.wait_recv()
    fb[0] = fb[0] + cx[0] * (xlo[...] - lb[0])
    fb[CX - 1] = fb[CX - 1] + cx[1] * (xhi[...] * hi_x) - cx[2] * lb[CX - 1]
    yc[0] = cy[0] * (ylo[...] - ly[0])
    yc[1] = cy[1] * (yhi[...] * hi_y) - cy[2] * ly[1]
    lane1 = lax.broadcasted_iota(i32, (CY, 128), 1)
    own, coef = lz[...], cz[...]
    zc[...] = jnp.where(
        lane1 < 32,
        coef * (pltpu.roll(zlo[...], 96, 1) - own),
        coef * (pltpu.roll(zhi[...], 32, 1) * hi_z) - pltpu.roll(coef, 96, 1) * own,
    )
    qx[...] = jnp.zeros_like(qx)

    def plane(x, carry):
        ri, li, lane = plane_iotas()
        up_y, down_y, up_z, down_z = shifts(ri, li)
        at = pl.ds(x, 1)
        nx = jnp.minimum(x + 1, CX - 1)
        inside = jnp.where(x < CX - 1, 1.0, 0.0).astype(f32)
        l, w = lb[x], weight_of(sb[x])
        a, b = pair(w, weight_of(sb[nx]) * inside, vxb[x])
        d = lb[nx] * inside - l
        lap = fb[x] + b * d - qx[...]
        qx[...] = a * d
        a, b = pair(w, up_y(w), vyb[x])
        d = up_y(l) - l
        lap = lap + b * d - down_y(a * d)
        a, b = pair(w, up_z(w), vzb[x])
        d = up_z(l) - l
        lap = lap + b * d - down_z(a * d)
        cols = zc[...]
        low = pltpu.roll(cols, lax.rem(128 - x, 128), 1)
        high = pltpu.roll(cols, 95 - x, 1)
        lap = lap + jnp.concatenate(
            [jnp.where(lane == 0, low, 0.0), jnp.where(lane == 127, high, 0.0)], axis=1
        )
        fb[x] = lap
        fb[x, 0:1, :] = lap[0:1, :] + yc[0, at, :]
        fb[x, CY - 1:CY, :] = lap[CY - 1:CY, :] + yc[1, at, :]
        return carry

    lax.fori_loop(0, 16, plane, 0)
    store = [pltpu.make_async_copy(fb.at[0:16], out.at[0:16], lsem.at[7])]
    store[0].start()
    for way in range(2):
        @pl.when(core == way)
        def _():
            each(second[way], "wait_recv")

    @pl.when(core == 0)
    def _():
        for x in range(2):
            acc = d1[x, gy]
            for o in range(7):
                acc = acc + r2y[o, x]
            s2y[x] = acc
        each(third[0], "start")

    @pl.when(core == 1)
    def _():
        for x in range(2):
            for h in range(8):
                acc = d1[x, h, gz]
                for o in range(3):
                    acc = acc + r2z[o, x, h]
                s2z[x, h] = acc
        each(third[1], "start")

    lax.fori_loop(16, 24, plane, 0)
    @pl.when(core == 0)
    def _():
        each(third[0], "wait_recv")
        for x in range(2):
            acc = s2y[x, gz]
            for o in range(3):
                acc = acc + r3z[o, x]
            s3[x] = acc
        each(second[0], "wait_send")
        each(third[0], "wait_send")

    @pl.when(core == 1)
    def _():
        each(third[1], "wait_recv")
        for x in range(2):
            acc = s2z[x, gy]
            for o in range(7):
                acc = acc + r3y[o, x]
            s3[x] = acc
        each(second[1], "wait_send")
        each(third[1], "wait_send")

    last = send(s3.at[1 - xh], r4, {"gx": gx + 2 - 4 * xh})
    lax.fori_loop(24, CX, plane, 0)
    store.append(pltpu.make_async_copy(fb.at[16:32], out.at[16:32], lsem.at[8]))
    store[1].start()
    last.wait_recv()
    grad[...] = s3[xh] + r4[...]
    for copy in started:
        copy.wait_send()
    for copy in store:
        copy.wait()


def call_finish(adj1, base, solid, vx, vy, vz, dense, ly, lz, cx, cy, cz):
    vmem = pl.BlockSpec(memory_space=pltpu.VMEM)
    whole = pltpu.VMEM((CX, CY, CZ), f32)
    return pl.pallas_call(
        finish_kernel,
        out_shape=(
            jax.ShapeDtypeStruct((CX, CY, CZ), f32), jax.ShapeDtypeStruct((16, 128), f32)
        ),
        in_specs=[ANY] * 7 + [vmem] * 5,
        out_specs=(ANY, vmem),
        scratch_shapes=[
            whole, whole, pltpu.VMEM((CX, CY, CZ), i32), whole, whole, whole,
            pltpu.VMEM((CY, CZ), f32), pltpu.VMEM((2, CX, CZ), f32), pltpu.VMEM((CY, 128), f32),
            pltpu.VMEM((CY, CZ), f32), pltpu.VMEM((CY, CZ), f32),
            pltpu.VMEM((CX, CZ), f32), pltpu.VMEM((CX, CZ), f32),
            pltpu.VMEM((CY, 128), f32), pltpu.VMEM((CY, 128), f32),
            pltpu.VMEM((2, 8, 4, 16, 128), f32), pltpu.VMEM((2, 8, 4, 16, 128), f32),
            pltpu.VMEM((7, 2, 4, 16, 128), f32), pltpu.VMEM((3, 2, 8, 16, 128), f32),
            pltpu.VMEM((2, 4, 16, 128), f32), pltpu.VMEM((2, 8, 16, 128), f32),
            pltpu.VMEM((3, 2, 16, 128), f32), pltpu.VMEM((7, 2, 16, 128), f32),
            pltpu.VMEM((2, 16, 128), f32), pltpu.VMEM((16, 128), f32),
            pltpu.SemaphoreType.DMA((9,)), pltpu.SemaphoreType.DMA((28,)),
            pltpu.SemaphoreType.DMA((28,)),
        ],
        compiler_params=pltpu.CompilerParams(
            collective_id=1, has_side_effects=True, vmem_limit_bytes=62 << 20
        ),
    )(adj1, base, solid, vx, vy, vz, dense, ly, lz, cx, cy, cz)


def per_device(
    conc, load, adj_conc, adj_load, vel_x, vel_y, vel_z, solid, voxel_slot, slot_grain, grain_home, rates
):
    block = (lax.axis_index("gx") * 32 + lax.axis_index("gy") * 4 + lax.axis_index("gz")).astype(i32)
    faces = call_faces(conc, adj_conc, vel_x, vel_y, vel_z, solid, rates.reshape(16, 128))
    arrays = (conc, load, adj_conc, adj_load, vel_x, solid, voxel_slot)
    adj1, base, load_start, dense, ly, lz, cx, cy, cz = call_main(
        block.reshape(1), arrays, faces, grain_home.reshape(128, 16, 128), slot_grain.reshape(32, 128)
    )
    start, grad = call_finish(
        adj1, base, solid, vel_x, vel_y, vel_z, dense.reshape(2, 2, 8, 4, 16, 128), ly, lz, cx, cy, cz
    )
    return start, load_start, grad.reshape(2048)


def solution(mesh):
    cells = P("gx", "gy", "gz")
    every = P(("gx", "gy", "gz"))
    return jax.shard_map(
        per_device,
        mesh=mesh,
        in_specs=(cells,) * 9 + (P(("gx", "gy", "gz"), None), P(), every),
        out_specs=(cells, cells, every),
        check_vma=False,
    )
```

```python
import functools

import jax
import jax.numpy as jnp
from jax import lax
from jax.experimental import pallas as pl
from jax.experimental.pallas import tpu as pltpu
from jax.sharding import PartitionSpec as P

f32, bf16, i32, f8 = jnp.float32, jnp.bfloat16, jnp.int32, jnp.float8_e4m3fn
DIGITS = 3
CHUNKS = 4
PLANES = 2
MESH = pl.DeviceIdType.MESH
ANY = pl.BlockSpec(memory_space=pl.ANY)
dispersion = 0.06
rate_step = 0.2 / 65535.0
CX, CY, CZ = 32, 64, 256


def greet():
    barrier = pltpu.get_barrier_semaphore()
    for axis, count in (("gx", 4), ("gy", 8), ("gz", 4)):
        me = lax.axis_index(axis)
        for o in range(1, count):
            pl.semaphore_signal(
                barrier, inc=1, device_id={axis: lax.rem(me + o, count)}, device_id_type=MESH
            )
    gx = lax.axis_index("gx")
    across = gx + 2 - 4 * (gx // 2)
    for axis, count in (("gy", 8), ("gz", 4)):
        me = lax.axis_index(axis)
        for o in range(1, count):
            pl.semaphore_signal(
                barrier, inc=1, device_id={"gx": across, axis: lax.rem(me + o, count)},
                device_id_type=MESH,
            )
    pl.semaphore_wait(barrier, 23)


def weight_of(s):
    return 1.0 - 0.7 * s.astype(f32)


def pair(w0, w1, v):
    k = (dispersion * w0) * w1
    return k - jnp.minimum(v, 0.0), k + jnp.maximum(v, 0.0)


def plane_iotas():
    return (
        lax.broadcasted_iota(i32, (CY, CZ), 0),
        lax.broadcasted_iota(i32, (CY, CZ), 1),
        lax.broadcasted_iota(i32, (CY, 128), 1),
    )


def shifts(ri, li):
    return (
        lambda v: jnp.where(ri == CY - 1, 0.0, pltpu.roll(v, CY - 1, 0)),
        lambda v: jnp.where(ri == 0, 0.0, pltpu.roll(v, 1, 0)),
        lambda v: jnp.where(li == CZ - 1, 0.0, pltpu.roll(v, CZ - 1, 1)),
        lambda v: jnp.where(li == 0, 0.0, pltpu.roll(v, 1, 1)),
    )


def sender(started, ssem, rsem):
    def send(src, dst, where, slot=None):
        k = len(started) if slot is None else slot
        copy = pltpu.make_async_remote_copy(
            src_ref=src, dst_ref=dst, send_sem=ssem.at[k], recv_sem=rsem.at[k],
            device_id=where, device_id_type=MESH,
        )
        if slot is None:
            copy.start()
            started.append(copy)
        return copy

    return send


def each(copies, what):
    for copy in copies:
        getattr(copy, what)()


def gather_faces(
    conc, adj, vx, vy, vz, solid, rates,
    xlo, xlo_s, xhi, xhi_s, ylo, yhi, zlo, zhi, yown, zown, yend, zend, rall, s1_out, s2_out,
    cb, lb, vxb, vyb, vzb, sb, s1, s2, hx, qx, yfwd, ybwd, zfwd, zbwd, lsem, rsem, osem, ssem,
):
    gx, gy, gz = (lax.axis_index(a) for a in ("gx", "gy", "gz"))
    xh, core = gx // 2, lax.rem(gx, 2)
    local = []
    for q in range(4):
        at = pl.ds(8 * q, 8)
        local.append([
            pltpu.make_async_copy(ref.at[at], buf.at[at], lsem.at[6 * q + k])
            for k, (ref, buf) in enumerate(
                ((conc, cb), (adj, lb), (solid, sb), (vx, vxb), (vy, vyb), (vz, vzb))
            )
        ])
        for copy in local[q]:
            copy.start()
    mine = pltpu.make_async_copy(rates, rall.at[xh, core, gy, gz], osem.at[0])
    mine.start()
    greet()

    started = []
    send = sender(started, ssem, rsem)
    one, row_y, row_z = rall.at[xh, core, gy, gz], rall.at[:, core, gy], rall.at[:, core, :, gz]
    near = [(dx, o) for dx in range(2) for o in range(8) if dx + o > 0]
    side = lambda dx: gx + dx * (2 - 4 * xh)
    second = (
        [
            send(rates, one, {"gx": side(dx), "gz": lax.rem(gz + o, 4)}, 12 + n)
            for n, (dx, o) in enumerate([p for p in near if p[1] < 4])
        ],
        [
            send(rates, one, {"gx": side(dx), "gy": lax.rem(gy + o, 8)}, 19 + n)
            for n, (dx, o) in enumerate(near)
        ],
    )
    third = (
        [send(row_y, row_y, {"gy": lax.rem(gy + o, 8)}, 33 + o) for o in range(1, 8)],
        [send(row_z, row_z, {"gz": lax.rem(gz + o, 4)}, 40 + o) for o in range(1, 4)],
    )
    for way in range(2):
        @pl.when(core == way)
        def _():
            each(second[way], "start")

    right, left = {"gx": lax.rem(gx + 1, 4)}, {"gx": lax.rem(gx + 3, 4)}
    faces = []
    for k, ref in enumerate((conc, adj, vx)):
        faces.append(send(ref.at[CX - 1], xlo.at[k], right))
    faces.append(send(solid.at[CX - 1], xlo_s, right))
    for k, ref in enumerate((conc, adj)):
        faces.append(send(ref.at[0], xhi.at[k], left))
    faces.append(send(solid.at[0], xhi_s, left))

    hx[...] = jnp.zeros_like(hx)
    qx[...] = jnp.zeros_like(qx)
    zfwd[...] = jnp.zeros_like(zfwd)
    zbwd[...] = jnp.zeros_like(zbwd)

    def plane(x, carry):
        ri, li, lane = plane_iotas()
        up_y, down_y, up_z, down_z = shifts(ri, li)
        at = pl.ds(x, 1)
        nx = jnp.minimum(x + 1, CX - 1)
        inside = jnp.where(x < CX - 1, 1.0, 0.0).astype(f32)
        c, l, w = cb[x], lb[x], weight_of(sb[x])
        v_x, v_y, v_z = vxb[x], vyb[x], vzb[x]
        a, b = pair(w, weight_of(sb[nx]) * inside, v_x)
        flux = a * (cb[nx] * inside) - b * c
        div = c + flux - hx[...]
        hx[...] = flux
        d = lb[nx] * inside - l
        lap = l + b * d - qx[...]
        qx[...] = a * d
        a, b = pair(w, up_y(w), v_y)
        flux = a * up_y(c) - b * c
        div = div + flux - down_y(flux)
        d = up_y(l) - l
        lap = lap + b * d - down_y(a * d)
        a, b = pair(w, up_z(w), v_z)
        flux = a * up_z(c) - b * c
        s1[x] = div + flux - down_z(flux)
        d = up_z(l) - l
        s2[x] = lap + b * d - down_z(a * d)
        for k, v in enumerate((c, l, v_y, w)):
            yfwd[k, at, :] = v[CY - 1:CY, :]
        for k, v in enumerate((c, l, w)):
            ybwd[k, at, :] = v[0:1, :]
        pack = zfwd[...]
        for k, v in enumerate((c, l, v_z, w)):
            pack = jnp.where(lane == x + 32 * k, v[:, CZ - 1:CZ], pack)
        zfwd[...] = pack
        pack = zbwd[...]
        for k, v in enumerate((c, l, w)):
            pack = jnp.where(lane == x + 32 * k, v[:, 0:1], pack)
        zbwd[...] = pack
        return carry

    def arrived(q):
        for copy in local[q]:
            copy.wait()

    mine.wait()
    arrived(0)
    arrived(1)
    lax.fori_loop(0, 5, plane, 0)
    for way in range(2):
        @pl.when(core == way)
        def _():
            each(second[way], "wait_recv")
            each(third[way], "start")

    arrived(2)
    arrived(3)
    lax.fori_loop(5, 24, plane, 0)
    for way in range(2):
        @pl.when(core == way)
        def _():
            each(third[way], "wait_recv")
            each(second[way], "wait_send")
            each(third[way], "wait_send")

    last = send(rall.at[:, core], rall.at[:, core], {"gx": gx + 1 - 2 * core})
    outs = [
        pltpu.make_async_copy(s1.at[0:24], s1_out.at[0:24], osem.at[1]),
        pltpu.make_async_copy(s2.at[0:24], s2_out.at[0:24], osem.at[2]),
    ]
    for copy in outs:
        copy.start()
    lax.fori_loop(24, CX, plane, 0)
    faces.append(send(yfwd, ylo, {"gy": lax.rem(gy + 1, 8)}))
    faces.append(send(ybwd, yhi, {"gy": lax.rem(gy + 7, 8)}))
    faces.append(send(zfwd, zlo, {"gz": lax.rem(gz + 1, 4)}))
    faces.append(send(zbwd, zhi, {"gz": lax.rem(gz + 3, 4)}))
    keep = [
        pltpu.make_async_copy(s1.at[24:32], s1_out.at[24:32], osem.at[3]),
        pltpu.make_async_copy(s2.at[24:32], s2_out.at[24:32], osem.at[4]),
        pltpu.make_async_copy(yfwd, yend, osem.at[5]),
        pltpu.make_async_copy(ybwd, yown, osem.at[6]),
        pltpu.make_async_copy(zfwd, zend, osem.at[7]),
        pltpu.make_async_copy(zbwd, zown, osem.at[8]),
    ]
    for copy in keep:
        copy.start()
    last.wait_recv()
    for copy in faces:
        copy.wait_recv()
    for copy in started:
        copy.wait_send()
    for copy in outs + keep:
        copy.wait()


def call_faces(conc, adj, vx, vy, vz, solid, rates):
    face = lambda *s: jax.ShapeDtypeStruct(s, f32)
    outs = (
        face(3, CY, CZ), jax.ShapeDtypeStruct((CY, CZ), i32),
        face(2, CY, CZ), jax.ShapeDtypeStruct((CY, CZ), i32),
        face(4, CX, CZ), face(3, CX, CZ),
        face(CY, 128), face(CY, 128), face(3, CX, CZ), face(CY, 128),
        face(4, CX, CZ), face(CY, 128),
        face(2, 2, 8, 4, 16, 128), face(CX, CY, CZ), face(CX, CY, CZ),
    )
    whole = pltpu.VMEM((CX, CY, CZ), f32)
    return pl.pallas_call(
        gather_faces,
        out_shape=outs,
        in_specs=[ANY] * 7,
        out_specs=[ANY] * len(outs),
        scratch_shapes=[
            whole, whole, whole, whole, whole, pltpu.VMEM((CX, CY, CZ), i32), whole, whole,
            pltpu.VMEM((CY, CZ), f32), pltpu.VMEM((CY, CZ), f32),
            pltpu.VMEM((4, CX, CZ), f32), pltpu.VMEM((3, CX, CZ), f32),
            pltpu.VMEM((CY, 128), f32), pltpu.VMEM((CY, 128), f32),
            pltpu.SemaphoreType.DMA((24,)), pltpu.SemaphoreType.DMA((44,)),
            pltpu.SemaphoreType.DMA((9,)), pltpu.SemaphoreType.DMA((44,)),
        ],
        compiler_params=pltpu.CompilerParams(
            collective_id=0, has_side_effects=True, vmem_limit_bytes=62 << 20
        ),
    )(conc, adj, vx, vy, vz, solid, rates)


def roll_tile(tile, shift):
    return pltpu.roll(tile, shift, 1)


def main_kernel(
    block_ref,
    s1_ref, s2_ref, conc_ref, adj_ref, solid_ref, load_ref, adjload_ref, slot_ref, vend_ref,
    xlo, xlo_s, xhi, xhi_s, ylo, yhi, zlo, zhi, yown, zown, yend, zend, rall, home0, home1, slot_grain,
    adj1_ref, base_ref, mstart_ref, dense_ref, ly_ref, lz_ref, cx_ref, cy_ref, cz_ref,
    packed, places_ref, table, xc, yc, zc,
    hi_f, lo_f, term_f, hot_lo, hot_hi, total, got_ref, look_ref,
):
    step = pl.program_id(0)
    gx, gy, gz = (lax.axis_index(a) for a in ("gx", "gy", "gz"))
    has = lambda cond: jnp.where(cond, 1.0, 0.0).astype(f32)
    lo_x, hi_x = has(gx > 0), has(gx < 3)
    lo_y, hi_y = has(gy > 0), has(gy < 7)
    lo_z, hi_z = has(gz > 0), has(gz < 3)
    lane1 = lax.broadcasted_iota(i32, (CY, 128), 1)
    @pl.when(step == 0)
    def _():
        total[...] = jnp.zeros_like(total)
        hot_lo[...] = jnp.zeros_like(hot_lo)
        term_f[...] = jnp.zeros_like(term_f)
        hi_f[...] = jnp.zeros_like(hi_f)
        lo_f[...] = jnp.zeros_like(lo_f)
        hot_hi[...] = jnp.zeros_like(hot_hi)
        def pack(r, carry):
            at = pl.ds(pl.multiple_of(r * 128, 128), 128)
            packed[at, :] = (rall[at, :] * (1.0 / rate_step) + 0.5).astype(i32)
            return carry

        lax.fori_loop(0, 16, pack, 0)
        base = (slot_grain[...] - block_ref[0] * 2048) & 262143
        lanes = [base[8 * j:8 * j + 8] & 127 for j in range(4)]
        rows = [base[8 * j:8 * j + 8] >> 7 for j in range(4)]
        found = [jnp.zeros((8, 128), i32)] * 4
        for r in range(32):
            src = home0 if r < 16 else home1
            row = jnp.broadcast_to(src[0, r % 16:r % 16 + 1, :], (8, 128))
            for j in range(4):
                found[j] = jnp.where(
                    rows[j] == r, jnp.take_along_axis(row, lanes[j], axis=1), found[j]
                )
        for j in range(4):
            places_ref[8 * j:8 * j + 8, :] = found[j]
        lanes = [f & 127 for f in found]
        rows = [(f >> 7) & 1023 for f in found]


        sub_ids = lax.broadcasted_iota(i32, (256, 128), 0).astype(f32).astype(bf16)
        ones, zeros = jnp.ones((256, 128), bf16), jnp.zeros((256, 128), bf16)

        def look(n, acc):
            at = pl.ds(pl.multiple_of(n * 256, 256), 256)
            q = packed[at, :]
            digits = jnp.concatenate([(q & 255).astype(f32).astype(bf16), ((q >> 8) & 255).astype(f32).astype(bf16)], axis=1)
            first = (n * 256).astype(f32)
            hot = jnp.concatenate(
                [
                    jnp.where(
                        sub_ids == jnp.broadcast_to((found[s // 8] >> 7).astype(f32)[s % 8:s % 8 + 1, :] - first, (256, 128)).astype(bf16),
                        ones, zeros,
                    )
                    for s in range(32)
                ],
                axis=1,
            )
            got_ref[...] = got_ref[...] + lax.dot_general(digits, hot, (((0,), (0,)), ((), ())), preferred_element_type=f32)
            return acc
        got_ref[...] = jnp.zeros_like(got_ref)
        lax.fori_loop(0, 8, look, 0)
        lids = lax.broadcasted_iota(i32, (128, 128), 0)
        for s in range(32):
            m = lids == (found[s // 8] & 127)[s % 8:s % 8 + 1, :]
            sp = slice(128 * s, 128 * s + 128)
            v = got_ref[0:128, sp] + 256.0 * got_ref[128:256, sp]
            look_ref[s:s + 1, :] = jnp.sum(jnp.where(m, v, 0.0), axis=0, keepdims=True)
        got = [look_ref[8 * j:8 * j + 8, :].astype(i32) for j in range(4)]
        table[0:8, :] = got[0] + (got[2] << 16)
        table[8:16, :] = got[1] + (got[3] << 16)

        a, b = pair(weight_of(xlo_s[...]) * lo_x, weight_of(solid_ref[0]), xlo[2] * lo_x)
        xc[0] = b * (xlo[0] * lo_x) - a * conc_ref[0]
        xc[1] = a * (xlo[1] * lo_x - adj_ref[0])
        xc[2] = xc[0]
        xc[3] = xc[1]
        cx_ref[0] = a
        a, b = pair(ylo[3] * lo_y, yown[2], ylo[2] * lo_y)
        yc[0] = b * (ylo[0] * lo_y) - a * yown[0]
        yc[1] = a * (ylo[1] * lo_y - yown[1])
        cy_ref[0] = a
        k = (dispersion * yend[3]) * (yhi[2] * hi_y)
        a, b = k - jnp.minimum(yend[2], 0.0), k + jnp.maximum(yend[2], 0.0)
        yc[2] = a * (yhi[0] * hi_y) - k * yend[0]
        yc[3] = b * (yhi[1] * hi_y) - k * yend[1]
        cy_ref[1] = b
        cy_ref[2] = k
        low, own = zlo[...] * lo_z, zown[...]
        a, b = pair(roll_tile(low, 32), roll_tile(own, 64), roll_tile(low, 64))
        low_c = b * low - a * own
        low_l = a * (roll_tile(low, 96) - roll_tile(own, 96))
        coef = jnp.where(lane1 < 32, a, 0.0)
        high, own = zhi[...] * hi_z, zend[...]
        k = (dispersion * roll_tile(own, 32)) * roll_tile(high, 64)
        v = roll_tile(own, 64)
        a, b = k - jnp.minimum(v, 0.0), k + jnp.maximum(v, 0.0)
        high_c = a * high - k * own
        high_l = b * roll_tile(high, 96) - k * roll_tile(own, 96)

        def lay(parts):
            out = parts[0]
            for n in range(1, 4):
                out = jnp.where(lane1 >= 32 * n, roll_tile(parts[n], 32 * n), out)
            return out

        zc[...] = lay([low_c, low_l, high_c, high_l])
        cz_ref[...] = lay([coef, b, k, jnp.zeros_like(k)])
        lz_ref[...] = jnp.zeros_like(lz_ref)

    @pl.when(step == CX // PLANES - 1)
    def _():
        k = (dispersion * weight_of(solid_ref[PLANES - 1])) * (weight_of(xhi_s[...]) * hi_x)
        v = vend_ref[0]
        a, b = k - jnp.minimum(v, 0.0), k + jnp.maximum(v, 0.0)
        xc[2] = a * (xhi[0] * hi_x) - k * conc_ref[PLANES - 1]
        xc[3] = b * (xhi[1] * hi_x) - k * adj_ref[PLANES - 1]
        cx_ref[1] = b
        cx_ref[2] = k

    ids = lax.broadcasted_iota(i32, (128, CZ), 0).astype(f32).astype(bf16)
    zero, one = jnp.zeros((32, CZ), bf16), jnp.ones((32, CZ), bf16)
    rows_of = CY // CHUNKS
    width = rows_of * CZ

    def product(g):
        span = slice(g * width, (g + 1) * width)
        return lax.dot_general(
            hot_lo[:, span], hot_hi[:, span], (((1,), (1,)), ((), ())), preferred_element_type=f32
        )

    def make_hot(g):
        def row(plane):
            half = jnp.broadcast_to(plane, (16, CZ)).astype(bf16)
            return jnp.concatenate([half, half], axis=0)

        for y in range(g * rows_of, (g + 1) * rows_of):
            span = slice(y * CZ, y * CZ + CZ)
            mask = ids[0:32] == row(hi_f[y:y + 1, :])
            for k in range(DIGITS):
                hot_hi[32 * k:32 * k + 32, span] = jnp.where(mask, row(term_f[k, y:y + 1, :]), zero).astype(f8)
            low = row(lo_f[y:y + 1, :])
            for j in range(4):
                at_j = slice(32 * j, 32 * j + 32)
                hot_lo[at_j, span] = jnp.where(ids[at_j] == low, one, zero).astype(f8)

    def rate_of(p, g):
        halves = []
        for h in range(2):
            s = slot_ref[p, 8 * g:8 * g + 8, 128 * h:128 * h + 128]
            lo, hi = s & 127, s >> 7
            level = [
                jnp.take_along_axis(jnp.broadcast_to(table[r:r + 1, :], (8, 128)), lo, axis=1)
                for r in range(16)
            ]
            for bit in range(4):
                mask = (hi & (1 << bit)) != 0
                level = [
                    jnp.where(mask, level[2 * j + 1], level[2 * j]) for j in range(len(level) // 2)
                ]
            both = level[0]
            value = jnp.where((hi & 16) != 0, lax.shift_right_logical(both, 16), both & 65535)
            halves.append(value.astype(f32) * rate_step)
        return jnp.concatenate(halves, axis=1)

    def one_plane(p):
        i = step * PLANES + p
        acc = total[...]
        lookups = []
        per = CY // 8 // CHUNKS
        for g in range(CHUNKS):
            acc = acc + product(g)
            for n in range(per):
                lookups.append(rate_of(p, g * per + n))
            make_hot(g)
        total[...] = acc
        at = pl.ds(i, 1)
        end = i == CX - 1
        ri = lax.broadcasted_iota(i32, (8, CZ), 0)
        edge = jnp.where((i == 0) | end, 1.0, 0.0).astype(f32)
        edge_at = 0 if p == 0 else 2

        def with_faces(v, n):
            v = v + edge * xc[edge_at + n]
            low = roll_tile(zc[...], lax.rem(256 - i - 32 * n, 128))
            high = roll_tile(zc[...], lax.rem(319 - i - 32 * n, 128))
            v = v + jnp.concatenate(
                [jnp.where(lane1 == 0, low, 0.0), jnp.where(lane1 == 127, high, 0.0)], axis=1
            )
            first = v[0:8, :] + jnp.where(ri == 0, yc[n, at, :], 0.0)
            final = v[CY - 8:CY, :] + jnp.where(ri == 7, yc[2 + n, at, :], 0.0)
            return jnp.concatenate([first, v[8:CY - 8, :], final], axis=0)

        c, l = conc_ref[p], adj_ref[p]
        sol = solid_ref[p].astype(f32)

        kv = sol * jnp.concatenate(lookups, axis=0)

        def inverse(v):
            r = pl.reciprocal(v, approx=True)
            return r * (2.0 - v * r)

        m = adjload_ref[p]
        u0 = inverse(1.0 + c)
        e0 = c * u0 - load_ref[p]
        r = kv * e0
        conc1 = with_faces(s1_ref[p], 0) - r
        load1 = load_ref[p] + r
        d1 = m - l
        u1 = inverse(1.0 + conc1)
        kd = kv * d1
        adj1 = with_faces(s2_ref[p], 1) + kd * (u1 * u1)
        m1 = m - kd
        d0 = m1 - adj1
        kd = kv * d0
        mstart_ref[p] = m1 - kd
        rest = sol * ((conc1 * u1 - load1) * d1 + e0 * d0)
        for k in range(DIGITS):
            digit = rest.astype(f8).astype(f32)
            term_f[k] = digit
            rest = (rest - digit) * 16.0
        base_ref[p] = adj1 + kd * (u0 * u0)
        adj1_ref[p] = adj1
        ly_ref[0, at, :] = adj1[0:1, :]
        ly_ref[1, at, :] = adj1[CY - 1:CY, :]
        packed_l = jnp.where(lane1 == i, adj1[:, 0:1], lz_ref[...])
        lz_ref[...] = jnp.where(lane1 == i + 32, adj1[:, CZ - 1:CZ], packed_l)

        slots = slot_ref[p]
        hi_f[...] = (slots >> 7).astype(f32)
        lo_f[...] = (slots & 127).astype(f32)

    for p in range(PLANES):
        one_plane(p)

    @pl.when(step == CX // PLANES - 1)
    def _():
        for g in range(CHUNKS):
            total[...] = total[...] + product(g)
            make_hot(g)
        for g in range(CHUNKS):
            total[...] = total[...] + product(g)
        by_lane = total[...].T
        sums = by_lane[32 * DIGITS - 32:32 * DIGITS]
        for k in range(DIGITS - 2, -1, -1):
            sums = by_lane[32 * k:32 * k + 32] + sums * (1.0 / 16.0)
        places = places_ref[...]
        high = sums.astype(bf16)
        high_f = high.astype(f32)
        low_f = sums - high_f
        place_lane = (places & 127).astype(f32)
        place_row = places >> 7
        lane_ids = lax.broadcasted_iota(i32, (128, 128), 0).astype(f32)

        row_ids = lax.broadcasted_iota(i32, (256, 128), 0).astype(f32).astype(bf16)
        row_f = place_row.astype(f32)
        ones, zeros = jnp.ones((256, 128), bf16), jnp.zeros((256, 128), bf16)

        values = []
        for s in range(32):
            match = lane_ids == place_lane[s:s + 1, :]
            values.append(
                jnp.concatenate(
                    [
                        jnp.where(match, high_f[s:s + 1, :], 0.0).astype(bf16),
                        jnp.where(match, low_f[s:s + 1, :], 0.0).astype(bf16),
                    ],
                    axis=0,
                )
            )
        value = jnp.concatenate(values, axis=1)

        def spread(n, carry):
            first = (n * 256).astype(f32)
            hot = jnp.concatenate(
                [
                    jnp.where(
                        row_ids == jnp.broadcast_to(row_f[s:s + 1, :] - first, (256, 128)).astype(bf16),
                        ones, zeros,
                    )
                    for s in range(32)
                ],
                axis=1,
            )
            got = lax.dot_general(
                hot, value, (((1,), (1,)), ((), ())), preferred_element_type=f32
            )
            dense_ref[pl.ds(pl.multiple_of(n * 256, 256), 256), :] = got[:, 0:128] + got[:, 128:256]
            return carry

        lax.fori_loop(0, 8, spread, 0)


def call_main(block, arrays, faces, home, slot_grain):
    conc, load, adj, adj_load, vx, solid, slot = arrays
    plane = pl.BlockSpec((PLANES, CY, CZ), lambda i, b: (i, 0, 0))

    def whole(shape):
        return pl.BlockSpec(shape, lambda i, b: (0,) * len(shape))

    face_shapes = [
        (3, CY, CZ), (CY, CZ), (2, CY, CZ), (CY, CZ), (4, CX, CZ), (3, CX, CZ),
        (CY, 128), (CY, 128), (3, CX, CZ), (CY, 128), (4, CX, CZ), (CY, 128), (2048, 128),
    ]
    block_shape = (CX, CY, CZ)
    out_shapes = [
        block_shape, block_shape, block_shape, (2048, 128), (2, CX, CZ), (CY, 128),
        (3, CY, CZ), (3, CX, CZ), (CY, 128),
    ]
    plane_scratch = pltpu.VMEM((CY, CZ), f32)
    return pl.pallas_call(
        main_kernel,
        out_shape=[jax.ShapeDtypeStruct(s, f32) for s in out_shapes],
        grid_spec=pltpu.PrefetchScalarGridSpec(
            num_scalar_prefetch=1,
            grid=(CX // PLANES,),
            in_specs=[plane] * 8
            + [pl.BlockSpec((1, CY, CZ), lambda i, b: (CX - 1, 0, 0))]
            + [whole(s) for s in face_shapes]
            + [
                pl.BlockSpec((1, 16, 128), lambda i, b: (b[0], 0, 0)),
                pl.BlockSpec((1, 16, 128), lambda i, b: (lax.rem(b[0] + 1, 128), 0, 0)),
                whole((32, 128)),
            ],
            out_specs=[plane] * 3 + [whole(s) for s in out_shapes[3:]],
            scratch_shapes=[
                pltpu.VMEM((2048, 128), i32), pltpu.VMEM((32, 128), i32), pltpu.VMEM((16, 128), i32),
                pltpu.VMEM((4, CY, CZ), f32), pltpu.VMEM((4, CX, CZ), f32), pltpu.VMEM((CY, 128), f32),
                plane_scratch, plane_scratch, pltpu.VMEM((DIGITS, CY, CZ), f32),
                pltpu.VMEM((128, CY * CZ), f8), pltpu.VMEM((32 * DIGITS, CY * CZ), f8),
                pltpu.VMEM((128, 32 * DIGITS), f32), pltpu.VMEM((256, 4096), f32), pltpu.VMEM((32, 128), f32),
            ],
        ),
        compiler_params=pltpu.CompilerParams(
            dimension_semantics=("arbitrary",), vmem_limit_bytes=58 << 20
        ),
        cost_estimate=pl.CostEstimate(flops=10 ** 9, bytes_accessed=25 << 20, transcendentals=0),
    )(
        block, faces[13], faces[14], conc, adj, solid, load, adj_load, slot, vx,
        *faces[:12], faces[12].reshape(2048, 128), home, home, slot_grain,
    )


def finish_kernel(
    adj1, base, solid, vx, vy, vz, dense, ly, lz, cx, cy, cz,
    out, grad,
    lb, fb, sb, vxb, vyb, vzb, qx, yc, zc,
    xlo, xhi, ylo, yhi, zlo, zhi, d1, r1, r2y, r2z, s2y, s2z, r3z, r3y,
    lsem, ssem, rsem,
):
    gx, gy, gz = (lax.axis_index(a) for a in ("gx", "gy", "gz"))
    xh, core = gx // 2, lax.rem(gx, 2)
    has = lambda cond: jnp.where(cond, 1.0, 0.0).astype(f32)
    hi_x, hi_y, hi_z = has(gx < 3), has(gy < 7), has(gz < 3)
    keep = pltpu.make_async_copy(dense.at[:, core], d1, lsem.at[0])
    keep.start()
    loads = [
        pltpu.make_async_copy(ref, buf, lsem.at[1 + k])
        for k, (ref, buf) in enumerate(
            ((adj1, lb), (base, fb), (solid, sb), (vx, vxb), (vy, vyb), (vz, vzb))
        )
    ]
    for copy in loads:
        copy.start()
    greet()
    started = []
    send = sender(started, ssem, rsem)
    first = send(dense.at[:, 1 - core], r1, {"gx": gx + 1 - 2 * core})
    faces = [
        send(adj1.at[CX - 1], xlo, {"gx": lax.rem(gx + 1, 4)}),
        send(adj1.at[0], xhi, {"gx": lax.rem(gx + 3, 4)}),
        send(ly.at[1], ylo, {"gy": lax.rem(gy + 1, 8)}),
        send(ly.at[0], yhi, {"gy": lax.rem(gy + 7, 8)}),
        send(lz, zlo, {"gz": lax.rem(gz + 1, 4)}),
        send(lz, zhi, {"gz": lax.rem(gz + 3, 4)}),
    ]
    keep.wait()
    first.wait_recv()

    def add_first(h, carry):
        for x in range(2):
            d1[x, h] = d1[x, h] + r1[x, h]
        return carry

    lax.fori_loop(0, 8, add_first, 0)
    ys = [lax.rem(gy + o, 8) for o in range(8)]
    zs = [lax.rem(gz + o, 4) for o in range(4)]
    near = [(dx, o) for dx in range(2) for o in range(8) if dx + o > 0]
    side = lambda dx: gx + dx * (2 - 4 * xh)
    half = lambda dx: xh + dx * (1 - 2 * xh)
    second = (
        [send(d1.at[:, ys[o]], r2y.at[o - 1], {"gy": ys[o]}, 6 + o) for o in range(1, 8)],
        [send(d1.at[:, :, zs[o]], r2z.at[o - 1], {"gz": zs[o]}, 13 + o) for o in range(1, 4)],
    )
    third = (
        [
            send(s2y.at[half(dx), zs[o]], r3z.at[n], {"gx": side(dx), "gz": zs[o]}, 17 + n)
            for n, (dx, o) in enumerate([p for p in near if p[1] < 4])
        ],
        [
            send(s2z.at[half(dx), ys[o]], r3y.at[n], {"gx": side(dx), "gy": ys[o]}, 24 + n)
            for n, (dx, o) in enumerate(near)
        ],
    )
    for way in range(2):
        @pl.when(core == way)
        def _():
            each(second[way], "start")

    for copy in loads:
        copy.wait()
    for copy in faces:
        copy.wait_recv()
    fb[0] = fb[0] + cx[0] * (xlo[...] - lb[0])
    fb[CX - 1] = fb[CX - 1] + cx[1] * (xhi[...] * hi_x) - cx[2] * lb[CX - 1]
    yc[0] = cy[0] * (ylo[...] - ly[0])
    yc[1] = cy[1] * (yhi[...] * hi_y) - cy[2] * ly[1]
    lane1 = lax.broadcasted_iota(i32, (CY, 128), 1)
    own, coef = lz[...], cz[...]
    zc[...] = jnp.where(
        lane1 < 32,
        coef * (pltpu.roll(zlo[...], 96, 1) - own),
        coef * (pltpu.roll(zhi[...], 32, 1) * hi_z) - pltpu.roll(coef, 96, 1) * own,
    )
    qx[...] = jnp.zeros_like(qx)

    def plane(x, carry):
        ri, li, lane = plane_iotas()
        up_y, down_y, up_z, down_z = shifts(ri, li)
        at = pl.ds(x, 1)
        nx = jnp.minimum(x + 1, CX - 1)
        inside = jnp.where(x < CX - 1, 1.0, 0.0).astype(f32)
        l, w = lb[x], weight_of(sb[x])
        a, b = pair(w, weight_of(sb[nx]) * inside, vxb[x])
        d = lb[nx] * inside - l
        lap = fb[x] + b * d - qx[...]
        qx[...] = a * d
        a, b = pair(w, up_y(w), vyb[x])
        d = up_y(l) - l
        lap = lap + b * d - down_y(a * d)
        a, b = pair(w, up_z(w), vzb[x])
        d = up_z(l) - l
        lap = lap + b * d - down_z(a * d)
        cols = zc[...]
        low = pltpu.roll(cols, lax.rem(128 - x, 128), 1)
        high = pltpu.roll(cols, 95 - x, 1)
        lap = lap + jnp.concatenate(
            [jnp.where(lane == 0, low, 0.0), jnp.where(lane == 127, high, 0.0)], axis=1
        )
        fb[x] = lap
        fb[x, 0:1, :] = lap[0:1, :] + yc[0, at, :]
        fb[x, CY - 1:CY, :] = lap[CY - 1:CY, :] + yc[1, at, :]
        return carry

    lax.fori_loop(0, 16, plane, 0)
    store = [pltpu.make_async_copy(fb.at[0:16], out.at[0:16], lsem.at[7])]
    store[0].start()
    for way in range(2):
        @pl.when(core == way)
        def _():
            each(second[way], "wait_recv")

    @pl.when(core == 0)
    def _():
        for x in range(2):
            acc = d1[x, gy]
            for o in range(7):
                acc = acc + r2y[o, x]
            s2y[x] = acc
        each(third[0], "start")

    @pl.when(core == 1)
    def _():
        for x in range(2):
            for h in range(8):
                acc = d1[x, h, gz]
                for o in range(3):
                    acc = acc + r2z[o, x, h]
                s2z[x, h] = acc
        each(third[1], "start")

    lax.fori_loop(16, CX, plane, 0)
    store.append(pltpu.make_async_copy(fb.at[16:32], out.at[16:32], lsem.at[8]))
    store[1].start()

    @pl.when(core == 0)
    def _():
        each(third[0], "wait_recv")
        acc = s2y[xh, gz]
        for n in range(7):
            acc = acc + r3z[n]
        grad[...] = acc

    @pl.when(core == 1)
    def _():
        each(third[1], "wait_recv")
        acc = s2z[xh, gy]
        for n in range(15):
            acc = acc + r3y[n]
        grad[...] = acc

    for way in range(2):
        @pl.when(core == way)
        def _():
            each(second[way], "wait_send")
            each(third[way], "wait_send")

    for copy in started:
        copy.wait_send()
    for copy in store:
        copy.wait()


def call_finish(adj1, base, solid, vx, vy, vz, dense, ly, lz, cx, cy, cz):
    vmem = pl.BlockSpec(memory_space=pltpu.VMEM)
    whole = pltpu.VMEM((CX, CY, CZ), f32)
    return pl.pallas_call(
        finish_kernel,
        out_shape=(
            jax.ShapeDtypeStruct((CX, CY, CZ), f32), jax.ShapeDtypeStruct((16, 128), f32)
        ),
        in_specs=[ANY] * 7 + [vmem] * 5,
        out_specs=(ANY, vmem),
        scratch_shapes=[
            whole, whole, pltpu.VMEM((CX, CY, CZ), i32), whole, whole, whole,
            pltpu.VMEM((CY, CZ), f32), pltpu.VMEM((2, CX, CZ), f32), pltpu.VMEM((CY, 128), f32),
            pltpu.VMEM((CY, CZ), f32), pltpu.VMEM((CY, CZ), f32),
            pltpu.VMEM((CX, CZ), f32), pltpu.VMEM((CX, CZ), f32),
            pltpu.VMEM((CY, 128), f32), pltpu.VMEM((CY, 128), f32),
            pltpu.VMEM((2, 8, 4, 16, 128), f32), pltpu.VMEM((2, 8, 4, 16, 128), f32),
            pltpu.VMEM((7, 2, 4, 16, 128), f32), pltpu.VMEM((3, 2, 8, 16, 128), f32),
            pltpu.VMEM((2, 4, 16, 128), f32), pltpu.VMEM((2, 8, 16, 128), f32),
            pltpu.VMEM((7, 16, 128), f32), pltpu.VMEM((15, 16, 128), f32),
            pltpu.SemaphoreType.DMA((9,)), pltpu.SemaphoreType.DMA((39,)),
            pltpu.SemaphoreType.DMA((39,)),
        ],
        compiler_params=pltpu.CompilerParams(
            collective_id=1, has_side_effects=True, vmem_limit_bytes=62 << 20
        ),
    )(adj1, base, solid, vx, vy, vz, dense, ly, lz, cx, cy, cz)


def hand_on_kernel(start_ref, grad_ref, start_out, grad_out):
    start_out[...] = start_ref[...]
    grad_out[...] = grad_ref[...]


def hand_on(start, grad):
    some = pl.BlockSpec((8, CY, CZ), lambda i: (i, 0, 0))
    small = pl.BlockSpec((16, 128), lambda i: (0, 0))
    return pl.pallas_call(
        hand_on_kernel,
        out_shape=(jax.ShapeDtypeStruct(start.shape, f32), jax.ShapeDtypeStruct(grad.shape, f32)),
        grid=(CX // 8,),
        in_specs=[some, small],
        out_specs=(some, small),
        compiler_params=pltpu.CompilerParams(vmem_limit_bytes=62 << 20),
    )(start, grad)


def per_device(
    conc, load, adj_conc, adj_load, vel_x, vel_y, vel_z, solid, voxel_slot, slot_grain, grain_home, rates
):
    block = (lax.axis_index("gx") * 32 + lax.axis_index("gy") * 4 + lax.axis_index("gz")).astype(i32)
    faces = call_faces(conc, adj_conc, vel_x, vel_y, vel_z, solid, rates.reshape(16, 128))
    arrays = (conc, load, adj_conc, adj_load, vel_x, solid, voxel_slot)
    adj1, base, load_start, dense, ly, lz, cx, cy, cz = call_main(
        block.reshape(1), arrays, faces, grain_home.reshape(128, 16, 128), slot_grain.reshape(32, 128)
    )
    start, grad = call_finish(
        adj1, base, solid, vel_x, vel_y, vel_z, dense.reshape(2, 2, 8, 4, 16, 128), ly, lz, cx, cy, cz
    )
    start, grad = hand_on(start, grad)
    return start, load_start, grad.reshape(2048)


def solution(mesh):
    cells = P("gx", "gy", "gz")
    every = P(("gx", "gy", "gz"))
    return jax.shard_map(
        per_device,
        mesh=mesh,
        in_specs=(cells,) * 9 + (P(("gx", "gy", "gz"), None), P(), every),
        out_specs=(cells, cells, every),
        check_vma=False,
    )
```

```python
import functools

import jax
import jax.numpy as jnp
from jax import lax
from jax.experimental import pallas as pl
from jax.experimental.pallas import tpu as pltpu
from jax.sharding import PartitionSpec as P

f32, bf16, i32, f8 = jnp.float32, jnp.bfloat16, jnp.int32, jnp.float8_e4m3fn
DIGITS = 3
CHUNKS = 4
PLANES = 4
MESH = pl.DeviceIdType.MESH
ANY = pl.BlockSpec(memory_space=pl.ANY)
dispersion = 0.06
rate_step = 0.2 / 65535.0
CX, CY, CZ = 32, 64, 256


def greet():
    barrier = pltpu.get_barrier_semaphore()
    for axis, count in (("gx", 4), ("gy", 8), ("gz", 4)):
        me = lax.axis_index(axis)
        for o in range(1, count):
            pl.semaphore_signal(
                barrier, inc=1, device_id={axis: lax.rem(me + o, count)}, device_id_type=MESH
            )
    gx = lax.axis_index("gx")
    across = gx + 2 - 4 * (gx // 2)
    for axis, count in (("gy", 8), ("gz", 4)):
        me = lax.axis_index(axis)
        for o in range(1, count):
            pl.semaphore_signal(
                barrier, inc=1, device_id={"gx": across, axis: lax.rem(me + o, count)},
                device_id_type=MESH,
            )
    pl.semaphore_wait(barrier, 23)


def weight_of(s):
    return 1.0 - 0.7 * s.astype(f32)


def pair(w0, w1, v):
    k = (dispersion * w0) * w1
    return k - jnp.minimum(v, 0.0), k + jnp.maximum(v, 0.0)


def plane_iotas():
    return (
        lax.broadcasted_iota(i32, (CY, CZ), 0),
        lax.broadcasted_iota(i32, (CY, CZ), 1),
        lax.broadcasted_iota(i32, (CY, 128), 1),
    )


def shifts(ri, li):
    return (
        lambda v: jnp.where(ri == CY - 1, 0.0, pltpu.roll(v, CY - 1, 0)),
        lambda v: jnp.where(ri == 0, 0.0, pltpu.roll(v, 1, 0)),
        lambda v: jnp.where(li == CZ - 1, 0.0, pltpu.roll(v, CZ - 1, 1)),
        lambda v: jnp.where(li == 0, 0.0, pltpu.roll(v, 1, 1)),
    )


def sender(started, ssem, rsem):
    def send(src, dst, where, slot=None):
        k = len(started) if slot is None else slot
        copy = pltpu.make_async_remote_copy(
            src_ref=src, dst_ref=dst, send_sem=ssem.at[k], recv_sem=rsem.at[k],
            device_id=where, device_id_type=MESH,
        )
        if slot is None:
            copy.start()
            started.append(copy)
        return copy

    return send


def each(copies, what):
    for copy in copies:
        getattr(copy, what)()


def gather_faces(
    conc, adj, vx, vy, vz, solid, rates,
    xlo, xlo_s, xhi, xhi_s, ylo, yhi, zlo, zhi, yown, zown, yend, zend, rall, s1_out, s2_out,
    cb, lb, vxb, vyb, vzb, sb, s1, s2, hx, qx, yfwd, ybwd, zfwd, zbwd, lsem, rsem, osem, ssem,
):
    gx, gy, gz = (lax.axis_index(a) for a in ("gx", "gy", "gz"))
    xh, core = gx // 2, lax.rem(gx, 2)
    local = []
    for q in range(4):
        at = pl.ds(8 * q, 8)
        local.append([
            pltpu.make_async_copy(ref.at[at], buf.at[at], lsem.at[6 * q + k])
            for k, (ref, buf) in enumerate(
                ((conc, cb), (adj, lb), (solid, sb), (vx, vxb), (vy, vyb), (vz, vzb))
            )
        ])
        for copy in local[q]:
            copy.start()
    mine = pltpu.make_async_copy(rates, rall.at[xh, core, gy, gz], osem.at[0])
    mine.start()
    greet()

    started = []
    send = sender(started, ssem, rsem)
    one, row_y, row_z = rall.at[xh, core, gy, gz], rall.at[:, core, gy], rall.at[:, core, :, gz]
    near = [(dx, o) for dx in range(2) for o in range(8) if dx + o > 0]
    side = lambda dx: gx + dx * (2 - 4 * xh)
    second = (
        [
            send(rates, one, {"gx": side(dx), "gz": lax.rem(gz + o, 4)}, 12 + n)
            for n, (dx, o) in enumerate([p for p in near if p[1] < 4])
        ],
        [
            send(rates, one, {"gx": side(dx), "gy": lax.rem(gy + o, 8)}, 19 + n)
            for n, (dx, o) in enumerate(near)
        ],
    )
    third = (
        [send(row_y, row_y, {"gy": lax.rem(gy + o, 8)}, 33 + o) for o in range(1, 8)],
        [send(row_z, row_z, {"gz": lax.rem(gz + o, 4)}, 40 + o) for o in range(1, 4)],
    )
    for way in range(2):
        @pl.when(core == way)
        def _():
            each(second[way], "start")

    right, left = {"gx": lax.rem(gx + 1, 4)}, {"gx": lax.rem(gx + 3, 4)}
    faces = []
    for k, ref in enumerate((conc, adj, vx)):
        faces.append(send(ref.at[CX - 1], xlo.at[k], right))
    faces.append(send(solid.at[CX - 1], xlo_s, right))
    for k, ref in enumerate((conc, adj)):
        faces.append(send(ref.at[0], xhi.at[k], left))
    faces.append(send(solid.at[0], xhi_s, left))

    hx[...] = jnp.zeros_like(hx)
    qx[...] = jnp.zeros_like(qx)
    zfwd[...] = jnp.zeros_like(zfwd)
    zbwd[...] = jnp.zeros_like(zbwd)

    def plane(x, carry):
        ri, li, lane = plane_iotas()
        up_y, down_y, up_z, down_z = shifts(ri, li)
        at = pl.ds(x, 1)
        nx = jnp.minimum(x + 1, CX - 1)
        inside = jnp.where(x < CX - 1, 1.0, 0.0).astype(f32)
        c, l, w = cb[x], lb[x], weight_of(sb[x])
        v_x, v_y, v_z = vxb[x], vyb[x], vzb[x]
        a, b = pair(w, weight_of(sb[nx]) * inside, v_x)
        flux = a * (cb[nx] * inside) - b * c
        div = c + flux - hx[...]
        hx[...] = flux
        d = lb[nx] * inside - l
        lap = l + b * d - qx[...]
        qx[...] = a * d
        a, b = pair(w, up_y(w), v_y)
        flux = a * up_y(c) - b * c
        div = div + flux - down_y(flux)
        d = up_y(l) - l
        lap = lap + b * d - down_y(a * d)
        a, b = pair(w, up_z(w), v_z)
        flux = a * up_z(c) - b * c
        s1[x] = div + flux - down_z(flux)
        d = up_z(l) - l
        s2[x] = lap + b * d - down_z(a * d)
        for k, v in enumerate((c, l, v_y, w)):
            yfwd[k, at, :] = v[CY - 1:CY, :]
        for k, v in enumerate((c, l, w)):
            ybwd[k, at, :] = v[0:1, :]
        pack = zfwd[...]
        for k, v in enumerate((c, l, v_z, w)):
            pack = jnp.where(lane == x + 32 * k, v[:, CZ - 1:CZ], pack)
        zfwd[...] = pack
        pack = zbwd[...]
        for k, v in enumerate((c, l, w)):
            pack = jnp.where(lane == x + 32 * k, v[:, 0:1], pack)
        zbwd[...] = pack
        return carry

    def arrived(q):
        for copy in local[q]:
            copy.wait()

    mine.wait()
    arrived(0)
    arrived(1)
    lax.fori_loop(0, 5, plane, 0)
    for way in range(2):
        @pl.when(core == way)
        def _():
            each(second[way], "wait_recv")
            each(third[way], "start")

    arrived(2)
    arrived(3)
    lax.fori_loop(5, 24, plane, 0)
    for way in range(2):
        @pl.when(core == way)
        def _():
            each(third[way], "wait_recv")
            each(second[way], "wait_send")
            each(third[way], "wait_send")

    last = send(rall.at[:, core], rall.at[:, core], {"gx": gx + 1 - 2 * core})
    outs = [
        pltpu.make_async_copy(s1.at[0:24], s1_out.at[0:24], osem.at[1]),
        pltpu.make_async_copy(s2.at[0:24], s2_out.at[0:24], osem.at[2]),
    ]
    for copy in outs:
        copy.start()
    lax.fori_loop(24, CX, plane, 0)
    faces.append(send(yfwd, ylo, {"gy": lax.rem(gy + 1, 8)}))
    faces.append(send(ybwd, yhi, {"gy": lax.rem(gy + 7, 8)}))
    faces.append(send(zfwd, zlo, {"gz": lax.rem(gz + 1, 4)}))
    faces.append(send(zbwd, zhi, {"gz": lax.rem(gz + 3, 4)}))
    keep = [
        pltpu.make_async_copy(s1.at[24:32], s1_out.at[24:32], osem.at[3]),
        pltpu.make_async_copy(s2.at[24:32], s2_out.at[24:32], osem.at[4]),
        pltpu.make_async_copy(yfwd, yend, osem.at[5]),
        pltpu.make_async_copy(ybwd, yown, osem.at[6]),
        pltpu.make_async_copy(zfwd, zend, osem.at[7]),
        pltpu.make_async_copy(zbwd, zown, osem.at[8]),
    ]
    for copy in keep:
        copy.start()
    last.wait_recv()
    for copy in faces:
        copy.wait_recv()
    for copy in started:
        copy.wait_send()
    for copy in outs + keep:
        copy.wait()


def call_faces(conc, adj, vx, vy, vz, solid, rates):
    face = lambda *s: jax.ShapeDtypeStruct(s, f32)
    outs = (
        face(3, CY, CZ), jax.ShapeDtypeStruct((CY, CZ), i32),
        face(2, CY, CZ), jax.ShapeDtypeStruct((CY, CZ), i32),
        face(4, CX, CZ), face(3, CX, CZ),
        face(CY, 128), face(CY, 128), face(3, CX, CZ), face(CY, 128),
        face(4, CX, CZ), face(CY, 128),
        face(2, 2, 8, 4, 16, 128), face(CX, CY, CZ), face(CX, CY, CZ),
    )
    whole = pltpu.VMEM((CX, CY, CZ), f32)
    return pl.pallas_call(
        gather_faces,
        out_shape=outs,
        in_specs=[ANY] * 7,
        out_specs=[ANY] * len(outs),
        scratch_shapes=[
            whole, whole, whole, whole, whole, pltpu.VMEM((CX, CY, CZ), i32), whole, whole,
            pltpu.VMEM((CY, CZ), f32), pltpu.VMEM((CY, CZ), f32),
            pltpu.VMEM((4, CX, CZ), f32), pltpu.VMEM((3, CX, CZ), f32),
            pltpu.VMEM((CY, 128), f32), pltpu.VMEM((CY, 128), f32),
            pltpu.SemaphoreType.DMA((24,)), pltpu.SemaphoreType.DMA((44,)),
            pltpu.SemaphoreType.DMA((9,)), pltpu.SemaphoreType.DMA((44,)),
        ],
        compiler_params=pltpu.CompilerParams(
            collective_id=0, has_side_effects=True, vmem_limit_bytes=62 << 20
        ),
    )(conc, adj, vx, vy, vz, solid, rates)


def roll_tile(tile, shift):
    return pltpu.roll(tile, shift, 1)


def main_kernel(
    block_ref,
    s1_ref, s2_ref, conc_ref, adj_ref, solid_ref, load_ref, adjload_ref, slot_ref, vend_ref,
    xlo, xlo_s, xhi, xhi_s, ylo, yhi, zlo, zhi, yown, zown, yend, zend, rall, home0, home1, slot_grain,
    adj1_ref, base_ref, mstart_ref, dense_ref, ly_ref, lz_ref, cx_ref, cy_ref, cz_ref,
    packed, places_ref, table, xc, yc, zc,
    hi_f, lo_f, term_f, hot_lo, hot_hi, total, got_ref, look_ref,
):
    step = pl.program_id(0)
    gx, gy, gz = (lax.axis_index(a) for a in ("gx", "gy", "gz"))
    has = lambda cond: jnp.where(cond, 1.0, 0.0).astype(f32)
    lo_x, hi_x = has(gx > 0), has(gx < 3)
    lo_y, hi_y = has(gy > 0), has(gy < 7)
    lo_z, hi_z = has(gz > 0), has(gz < 3)
    lane1 = lax.broadcasted_iota(i32, (CY, 128), 1)
    @pl.when(step == 0)
    def _():
        total[...] = jnp.zeros_like(total)
        hot_lo[...] = jnp.zeros_like(hot_lo)
        term_f[...] = jnp.zeros_like(term_f)
        hi_f[...] = jnp.zeros_like(hi_f)
        lo_f[...] = jnp.zeros_like(lo_f)
        hot_hi[...] = jnp.zeros_like(hot_hi)
        def pack(r, carry):
            at = pl.ds(pl.multiple_of(r * 128, 128), 128)
            packed[at, :] = (rall[at, :] * (1.0 / rate_step) + 0.5).astype(i32)
            return carry

        lax.fori_loop(0, 16, pack, 0)
        base = (slot_grain[...] - block_ref[0] * 2048) & 262143
        lanes = [base[8 * j:8 * j + 8] & 127 for j in range(4)]
        rows = [base[8 * j:8 * j + 8] >> 7 for j in range(4)]
        found = [jnp.zeros((8, 128), i32)] * 4
        for r in range(32):
            src = home0 if r < 16 else home1
            row = jnp.broadcast_to(src[0, r % 16:r % 16 + 1, :], (8, 128))
            for j in range(4):
                found[j] = jnp.where(
                    rows[j] == r, jnp.take_along_axis(row, lanes[j], axis=1), found[j]
                )
        for j in range(4):
            places_ref[8 * j:8 * j + 8, :] = found[j]
        lanes = [f & 127 for f in found]
        rows = [(f >> 7) & 1023 for f in found]


        sub_ids = lax.broadcasted_iota(i32, (256, 128), 0).astype(f32).astype(bf16)
        ones, zeros = jnp.ones((256, 128), bf16), jnp.zeros((256, 128), bf16)

        def look(n, acc):
            at = pl.ds(pl.multiple_of(n * 256, 256), 256)
            q = packed[at, :]
            digits = jnp.concatenate([(q & 255).astype(f32).astype(bf16), ((q >> 8) & 255).astype(f32).astype(bf16)], axis=1)
            first = (n * 256).astype(f32)
            hot = jnp.concatenate(
                [
                    jnp.where(
                        sub_ids == jnp.broadcast_to((found[s // 8] >> 7).astype(f32)[s % 8:s % 8 + 1, :] - first, (256, 128)).astype(bf16),
                        ones, zeros,
                    )
                    for s in range(32)
                ],
                axis=1,
            )
            got_ref[...] = got_ref[...] + lax.dot_general(digits, hot, (((0,), (0,)), ((), ())), preferred_element_type=f32)
            return acc
        got_ref[...] = jnp.zeros_like(got_ref)
        lax.fori_loop(0, 8, look, 0)
        lids = lax.broadcasted_iota(i32, (128, 128), 0)
        for s in range(32):
            m = lids == (found[s // 8] & 127)[s % 8:s % 8 + 1, :]
            sp = slice(128 * s, 128 * s + 128)
            v = got_ref[0:128, sp] + 256.0 * got_ref[128:256, sp]
            look_ref[s:s + 1, :] = jnp.sum(jnp.where(m, v, 0.0), axis=0, keepdims=True)
        got = [look_ref[8 * j:8 * j + 8, :].astype(i32) for j in range(4)]
        table[0:8, :] = got[0] + (got[2] << 16)
        table[8:16, :] = got[1] + (got[3] << 16)

        a, b = pair(weight_of(xlo_s[...]) * lo_x, weight_of(solid_ref[0]), xlo[2] * lo_x)
        xc[0] = b * (xlo[0] * lo_x) - a * conc_ref[0]
        xc[1] = a * (xlo[1] * lo_x - adj_ref[0])
        xc[2] = xc[0]
        xc[3] = xc[1]
        cx_ref[0] = a
        a, b = pair(ylo[3] * lo_y, yown[2], ylo[2] * lo_y)
        yc[0] = b * (ylo[0] * lo_y) - a * yown[0]
        yc[1] = a * (ylo[1] * lo_y - yown[1])
        cy_ref[0] = a
        k = (dispersion * yend[3]) * (yhi[2] * hi_y)
        a, b = k - jnp.minimum(yend[2], 0.0), k + jnp.maximum(yend[2], 0.0)
        yc[2] = a * (yhi[0] * hi_y) - k * yend[0]
        yc[3] = b * (yhi[1] * hi_y) - k * yend[1]
        cy_ref[1] = b
        cy_ref[2] = k
        low, own = zlo[...] * lo_z, zown[...]
        a, b = pair(roll_tile(low, 32), roll_tile(own, 64), roll_tile(low, 64))
        low_c = b * low - a * own
        low_l = a * (roll_tile(low, 96) - roll_tile(own, 96))
        coef = jnp.where(lane1 < 32, a, 0.0)
        high, own = zhi[...] * hi_z, zend[...]
        k = (dispersion * roll_tile(own, 32)) * roll_tile(high, 64)
        v = roll_tile(own, 64)
        a, b = k - jnp.minimum(v, 0.0), k + jnp.maximum(v, 0.0)
        high_c = a * high - k * own
        high_l = b * roll_tile(high, 96) - k * roll_tile(own, 96)

        def lay(parts):
            out = parts[0]
            for n in range(1, 4):
                out = jnp.where(lane1 >= 32 * n, roll_tile(parts[n], 32 * n), out)
            return out

        zc[...] = lay([low_c, low_l, high_c, high_l])
        cz_ref[...] = lay([coef, b, k, jnp.zeros_like(k)])
        lz_ref[...] = jnp.zeros_like(lz_ref)

    @pl.when(step == CX // PLANES - 1)
    def _():
        k = (dispersion * weight_of(solid_ref[PLANES - 1])) * (weight_of(xhi_s[...]) * hi_x)
        v = vend_ref[0]
        a, b = k - jnp.minimum(v, 0.0), k + jnp.maximum(v, 0.0)
        xc[2] = a * (xhi[0] * hi_x) - k * conc_ref[PLANES - 1]
        xc[3] = b * (xhi[1] * hi_x) - k * adj_ref[PLANES - 1]
        cx_ref[1] = b
        cx_ref[2] = k

    ids = lax.broadcasted_iota(i32, (128, CZ), 0).astype(f32).astype(bf16)
    zero, one = jnp.zeros((32, CZ), bf16), jnp.ones((32, CZ), bf16)
    rows_of = CY // CHUNKS
    width = rows_of * CZ

    def product(g):
        span = slice(g * width, (g + 1) * width)
        return lax.dot_general(
            hot_lo[:, span], hot_hi[:, span], (((1,), (1,)), ((), ())), preferred_element_type=f32
        )

    def make_hot(g):
        def row(plane):
            half = jnp.broadcast_to(plane, (16, CZ)).astype(bf16)
            return jnp.concatenate([half, half], axis=0)

        for y in range(g * rows_of, (g + 1) * rows_of):
            span = slice(y * CZ, y * CZ + CZ)
            mask = ids[0:32] == row(hi_f[y:y + 1, :])
            for k in range(DIGITS):
                hot_hi[32 * k:32 * k + 32, span] = jnp.where(mask, row(term_f[k, y:y + 1, :]), zero).astype(f8)
            low = row(lo_f[y:y + 1, :])
            for j in range(4):
                at_j = slice(32 * j, 32 * j + 32)
                hot_lo[at_j, span] = jnp.where(ids[at_j] == low, one, zero).astype(f8)

    def rate_of(p, g):
        halves = []
        for h in range(2):
            s = slot_ref[p, 8 * g:8 * g + 8, 128 * h:128 * h + 128]
            lo, hi = s & 127, s >> 7
            level = [
                jnp.take_along_axis(jnp.broadcast_to(table[r:r + 1, :], (8, 128)), lo, axis=1)
                for r in range(16)
            ]
            for bit in range(4):
                mask = (hi & (1 << bit)) != 0
                level = [
                    jnp.where(mask, level[2 * j + 1], level[2 * j]) for j in range(len(level) // 2)
                ]
            both = level[0]
            value = jnp.where((hi & 16) != 0, lax.shift_right_logical(both, 16), both & 65535)
            halves.append(value.astype(f32) * rate_step)
        return jnp.concatenate(halves, axis=1)

    def one_plane(p):
        i = step * PLANES + p
        acc = total[...]
        lookups = []
        per = CY // 8 // CHUNKS
        for g in range(CHUNKS):
            acc = acc + product(g)
            for n in range(per):
                lookups.append(rate_of(p, g * per + n))
            make_hot(g)
        total[...] = acc
        at = pl.ds(i, 1)
        end = i == CX - 1
        ri = lax.broadcasted_iota(i32, (8, CZ), 0)
        edge = jnp.where((i == 0) | end, 1.0, 0.0).astype(f32)
        edge_at = 0 if p == 0 else 2

        def with_faces(v, n):
            v = v + edge * xc[edge_at + n]
            low = roll_tile(zc[...], lax.rem(256 - i - 32 * n, 128))
            high = roll_tile(zc[...], lax.rem(319 - i - 32 * n, 128))
            v = v + jnp.concatenate(
                [jnp.where(lane1 == 0, low, 0.0), jnp.where(lane1 == 127, high, 0.0)], axis=1
            )
            first = v[0:8, :] + jnp.where(ri == 0, yc[n, at, :], 0.0)
            final = v[CY - 8:CY, :] + jnp.where(ri == 7, yc[2 + n, at, :], 0.0)
            return jnp.concatenate([first, v[8:CY - 8, :], final], axis=0)

        c, l = conc_ref[p], adj_ref[p]
        sol = solid_ref[p].astype(f32)

        kv = sol * jnp.concatenate(lookups, axis=0)

        def inverse(v):
            r = pl.reciprocal(v, approx=True)
            return r * (2.0 - v * r)

        m = adjload_ref[p]
        u0 = inverse(1.0 + c)
        e0 = c * u0 - load_ref[p]
        r = kv * e0
        conc1 = with_faces(s1_ref[p], 0) - r
        load1 = load_ref[p] + r
        d1 = m - l
        u1 = inverse(1.0 + conc1)
        kd = kv * d1
        adj1 = with_faces(s2_ref[p], 1) + kd * (u1 * u1)
        m1 = m - kd
        d0 = m1 - adj1
        kd = kv * d0
        mstart_ref[p] = m1 - kd
        rest = sol * ((conc1 * u1 - load1) * d1 + e0 * d0)
        for k in range(DIGITS):
            digit = rest.astype(f8).astype(f32)
            term_f[k] = digit
            rest = (rest - digit) * 16.0
        base_ref[p] = adj1 + kd * (u0 * u0)
        adj1_ref[p] = adj1
        ly_ref[0, at, :] = adj1[0:1, :]
        ly_ref[1, at, :] = adj1[CY - 1:CY, :]
        packed_l = jnp.where(lane1 == i, adj1[:, 0:1], lz_ref[...])
        lz_ref[...] = jnp.where(lane1 == i + 32, adj1[:, CZ - 1:CZ], packed_l)

        slots = slot_ref[p]
        hi_f[...] = (slots >> 7).astype(f32)
        lo_f[...] = (slots & 127).astype(f32)

    for p in range(PLANES):
        one_plane(p)

    @pl.when(step == CX // PLANES - 1)
    def _():
        for g in range(CHUNKS):
            total[...] = total[...] + product(g)
            make_hot(g)
        for g in range(CHUNKS):
            total[...] = total[...] + product(g)
        by_lane = total[...].T
        sums = by_lane[32 * DIGITS - 32:32 * DIGITS]
        for k in range(DIGITS - 2, -1, -1):
            sums = by_lane[32 * k:32 * k + 32] + sums * (1.0 / 16.0)
        places = places_ref[...]
        high = sums.astype(bf16)
        high_f = high.astype(f32)
        low_f = sums - high_f
        place_lane = (places & 127).astype(f32)
        place_row = places >> 7
        lane_ids = lax.broadcasted_iota(i32, (128, 128), 0).astype(f32)

        row_ids = lax.broadcasted_iota(i32, (256, 128), 0).astype(f32).astype(bf16)
        row_f = place_row.astype(f32)
        ones, zeros = jnp.ones((256, 128), bf16), jnp.zeros((256, 128), bf16)

        values = []
        for s in range(32):
            match = lane_ids == place_lane[s:s + 1, :]
            values.append(
                jnp.concatenate(
                    [
                        jnp.where(match, high_f[s:s + 1, :], 0.0).astype(bf16),
                        jnp.where(match, low_f[s:s + 1, :], 0.0).astype(bf16),
                    ],
                    axis=0,
                )
            )
        value = jnp.concatenate(values, axis=1)

        def spread(n, carry):
            first = (n * 256).astype(f32)
            hot = jnp.concatenate(
                [
                    jnp.where(
                        row_ids == jnp.broadcast_to(row_f[s:s + 1, :] - first, (256, 128)).astype(bf16),
                        ones, zeros,
                    )
                    for s in range(32)
                ],
                axis=1,
            )
            got = lax.dot_general(
                hot, value, (((1,), (1,)), ((), ())), preferred_element_type=f32
            )
            dense_ref[pl.ds(pl.multiple_of(n * 256, 256), 256), :] = got[:, 0:128] + got[:, 128:256]
            return carry

        lax.fori_loop(0, 8, spread, 0)


def call_main(block, arrays, faces, home, slot_grain):
    conc, load, adj, adj_load, vx, solid, slot = arrays
    plane = pl.BlockSpec((PLANES, CY, CZ), lambda i, b: (i, 0, 0))

    def whole(shape):
        return pl.BlockSpec(shape, lambda i, b: (0,) * len(shape))

    face_shapes = [
        (3, CY, CZ), (CY, CZ), (2, CY, CZ), (CY, CZ), (4, CX, CZ), (3, CX, CZ),
        (CY, 128), (CY, 128), (3, CX, CZ), (CY, 128), (4, CX, CZ), (CY, 128), (2048, 128),
    ]
    block_shape = (CX, CY, CZ)
    out_shapes = [
        block_shape, block_shape, block_shape, (2048, 128), (2, CX, CZ), (CY, 128),
        (3, CY, CZ), (3, CX, CZ), (CY, 128),
    ]
    plane_scratch = pltpu.VMEM((CY, CZ), f32)
    return pl.pallas_call(
        main_kernel,
        out_shape=[jax.ShapeDtypeStruct(s, f32) for s in out_shapes],
        grid_spec=pltpu.PrefetchScalarGridSpec(
            num_scalar_prefetch=1,
            grid=(CX // PLANES,),
            in_specs=[plane] * 8
            + [pl.BlockSpec((1, CY, CZ), lambda i, b: (CX - 1, 0, 0))]
            + [whole(s) for s in face_shapes]
            + [
                pl.BlockSpec((1, 16, 128), lambda i, b: (b[0], 0, 0)),
                pl.BlockSpec((1, 16, 128), lambda i, b: (lax.rem(b[0] + 1, 128), 0, 0)),
                whole((32, 128)),
            ],
            out_specs=[plane] * 3 + [whole(s) for s in out_shapes[3:]],
            scratch_shapes=[
                pltpu.VMEM((2048, 128), i32), pltpu.VMEM((32, 128), i32), pltpu.VMEM((16, 128), i32),
                pltpu.VMEM((4, CY, CZ), f32), pltpu.VMEM((4, CX, CZ), f32), pltpu.VMEM((CY, 128), f32),
                plane_scratch, plane_scratch, pltpu.VMEM((DIGITS, CY, CZ), f32),
                pltpu.VMEM((128, CY * CZ), f8), pltpu.VMEM((32 * DIGITS, CY * CZ), f8),
                pltpu.VMEM((128, 32 * DIGITS), f32), pltpu.VMEM((256, 4096), f32), pltpu.VMEM((32, 128), f32),
            ],
        ),
        compiler_params=pltpu.CompilerParams(
            dimension_semantics=("arbitrary",), vmem_limit_bytes=58 << 20
        ),
        cost_estimate=pl.CostEstimate(flops=10 ** 9, bytes_accessed=25 << 20, transcendentals=0),
    )(
        block, faces[13], faces[14], conc, adj, solid, load, adj_load, slot, vx,
        *faces[:12], faces[12].reshape(2048, 128), home, home, slot_grain,
    )


def finish_kernel(
    adj1, base, solid, vx, vy, vz, dense, ly, lz, cx, cy, cz,
    out, grad,
    lb, fb, sb, vxb, vyb, vzb, qx, yc, zc,
    xlo, xhi, ylo, yhi, zlo, zhi, d1, r1, r2y, r2z, s2y, s2z, r3z, r3y,
    lsem, ssem, rsem,
):
    gx, gy, gz = (lax.axis_index(a) for a in ("gx", "gy", "gz"))
    xh, core = gx // 2, lax.rem(gx, 2)
    has = lambda cond: jnp.where(cond, 1.0, 0.0).astype(f32)
    hi_x, hi_y, hi_z = has(gx < 3), has(gy < 7), has(gz < 3)
    keep = pltpu.make_async_copy(dense.at[:, core], d1, lsem.at[0])
    keep.start()
    loads = [
        pltpu.make_async_copy(ref, buf, lsem.at[1 + k])
        for k, (ref, buf) in enumerate(
            ((adj1, lb), (base, fb), (solid, sb), (vx, vxb), (vy, vyb), (vz, vzb))
        )
    ]
    for copy in loads:
        copy.start()
    greet()
    started = []
    send = sender(started, ssem, rsem)
    first = send(dense.at[:, 1 - core], r1, {"gx": gx + 1 - 2 * core})
    faces = [
        send(adj1.at[CX - 1], xlo, {"gx": lax.rem(gx + 1, 4)}),
        send(adj1.at[0], xhi, {"gx": lax.rem(gx + 3, 4)}),
        send(ly.at[1], ylo, {"gy": lax.rem(gy + 1, 8)}),
        send(ly.at[0], yhi, {"gy": lax.rem(gy + 7, 8)}),
        send(lz, zlo, {"gz": lax.rem(gz + 1, 4)}),
        send(lz, zhi, {"gz": lax.rem(gz + 3, 4)}),
    ]
    keep.wait()
    first.wait_recv()

    def add_first(h, carry):
        for x in range(2):
            d1[x, h] = d1[x, h] + r1[x, h]
        return carry

    lax.fori_loop(0, 8, add_first, 0)
    ys = [lax.rem(gy + o, 8) for o in range(8)]
    zs = [lax.rem(gz + o, 4) for o in range(4)]
    near = [(dx, o) for dx in range(2) for o in range(8) if dx + o > 0]
    side = lambda dx: gx + dx * (2 - 4 * xh)
    half = lambda dx: xh + dx * (1 - 2 * xh)
    second = (
        [send(d1.at[:, ys[o]], r2y.at[o - 1], {"gy": ys[o]}, 6 + o) for o in range(1, 8)],
        [send(d1.at[:, :, zs[o]], r2z.at[o - 1], {"gz": zs[o]}, 13 + o) for o in range(1, 4)],
    )
    third = (
        [
            send(s2y.at[half(dx), zs[o]], r3z.at[n], {"gx": side(dx), "gz": zs[o]}, 17 + n)
            for n, (dx, o) in enumerate([p for p in near if p[1] < 4])
        ],
        [
            send(s2z.at[half(dx), ys[o]], r3y.at[n], {"gx": side(dx), "gy": ys[o]}, 24 + n)
            for n, (dx, o) in enumerate(near)
        ],
    )
    for way in range(2):
        @pl.when(core == way)
        def _():
            each(second[way], "start")

    for copy in loads:
        copy.wait()
    for copy in faces:
        copy.wait_recv()
    fb[0] = fb[0] + cx[0] * (xlo[...] - lb[0])
    fb[CX - 1] = fb[CX - 1] + cx[1] * (xhi[...] * hi_x) - cx[2] * lb[CX - 1]
    yc[0] = cy[0] * (ylo[...] - ly[0])
    yc[1] = cy[1] * (yhi[...] * hi_y) - cy[2] * ly[1]
    lane1 = lax.broadcasted_iota(i32, (CY, 128), 1)
    own, coef = lz[...], cz[...]
    zc[...] = jnp.where(
        lane1 < 32,
        coef * (pltpu.roll(zlo[...], 96, 1) - own),
        coef * (pltpu.roll(zhi[...], 32, 1) * hi_z) - pltpu.roll(coef, 96, 1) * own,
    )
    qx[...] = jnp.zeros_like(qx)

    def plane(x, carry):
        ri, li, lane = plane_iotas()
        up_y, down_y, up_z, down_z = shifts(ri, li)
        at = pl.ds(x, 1)
        nx = jnp.minimum(x + 1, CX - 1)
        inside = jnp.where(x < CX - 1, 1.0, 0.0).astype(f32)
        l, w = lb[x], weight_of(sb[x])
        a, b = pair(w, weight_of(sb[nx]) * inside, vxb[x])
        d = lb[nx] * inside - l
        lap = fb[x] + b * d - qx[...]
        qx[...] = a * d
        a, b = pair(w, up_y(w), vyb[x])
        d = up_y(l) - l
        lap = lap + b * d - down_y(a * d)
        a, b = pair(w, up_z(w), vzb[x])
        d = up_z(l) - l
        lap = lap + b * d - down_z(a * d)
        cols = zc[...]
        low = pltpu.roll(cols, lax.rem(128 - x, 128), 1)
        high = pltpu.roll(cols, 95 - x, 1)
        lap = lap + jnp.concatenate(
            [jnp.where(lane == 0, low, 0.0), jnp.where(lane == 127, high, 0.0)], axis=1
        )
        fb[x] = lap
        fb[x, 0:1, :] = lap[0:1, :] + yc[0, at, :]
        fb[x, CY - 1:CY, :] = lap[CY - 1:CY, :] + yc[1, at, :]
        return carry

    lax.fori_loop(0, 16, plane, 0)
    store = [pltpu.make_async_copy(fb.at[0:16], out.at[0:16], lsem.at[7])]
    store[0].start()
    for way in range(2):
        @pl.when(core == way)
        def _():
            each(second[way], "wait_recv")

    @pl.when(core == 0)
    def _():
        for x in range(2):
            acc = d1[x, gy]
            for o in range(7):
                acc = acc + r2y[o, x]
            s2y[x] = acc
        each(third[0], "start")

    @pl.when(core == 1)
    def _():
        for x in range(2):
            for h in range(8):
                acc = d1[x, h, gz]
                for o in range(3):
                    acc = acc + r2z[o, x, h]
                s2z[x, h] = acc
        each(third[1], "start")

    lax.fori_loop(16, CX, plane, 0)
    store.append(pltpu.make_async_copy(fb.at[16:32], out.at[16:32], lsem.at[8]))
    store[1].start()

    @pl.when(core == 0)
    def _():
        each(third[0], "wait_recv")
        acc = s2y[xh, gz]
        for n in range(7):
            acc = acc + r3z[n]
        grad[...] = acc

    @pl.when(core == 1)
    def _():
        each(third[1], "wait_recv")
        acc = s2z[xh, gy]
        for n in range(15):
            acc = acc + r3y[n]
        grad[...] = acc

    for way in range(2):
        @pl.when(core == way)
        def _():
            each(second[way], "wait_send")
            each(third[way], "wait_send")

    for copy in started:
        copy.wait_send()
    for copy in store:
        copy.wait()


def call_finish(adj1, base, solid, vx, vy, vz, dense, ly, lz, cx, cy, cz):
    vmem = pl.BlockSpec(memory_space=pltpu.VMEM)
    whole = pltpu.VMEM((CX, CY, CZ), f32)
    return pl.pallas_call(
        finish_kernel,
        out_shape=(
            jax.ShapeDtypeStruct((CX, CY, CZ), f32), jax.ShapeDtypeStruct((16, 128), f32)
        ),
        in_specs=[ANY] * 7 + [vmem] * 5,
        out_specs=(ANY, vmem),
        scratch_shapes=[
            whole, whole, pltpu.VMEM((CX, CY, CZ), i32), whole, whole, whole,
            pltpu.VMEM((CY, CZ), f32), pltpu.VMEM((2, CX, CZ), f32), pltpu.VMEM((CY, 128), f32),
            pltpu.VMEM((CY, CZ), f32), pltpu.VMEM((CY, CZ), f32),
            pltpu.VMEM((CX, CZ), f32), pltpu.VMEM((CX, CZ), f32),
            pltpu.VMEM((CY, 128), f32), pltpu.VMEM((CY, 128), f32),
            pltpu.VMEM((2, 8, 4, 16, 128), f32), pltpu.VMEM((2, 8, 4, 16, 128), f32),
            pltpu.VMEM((7, 2, 4, 16, 128), f32), pltpu.VMEM((3, 2, 8, 16, 128), f32),
            pltpu.VMEM((2, 4, 16, 128), f32), pltpu.VMEM((2, 8, 16, 128), f32),
            pltpu.VMEM((7, 16, 128), f32), pltpu.VMEM((15, 16, 128), f32),
            pltpu.SemaphoreType.DMA((9,)), pltpu.SemaphoreType.DMA((39,)),
            pltpu.SemaphoreType.DMA((39,)),
        ],
        compiler_params=pltpu.CompilerParams(
            collective_id=1, has_side_effects=True, vmem_limit_bytes=62 << 20
        ),
    )(adj1, base, solid, vx, vy, vz, dense, ly, lz, cx, cy, cz)


PARTS = 8


def hand_on_kernel(start, grad, start_out, grad_out, buf, in_sem, out_sem):
    size = CX // PARTS
    small = pltpu.make_async_copy(grad, grad_out, in_sem.at[PARTS])
    small.start()
    parts = [pl.ds(size * q, size) for q in range(PARTS)]
    ins = [pltpu.make_async_copy(start.at[p], buf.at[p], in_sem.at[q]) for q, p in enumerate(parts)]
    outs = [
        pltpu.make_async_copy(buf.at[p], start_out.at[p], out_sem.at[q]) for q, p in enumerate(parts)
    ]
    for copy in ins:
        copy.start()
    for q in range(PARTS):
        ins[q].wait()
        outs[q].start()
    for copy in outs:
        copy.wait()
    small.wait()


def hand_on(start, grad):
    return pl.pallas_call(
        hand_on_kernel,
        out_shape=(jax.ShapeDtypeStruct(start.shape, f32), jax.ShapeDtypeStruct(grad.shape, f32)),
        in_specs=[ANY] * 2,
        out_specs=[ANY] * 2,
        scratch_shapes=[
            pltpu.VMEM((CX, CY, CZ), f32), pltpu.SemaphoreType.DMA((PARTS + 1,)),
            pltpu.SemaphoreType.DMA((PARTS,)),
        ],
        compiler_params=pltpu.CompilerParams(vmem_limit_bytes=62 << 20),
    )(start, grad)


def per_device(
    conc, load, adj_conc, adj_load, vel_x, vel_y, vel_z, solid, voxel_slot, slot_grain, grain_home, rates
):
    block = (lax.axis_index("gx") * 32 + lax.axis_index("gy") * 4 + lax.axis_index("gz")).astype(i32)
    faces = call_faces(conc, adj_conc, vel_x, vel_y, vel_z, solid, rates.reshape(16, 128))
    arrays = (conc, load, adj_conc, adj_load, vel_x, solid, voxel_slot)
    adj1, base, load_start, dense, ly, lz, cx, cy, cz = call_main(
        block.reshape(1), arrays, faces, grain_home.reshape(128, 16, 128), slot_grain.reshape(32, 128)
    )
    start, grad = call_finish(
        adj1, base, solid, vel_x, vel_y, vel_z, dense.reshape(2, 2, 8, 4, 16, 128), ly, lz, cx, cy, cz
    )
    start, grad = hand_on(start, grad)
    return start, load_start, grad.reshape(2048)


def solution(mesh):
    cells = P("gx", "gy", "gz")
    every = P(("gx", "gy", "gz"))
    return jax.shard_map(
        per_device,
        mesh=mesh,
        in_specs=(cells,) * 9 + (P(("gx", "gy", "gz"), None), P(), every),
        out_specs=(cells, cells, every),
        check_vma=False,
    )
```

```python
import functools

import jax
import jax.numpy as jnp
from jax import lax
from jax.experimental import pallas as pl
from jax.experimental.pallas import tpu as pltpu
from jax.sharding import PartitionSpec as P

f32, bf16, i32, f8 = jnp.float32, jnp.bfloat16, jnp.int32, jnp.float8_e4m3fn
DIGITS = 3
CHUNKS = 4
PLANES = 4
MESH = pl.DeviceIdType.MESH
ANY = pl.BlockSpec(memory_space=pl.ANY)
dispersion = 0.06
rate_step = 0.2 / 65535.0
CX, CY, CZ = 32, 64, 256


def greet():
    barrier = pltpu.get_barrier_semaphore()
    for axis, count in (("gx", 4), ("gy", 8), ("gz", 4)):
        me = lax.axis_index(axis)
        for o in range(1, count):
            pl.semaphore_signal(
                barrier, inc=1, device_id={axis: lax.rem(me + o, count)}, device_id_type=MESH
            )
    gx = lax.axis_index("gx")
    across = gx + 2 - 4 * (gx // 2)
    for axis, count in (("gy", 8), ("gz", 4)):
        me = lax.axis_index(axis)
        for o in range(1, count):
            pl.semaphore_signal(
                barrier, inc=1, device_id={"gx": across, axis: lax.rem(me + o, count)},
                device_id_type=MESH,
            )
    pl.semaphore_wait(barrier, 23)


def weight_of(s):
    return 1.0 - 0.7 * s.astype(f32)


def pair(w0, w1, v):
    k = (dispersion * w0) * w1
    return k - jnp.minimum(v, 0.0), k + jnp.maximum(v, 0.0)


def plane_iotas():
    return (
        lax.broadcasted_iota(i32, (CY, CZ), 0),
        lax.broadcasted_iota(i32, (CY, CZ), 1),
        lax.broadcasted_iota(i32, (CY, 128), 1),
    )


def shifts(ri, li):
    return (
        lambda v: jnp.where(ri == CY - 1, 0.0, pltpu.roll(v, CY - 1, 0)),
        lambda v: jnp.where(ri == 0, 0.0, pltpu.roll(v, 1, 0)),
        lambda v: jnp.where(li == CZ - 1, 0.0, pltpu.roll(v, CZ - 1, 1)),
        lambda v: jnp.where(li == 0, 0.0, pltpu.roll(v, 1, 1)),
    )


def sender(started, ssem, rsem):
    def send(src, dst, where, slot=None):
        k = len(started) if slot is None else slot
        copy = pltpu.make_async_remote_copy(
            src_ref=src, dst_ref=dst, send_sem=ssem.at[k], recv_sem=rsem.at[k],
            device_id=where, device_id_type=MESH,
        )
        if slot is None:
            copy.start()
            started.append(copy)
        return copy

    return send


def each(copies, what):
    for copy in copies:
        getattr(copy, what)()


def gather_faces(
    conc, adj, vx, vy, vz, solid, rates,
    xlo, xlo_s, xhi, xhi_s, ylo, yhi, zlo, zhi, yown, zown, yend, zend, rall, s1_out, s2_out,
    cb, lb, vxb, vyb, vzb, sb, s1, s2, hx, qx, yfwd, ybwd, zfwd, zbwd, lsem, rsem, osem, ssem,
):
    gx, gy, gz = (lax.axis_index(a) for a in ("gx", "gy", "gz"))
    xh, core = gx // 2, lax.rem(gx, 2)
    local = []
    for q in range(4):
        at = pl.ds(8 * q, 8)
        local.append([
            pltpu.make_async_copy(ref.at[at], buf.at[at], lsem.at[6 * q + k])
            for k, (ref, buf) in enumerate(
                ((conc, cb), (adj, lb), (solid, sb), (vx, vxb), (vy, vyb), (vz, vzb))
            )
        ])
        for copy in local[q]:
            copy.start()
    mine = pltpu.make_async_copy(rates, rall.at[xh, core, gy, gz], osem.at[0])
    mine.start()
    greet()

    started = []
    send = sender(started, ssem, rsem)
    one, row_y, row_z = rall.at[xh, core, gy, gz], rall.at[:, core, gy], rall.at[:, core, :, gz]
    near = [(dx, o) for dx in range(2) for o in range(8) if dx + o > 0]
    side = lambda dx: gx + dx * (2 - 4 * xh)
    second = (
        [
            send(rates, one, {"gx": side(dx), "gz": lax.rem(gz + o, 4)}, 12 + n)
            for n, (dx, o) in enumerate([p for p in near if p[1] < 4])
        ],
        [
            send(rates, one, {"gx": side(dx), "gy": lax.rem(gy + o, 8)}, 19 + n)
            for n, (dx, o) in enumerate(near)
        ],
    )
    third = (
        [send(row_y, row_y, {"gy": lax.rem(gy + o, 8)}, 33 + o) for o in range(1, 8)],
        [send(row_z, row_z, {"gz": lax.rem(gz + o, 4)}, 40 + o) for o in range(1, 4)],
    )
    for way in range(2):
        @pl.when(core == way)
        def _():
            each(second[way], "start")

    right, left = {"gx": lax.rem(gx + 1, 4)}, {"gx": lax.rem(gx + 3, 4)}
    faces = []
    for k, ref in enumerate((conc, adj, vx)):
        faces.append(send(ref.at[CX - 1], xlo.at[k], right))
    faces.append(send(solid.at[CX - 1], xlo_s, right))
    for k, ref in enumerate((conc, adj)):
        faces.append(send(ref.at[0], xhi.at[k], left))
    faces.append(send(solid.at[0], xhi_s, left))

    hx[...] = jnp.zeros_like(hx)
    qx[...] = jnp.zeros_like(qx)
    zfwd[...] = jnp.zeros_like(zfwd)
    zbwd[...] = jnp.zeros_like(zbwd)

    def plane(x, carry):
        ri, li, lane = plane_iotas()
        up_y, down_y, up_z, down_z = shifts(ri, li)
        at = pl.ds(x, 1)
        nx = jnp.minimum(x + 1, CX - 1)
        inside = jnp.where(x < CX - 1, 1.0, 0.0).astype(f32)
        c, l, w = cb[x], lb[x], weight_of(sb[x])
        v_x, v_y, v_z = vxb[x], vyb[x], vzb[x]
        a, b = pair(w, weight_of(sb[nx]) * inside, v_x)
        flux = a * (cb[nx] * inside) - b * c
        div = c + flux - hx[...]
        hx[...] = flux
        d = lb[nx] * inside - l
        lap = l + b * d - qx[...]
        qx[...] = a * d
        a, b = pair(w, up_y(w), v_y)
        flux = a * up_y(c) - b * c
        div = div + flux - down_y(flux)
        d = up_y(l) - l
        lap = lap + b * d - down_y(a * d)
        a, b = pair(w, up_z(w), v_z)
        flux = a * up_z(c) - b * c
        s1[x] = div + flux - down_z(flux)
        d = up_z(l) - l
        s2[x] = lap + b * d - down_z(a * d)
        return carry

    def edges(x, carry):
        lane = lax.broadcasted_iota(i32, (CY, 128), 1)
        at = pl.ds(x, 1)
        c, l, w, v_y, v_z = cb[x], lb[x], weight_of(sb[x]), vyb[x], vzb[x]
        for k, v in enumerate((c, l, v_y, w)):
            yfwd[k, at, :] = v[CY - 1:CY, :]
        for k, v in enumerate((c, l, w)):
            ybwd[k, at, :] = v[0:1, :]
        pack = zfwd[...]
        for k, v in enumerate((c, l, v_z, w)):
            pack = jnp.where(lane == x + 32 * k, v[:, CZ - 1:CZ], pack)
        zfwd[...] = pack
        pack = zbwd[...]
        for k, v in enumerate((c, l, w)):
            pack = jnp.where(lane == x + 32 * k, v[:, 0:1], pack)
        zbwd[...] = pack
        return carry

    def arrived(q):
        for copy in local[q]:
            copy.wait()

    mine.wait()
    for q in range(4):
        arrived(q)
    lax.fori_loop(0, CX, edges, 0)
    faces.append(send(yfwd, ylo, {"gy": lax.rem(gy + 1, 8)}))
    faces.append(send(ybwd, yhi, {"gy": lax.rem(gy + 7, 8)}))
    faces.append(send(zfwd, zlo, {"gz": lax.rem(gz + 1, 4)}))
    faces.append(send(zbwd, zhi, {"gz": lax.rem(gz + 3, 4)}))
    for way in range(2):
        @pl.when(core == way)
        def _():
            each(second[way], "wait_recv")
            each(third[way], "start")

    lax.fori_loop(0, 24, plane, 0)
    for way in range(2):
        @pl.when(core == way)
        def _():
            each(third[way], "wait_recv")
            each(second[way], "wait_send")
            each(third[way], "wait_send")

    last = send(rall.at[:, core], rall.at[:, core], {"gx": gx + 1 - 2 * core})
    outs = [
        pltpu.make_async_copy(s1.at[0:24], s1_out.at[0:24], osem.at[1]),
        pltpu.make_async_copy(s2.at[0:24], s2_out.at[0:24], osem.at[2]),
    ]
    for copy in outs:
        copy.start()
    lax.fori_loop(24, CX, plane, 0)
    keep = [
        pltpu.make_async_copy(s1.at[24:32], s1_out.at[24:32], osem.at[3]),
        pltpu.make_async_copy(s2.at[24:32], s2_out.at[24:32], osem.at[4]),
        pltpu.make_async_copy(yfwd, yend, osem.at[5]),
        pltpu.make_async_copy(ybwd, yown, osem.at[6]),
        pltpu.make_async_copy(zfwd, zend, osem.at[7]),
        pltpu.make_async_copy(zbwd, zown, osem.at[8]),
    ]
    for copy in keep:
        copy.start()
    last.wait_recv()
    for copy in faces:
        copy.wait_recv()
    for copy in started:
        copy.wait_send()
    for copy in outs + keep:
        copy.wait()


def call_faces(conc, adj, vx, vy, vz, solid, rates):
    face = lambda *s: jax.ShapeDtypeStruct(s, f32)
    outs = (
        face(3, CY, CZ), jax.ShapeDtypeStruct((CY, CZ), i32),
        face(2, CY, CZ), jax.ShapeDtypeStruct((CY, CZ), i32),
        face(4, CX, CZ), face(3, CX, CZ),
        face(CY, 128), face(CY, 128), face(3, CX, CZ), face(CY, 128),
        face(4, CX, CZ), face(CY, 128),
        face(2, 2, 8, 4, 16, 128), face(CX, CY, CZ), face(CX, CY, CZ),
    )
    whole = pltpu.VMEM((CX, CY, CZ), f32)
    return pl.pallas_call(
        gather_faces,
        out_shape=outs,
        in_specs=[ANY] * 7,
        out_specs=[ANY] * len(outs),
        scratch_shapes=[
            whole, whole, whole, whole, whole, pltpu.VMEM((CX, CY, CZ), i32), whole, whole,
            pltpu.VMEM((CY, CZ), f32), pltpu.VMEM((CY, CZ), f32),
            pltpu.VMEM((4, CX, CZ), f32), pltpu.VMEM((3, CX, CZ), f32),
            pltpu.VMEM((CY, 128), f32), pltpu.VMEM((CY, 128), f32),
            pltpu.SemaphoreType.DMA((24,)), pltpu.SemaphoreType.DMA((44,)),
            pltpu.SemaphoreType.DMA((9,)), pltpu.SemaphoreType.DMA((44,)),
        ],
        compiler_params=pltpu.CompilerParams(
            collective_id=0, has_side_effects=True, vmem_limit_bytes=62 << 20
        ),
    )(conc, adj, vx, vy, vz, solid, rates)


def roll_tile(tile, shift):
    return pltpu.roll(tile, shift, 1)


def main_kernel(
    block_ref,
    s1_ref, s2_ref, conc_ref, adj_ref, solid_ref, load_ref, adjload_ref, slot_ref, vend_ref,
    xlo, xlo_s, xhi, xhi_s, ylo, yhi, zlo, zhi, yown, zown, yend, zend, rall, home0, home1, slot_grain,
    adj1_ref, base_ref, mstart_ref, dense_ref, ly_ref, lz_ref, cx_ref, cy_ref, cz_ref,
    packed, places_ref, table, xc, yc, zc,
    hi_f, lo_f, term_f, hot_lo, hot_hi, total, got_ref, look_ref,
):
    step = pl.program_id(0)
    gx, gy, gz = (lax.axis_index(a) for a in ("gx", "gy", "gz"))
    has = lambda cond: jnp.where(cond, 1.0, 0.0).astype(f32)
    lo_x, hi_x = has(gx > 0), has(gx < 3)
    lo_y, hi_y = has(gy > 0), has(gy < 7)
    lo_z, hi_z = has(gz > 0), has(gz < 3)
    lane1 = lax.broadcasted_iota(i32, (CY, 128), 1)
    @pl.when(step == 0)
    def _():
        total[...] = jnp.zeros_like(total)
        hot_lo[...] = jnp.zeros_like(hot_lo)
        term_f[...] = jnp.zeros_like(term_f)
        hi_f[...] = jnp.zeros_like(hi_f)
        lo_f[...] = jnp.zeros_like(lo_f)
        hot_hi[...] = jnp.zeros_like(hot_hi)
        def pack(r, carry):
            at = pl.ds(pl.multiple_of(r * 128, 128), 128)
            packed[at, :] = (rall[at, :] * (1.0 / rate_step) + 0.5).astype(i32)
            return carry

        lax.fori_loop(0, 16, pack, 0)
        base = (slot_grain[...] - block_ref[0] * 2048) & 262143
        lanes = [base[8 * j:8 * j + 8] & 127 for j in range(4)]
        rows = [base[8 * j:8 * j + 8] >> 7 for j in range(4)]
        found = [jnp.zeros((8, 128), i32)] * 4
        for r in range(32):
            src = home0 if r < 16 else home1
            row = jnp.broadcast_to(src[0, r % 16:r % 16 + 1, :], (8, 128))
            for j in range(4):
                found[j] = jnp.where(
                    rows[j] == r, jnp.take_along_axis(row, lanes[j], axis=1), found[j]
                )
        for j in range(4):
            places_ref[8 * j:8 * j + 8, :] = found[j]
        lanes = [f & 127 for f in found]
        rows = [(f >> 7) & 1023 for f in found]


        sub_ids = lax.broadcasted_iota(i32, (256, 128), 0).astype(f32).astype(bf16)
        ones, zeros = jnp.ones((256, 128), bf16), jnp.zeros((256, 128), bf16)

        def look(n, acc):
            at = pl.ds(pl.multiple_of(n * 256, 256), 256)
            q = packed[at, :]
            digits = jnp.concatenate([(q & 255).astype(f32).astype(bf16), ((q >> 8) & 255).astype(f32).astype(bf16)], axis=1)
            first = (n * 256).astype(f32)
            hot = jnp.concatenate(
                [
                    jnp.where(
                        sub_ids == jnp.broadcast_to((found[s // 8] >> 7).astype(f32)[s % 8:s % 8 + 1, :] - first, (256, 128)).astype(bf16),
                        ones, zeros,
                    )
                    for s in range(32)
                ],
                axis=1,
            )
            got_ref[...] = got_ref[...] + lax.dot_general(digits, hot, (((0,), (0,)), ((), ())), preferred_element_type=f32)
            return acc
        got_ref[...] = jnp.zeros_like(got_ref)
        lax.fori_loop(0, 8, look, 0)
        lids = lax.broadcasted_iota(i32, (128, 128), 0)
        for s in range(32):
            m = lids == (found[s // 8] & 127)[s % 8:s % 8 + 1, :]
            sp = slice(128 * s, 128 * s + 128)
            v = got_ref[0:128, sp] + 256.0 * got_ref[128:256, sp]
            look_ref[s:s + 1, :] = jnp.sum(jnp.where(m, v, 0.0), axis=0, keepdims=True)
        got = [look_ref[8 * j:8 * j + 8, :].astype(i32) for j in range(4)]
        table[0:8, :] = got[0] + (got[2] << 16)
        table[8:16, :] = got[1] + (got[3] << 16)

        a, b = pair(weight_of(xlo_s[...]) * lo_x, weight_of(solid_ref[0]), xlo[2] * lo_x)
        xc[0] = b * (xlo[0] * lo_x) - a * conc_ref[0]
        xc[1] = a * (xlo[1] * lo_x - adj_ref[0])
        xc[2] = xc[0]
        xc[3] = xc[1]
        cx_ref[0] = a
        a, b = pair(ylo[3] * lo_y, yown[2], ylo[2] * lo_y)
        yc[0] = b * (ylo[0] * lo_y) - a * yown[0]
        yc[1] = a * (ylo[1] * lo_y - yown[1])
        cy_ref[0] = a
        k = (dispersion * yend[3]) * (yhi[2] * hi_y)
        a, b = k - jnp.minimum(yend[2], 0.0), k + jnp.maximum(yend[2], 0.0)
        yc[2] = a * (yhi[0] * hi_y) - k * yend[0]
        yc[3] = b * (yhi[1] * hi_y) - k * yend[1]
        cy_ref[1] = b
        cy_ref[2] = k
        low, own = zlo[...] * lo_z, zown[...]
        a, b = pair(roll_tile(low, 32), roll_tile(own, 64), roll_tile(low, 64))
        low_c = b * low - a * own
        low_l = a * (roll_tile(low, 96) - roll_tile(own, 96))
        coef = jnp.where(lane1 < 32, a, 0.0)
        high, own = zhi[...] * hi_z, zend[...]
        k = (dispersion * roll_tile(own, 32)) * roll_tile(high, 64)
        v = roll_tile(own, 64)
        a, b = k - jnp.minimum(v, 0.0), k + jnp.maximum(v, 0.0)
        high_c = a * high - k * own
        high_l = b * roll_tile(high, 96) - k * roll_tile(own, 96)

        def lay(parts):
            out = parts[0]
            for n in range(1, 4):
                out = jnp.where(lane1 >= 32 * n, roll_tile(parts[n], 32 * n), out)
            return out

        zc[...] = lay([low_c, low_l, high_c, high_l])
        cz_ref[...] = lay([coef, b, k, jnp.zeros_like(k)])
        lz_ref[...] = jnp.zeros_like(lz_ref)

    @pl.when(step == CX // PLANES - 1)
    def _():
        k = (dispersion * weight_of(solid_ref[PLANES - 1])) * (weight_of(xhi_s[...]) * hi_x)
        v = vend_ref[0]
        a, b = k - jnp.minimum(v, 0.0), k + jnp.maximum(v, 0.0)
        xc[2] = a * (xhi[0] * hi_x) - k * conc_ref[PLANES - 1]
        xc[3] = b * (xhi[1] * hi_x) - k * adj_ref[PLANES - 1]
        cx_ref[1] = b
        cx_ref[2] = k

    ids = lax.broadcasted_iota(i32, (128, CZ), 0).astype(f32).astype(bf16)
    zero, one = jnp.zeros((32, CZ), bf16), jnp.ones((32, CZ), bf16)
    rows_of = CY // CHUNKS
    width = rows_of * CZ

    def product(g):
        span = slice(g * width, (g + 1) * width)
        return lax.dot_general(
            hot_lo[:, span], hot_hi[:, span], (((1,), (1,)), ((), ())), preferred_element_type=f32
        )

    def make_hot(g):
        def row(plane):
            half = jnp.broadcast_to(plane, (16, CZ)).astype(bf16)
            return jnp.concatenate([half, half], axis=0)

        for y in range(g * rows_of, (g + 1) * rows_of):
            span = slice(y * CZ, y * CZ + CZ)
            mask = ids[0:32] == row(hi_f[y:y + 1, :])
            for k in range(DIGITS):
                hot_hi[32 * k:32 * k + 32, span] = jnp.where(mask, row(term_f[k, y:y + 1, :]), zero).astype(f8)
            low = row(lo_f[y:y + 1, :])
            for j in range(4):
                at_j = slice(32 * j, 32 * j + 32)
                hot_lo[at_j, span] = jnp.where(ids[at_j] == low, one, zero).astype(f8)

    def rate_of(p, g):
        halves = []
        for h in range(2):
            s = slot_ref[p, 8 * g:8 * g + 8, 128 * h:128 * h + 128]
            lo, hi = s & 127, s >> 7
            level = [
                jnp.take_along_axis(jnp.broadcast_to(table[r:r + 1, :], (8, 128)), lo, axis=1)
                for r in range(16)
            ]
            for bit in range(4):
                mask = (hi & (1 << bit)) != 0
                level = [
                    jnp.where(mask, level[2 * j + 1], level[2 * j]) for j in range(len(level) // 2)
                ]
            both = level[0]
            value = jnp.where((hi & 16) != 0, lax.shift_right_logical(both, 16), both & 65535)
            halves.append(value.astype(f32) * rate_step)
        return jnp.concatenate(halves, axis=1)

    def one_plane(p):
        i = step * PLANES + p
        acc = total[...]
        lookups = []
        per = CY // 8 // CHUNKS
        for g in range(CHUNKS):
            acc = acc + product(g)
            for n in range(per):
                lookups.append(rate_of(p, g * per + n))
            make_hot(g)
        total[...] = acc
        at = pl.ds(i, 1)
        end = i == CX - 1
        ri = lax.broadcasted_iota(i32, (8, CZ), 0)
        edge = jnp.where((i == 0) | end, 1.0, 0.0).astype(f32)
        edge_at = 0 if p == 0 else 2

        def with_faces(v, n):
            v = v + edge * xc[edge_at + n]
            low = roll_tile(zc[...], lax.rem(256 - i - 32 * n, 128))
            high = roll_tile(zc[...], lax.rem(319 - i - 32 * n, 128))
            v = v + jnp.concatenate(
                [jnp.where(lane1 == 0, low, 0.0), jnp.where(lane1 == 127, high, 0.0)], axis=1
            )
            first = v[0:8, :] + jnp.where(ri == 0, yc[n, at, :], 0.0)
            final = v[CY - 8:CY, :] + jnp.where(ri == 7, yc[2 + n, at, :], 0.0)
            return jnp.concatenate([first, v[8:CY - 8, :], final], axis=0)

        c, l = conc_ref[p], adj_ref[p]
        sol = solid_ref[p].astype(f32)

        kv = sol * jnp.concatenate(lookups, axis=0)

        def inverse(v):
            r = pl.reciprocal(v, approx=True)
            return r * (2.0 - v * r)

        m = adjload_ref[p]
        u0 = inverse(1.0 + c)
        e0 = c * u0 - load_ref[p]
        r = kv * e0
        conc1 = with_faces(s1_ref[p], 0) - r
        load1 = load_ref[p] + r
        d1 = m - l
        u1 = inverse(1.0 + conc1)
        kd = kv * d1
        adj1 = with_faces(s2_ref[p], 1) + kd * (u1 * u1)
        m1 = m - kd
        d0 = m1 - adj1
        kd = kv * d0
        mstart_ref[p] = m1 - kd
        rest = sol * ((conc1 * u1 - load1) * d1 + e0 * d0)
        for k in range(DIGITS):
            digit = rest.astype(f8).astype(f32)
            term_f[k] = digit
            rest = (rest - digit) * 16.0
        base_ref[p] = adj1 + kd * (u0 * u0)
        adj1_ref[p] = adj1
        ly_ref[0, at, :] = adj1[0:1, :]
        ly_ref[1, at, :] = adj1[CY - 1:CY, :]
        packed_l = jnp.where(lane1 == i, adj1[:, 0:1], lz_ref[...])
        lz_ref[...] = jnp.where(lane1 == i + 32, adj1[:, CZ - 1:CZ], packed_l)

        slots = slot_ref[p]
        hi_f[...] = (slots >> 7).astype(f32)
        lo_f[...] = (slots & 127).astype(f32)

    for p in range(PLANES):
        one_plane(p)

    @pl.when(step == CX // PLANES - 1)
    def _():
        for g in range(CHUNKS):
            total[...] = total[...] + product(g)
            make_hot(g)
        for g in range(CHUNKS):
            total[...] = total[...] + product(g)
        by_lane = total[...].T
        sums = by_lane[32 * DIGITS - 32:32 * DIGITS]
        for k in range(DIGITS - 2, -1, -1):
            sums = by_lane[32 * k:32 * k + 32] + sums * (1.0 / 16.0)
        places = places_ref[...]
        high = sums.astype(bf16)
        high_f = high.astype(f32)
        low_f = sums - high_f
        place_lane = (places & 127).astype(f32)
        place_row = places >> 7
        lane_ids = lax.broadcasted_iota(i32, (128, 128), 0).astype(f32)

        row_ids = lax.broadcasted_iota(i32, (256, 128), 0).astype(f32).astype(bf16)
        row_f = place_row.astype(f32)
        ones, zeros = jnp.ones((256, 128), bf16), jnp.zeros((256, 128), bf16)

        values = []
        for s in range(32):
            match = lane_ids == place_lane[s:s + 1, :]
            values.append(
                jnp.concatenate(
                    [
                        jnp.where(match, high_f[s:s + 1, :], 0.0).astype(bf16),
                        jnp.where(match, low_f[s:s + 1, :], 0.0).astype(bf16),
                    ],
                    axis=0,
                )
            )
        value = jnp.concatenate(values, axis=1)

        def spread(n, carry):
            first = (n * 256).astype(f32)
            hot = jnp.concatenate(
                [
                    jnp.where(
                        row_ids == jnp.broadcast_to(row_f[s:s + 1, :] - first, (256, 128)).astype(bf16),
                        ones, zeros,
                    )
                    for s in range(32)
                ],
                axis=1,
            )
            got = lax.dot_general(
                hot, value, (((1,), (1,)), ((), ())), preferred_element_type=f32
            )
            dense_ref[pl.ds(pl.multiple_of(n * 256, 256), 256), :] = got[:, 0:128] + got[:, 128:256]
            return carry

        lax.fori_loop(0, 8, spread, 0)


def call_main(block, arrays, faces, home, slot_grain):
    conc, load, adj, adj_load, vx, solid, slot = arrays
    plane = pl.BlockSpec((PLANES, CY, CZ), lambda i, b: (i, 0, 0))

    def whole(shape):
        return pl.BlockSpec(shape, lambda i, b: (0,) * len(shape))

    face_shapes = [
        (3, CY, CZ), (CY, CZ), (2, CY, CZ), (CY, CZ), (4, CX, CZ), (3, CX, CZ),
        (CY, 128), (CY, 128), (3, CX, CZ), (CY, 128), (4, CX, CZ), (CY, 128), (2048, 128),
    ]
    block_shape = (CX, CY, CZ)
    out_shapes = [
        block_shape, block_shape, block_shape, (2048, 128), (2, CX, CZ), (CY, 128),
        (3, CY, CZ), (3, CX, CZ), (CY, 128),
    ]
    plane_scratch = pltpu.VMEM((CY, CZ), f32)
    return pl.pallas_call(
        main_kernel,
        out_shape=[jax.ShapeDtypeStruct(s, f32) for s in out_shapes],
        grid_spec=pltpu.PrefetchScalarGridSpec(
            num_scalar_prefetch=1,
            grid=(CX // PLANES,),
            in_specs=[plane] * 8
            + [pl.BlockSpec((1, CY, CZ), lambda i, b: (CX - 1, 0, 0))]
            + [whole(s) for s in face_shapes]
            + [
                pl.BlockSpec((1, 16, 128), lambda i, b: (b[0], 0, 0)),
                pl.BlockSpec((1, 16, 128), lambda i, b: (lax.rem(b[0] + 1, 128), 0, 0)),
                whole((32, 128)),
            ],
            out_specs=[plane] * 3 + [whole(s) for s in out_shapes[3:]],
            scratch_shapes=[
                pltpu.VMEM((2048, 128), i32), pltpu.VMEM((32, 128), i32), pltpu.VMEM((16, 128), i32),
                pltpu.VMEM((4, CY, CZ), f32), pltpu.VMEM((4, CX, CZ), f32), pltpu.VMEM((CY, 128), f32),
                plane_scratch, plane_scratch, pltpu.VMEM((DIGITS, CY, CZ), f32),
                pltpu.VMEM((128, CY * CZ), f8), pltpu.VMEM((32 * DIGITS, CY * CZ), f8),
                pltpu.VMEM((128, 32 * DIGITS), f32), pltpu.VMEM((256, 4096), f32), pltpu.VMEM((32, 128), f32),
            ],
        ),
        compiler_params=pltpu.CompilerParams(
            dimension_semantics=("arbitrary",), vmem_limit_bytes=58 << 20
        ),
        cost_estimate=pl.CostEstimate(flops=10 ** 9, bytes_accessed=25 << 20, transcendentals=0),
    )(
        block, faces[13], faces[14], conc, adj, solid, load, adj_load, slot, vx,
        *faces[:12], faces[12].reshape(2048, 128), home, home, slot_grain,
    )


def finish_kernel(
    adj1, base, solid, vx, vy, vz, dense, ly, lz, cx, cy, cz,
    out, grad,
    lb, fb, sb, vxb, vyb, vzb, qx, yc, zc,
    xlo, xhi, ylo, yhi, zlo, zhi, d1, r1, r2y, r2z, s2y, s2z, r3z, r3y,
    lsem, ssem, rsem,
):
    gx, gy, gz = (lax.axis_index(a) for a in ("gx", "gy", "gz"))
    xh, core = gx // 2, lax.rem(gx, 2)
    has = lambda cond: jnp.where(cond, 1.0, 0.0).astype(f32)
    hi_x, hi_y, hi_z = has(gx < 3), has(gy < 7), has(gz < 3)
    keep = pltpu.make_async_copy(dense.at[:, core], d1, lsem.at[0])
    keep.start()
    loads = [
        pltpu.make_async_copy(ref, buf, lsem.at[1 + k])
        for k, (ref, buf) in enumerate(
            ((adj1, lb), (base, fb), (solid, sb), (vx, vxb), (vy, vyb), (vz, vzb))
        )
    ]
    for copy in loads:
        copy.start()
    greet()
    started = []
    send = sender(started, ssem, rsem)
    first = send(dense.at[:, 1 - core], r1, {"gx": gx + 1 - 2 * core})
    faces = [
        send(adj1.at[CX - 1], xlo, {"gx": lax.rem(gx + 1, 4)}),
        send(adj1.at[0], xhi, {"gx": lax.rem(gx + 3, 4)}),
        send(ly.at[1], ylo, {"gy": lax.rem(gy + 1, 8)}),
        send(ly.at[0], yhi, {"gy": lax.rem(gy + 7, 8)}),
        send(lz, zlo, {"gz": lax.rem(gz + 1, 4)}),
        send(lz, zhi, {"gz": lax.rem(gz + 3, 4)}),
    ]
    keep.wait()
    first.wait_recv()

    def add_first(h, carry):
        for x in range(2):
            d1[x, h] = d1[x, h] + r1[x, h]
        return carry

    lax.fori_loop(0, 8, add_first, 0)
    ys = [lax.rem(gy + o, 8) for o in range(8)]
    zs = [lax.rem(gz + o, 4) for o in range(4)]
    near = [(dx, o) for dx in range(2) for o in range(8) if dx + o > 0]
    side = lambda dx: gx + dx * (2 - 4 * xh)
    half = lambda dx: xh + dx * (1 - 2 * xh)
    second = (
        [send(d1.at[:, ys[o]], r2y.at[o - 1], {"gy": ys[o]}, 6 + o) for o in range(1, 8)],
        [send(d1.at[:, :, zs[o]], r2z.at[o - 1], {"gz": zs[o]}, 13 + o) for o in range(1, 4)],
    )
    third = (
        [
            send(s2y.at[half(dx), zs[o]], r3z.at[n], {"gx": side(dx), "gz": zs[o]}, 17 + n)
            for n, (dx, o) in enumerate([p for p in near if p[1] < 4])
        ],
        [
            send(s2z.at[half(dx), ys[o]], r3y.at[n], {"gx": side(dx), "gy": ys[o]}, 24 + n)
            for n, (dx, o) in enumerate(near)
        ],
    )
    for way in range(2):
        @pl.when(core == way)
        def _():
            each(second[way], "start")

    for copy in loads:
        copy.wait()
    for copy in faces:
        copy.wait_recv()
    fb[0] = fb[0] + cx[0] * (xlo[...] - lb[0])
    fb[CX - 1] = fb[CX - 1] + cx[1] * (xhi[...] * hi_x) - cx[2] * lb[CX - 1]
    yc[0] = cy[0] * (ylo[...] - ly[0])
    yc[1] = cy[1] * (yhi[...] * hi_y) - cy[2] * ly[1]
    lane1 = lax.broadcasted_iota(i32, (CY, 128), 1)
    own, coef = lz[...], cz[...]
    zc[...] = jnp.where(
        lane1 < 32,
        coef * (pltpu.roll(zlo[...], 96, 1) - own),
        coef * (pltpu.roll(zhi[...], 32, 1) * hi_z) - pltpu.roll(coef, 96, 1) * own,
    )
    qx[...] = jnp.zeros_like(qx)

    def plane(x, carry):
        ri, li, lane = plane_iotas()
        up_y, down_y, up_z, down_z = shifts(ri, li)
        at = pl.ds(x, 1)
        nx = jnp.minimum(x + 1, CX - 1)
        inside = jnp.where(x < CX - 1, 1.0, 0.0).astype(f32)
        l, w = lb[x], weight_of(sb[x])
        a, b = pair(w, weight_of(sb[nx]) * inside, vxb[x])
        d = lb[nx] * inside - l
        lap = fb[x] + b * d - qx[...]
        qx[...] = a * d
        a, b = pair(w, up_y(w), vyb[x])
        d = up_y(l) - l
        lap = lap + b * d - down_y(a * d)
        a, b = pair(w, up_z(w), vzb[x])
        d = up_z(l) - l
        lap = lap + b * d - down_z(a * d)
        cols = zc[...]
        low = pltpu.roll(cols, lax.rem(128 - x, 128), 1)
        high = pltpu.roll(cols, 95 - x, 1)
        lap = lap + jnp.concatenate(
            [jnp.where(lane == 0, low, 0.0), jnp.where(lane == 127, high, 0.0)], axis=1
        )
        fb[x] = lap
        fb[x, 0:1, :] = lap[0:1, :] + yc[0, at, :]
        fb[x, CY - 1:CY, :] = lap[CY - 1:CY, :] + yc[1, at, :]
        return carry

    lax.fori_loop(0, 16, plane, 0)
    store = [pltpu.make_async_copy(fb.at[0:16], out.at[0:16], lsem.at[7])]
    store[0].start()
    for way in range(2):
        @pl.when(core == way)
        def _():
            each(second[way], "wait_recv")

    @pl.when(core == 0)
    def _():
        for x in range(2):
            acc = d1[x, gy]
            for o in range(7):
                acc = acc + r2y[o, x]
            s2y[x] = acc
        each(third[0], "start")

    @pl.when(core == 1)
    def _():
        for x in range(2):
            for h in range(8):
                acc = d1[x, h, gz]
                for o in range(3):
                    acc = acc + r2z[o, x, h]
                s2z[x, h] = acc
        each(third[1], "start")

    lax.fori_loop(16, CX, plane, 0)
    store.append(pltpu.make_async_copy(fb.at[16:32], out.at[16:32], lsem.at[8]))
    store[1].start()

    @pl.when(core == 0)
    def _():
        each(third[0], "wait_recv")
        acc = s2y[xh, gz]
        for n in range(7):
            acc = acc + r3z[n]
        grad[...] = acc

    @pl.when(core == 1)
    def _():
        each(third[1], "wait_recv")
        acc = s2z[xh, gy]
        for n in range(15):
            acc = acc + r3y[n]
        grad[...] = acc

    for way in range(2):
        @pl.when(core == way)
        def _():
            each(second[way], "wait_send")
            each(third[way], "wait_send")

    for copy in started:
        copy.wait_send()
    for copy in store:
        copy.wait()


def call_finish(adj1, base, solid, vx, vy, vz, dense, ly, lz, cx, cy, cz):
    vmem = pl.BlockSpec(memory_space=pltpu.VMEM)
    whole = pltpu.VMEM((CX, CY, CZ), f32)
    return pl.pallas_call(
        finish_kernel,
        out_shape=(
            jax.ShapeDtypeStruct((CX, CY, CZ), f32), jax.ShapeDtypeStruct((16, 128), f32)
        ),
        in_specs=[ANY] * 7 + [vmem] * 5,
        out_specs=(ANY, vmem),
        scratch_shapes=[
            whole, whole, pltpu.VMEM((CX, CY, CZ), i32), whole, whole, whole,
            pltpu.VMEM((CY, CZ), f32), pltpu.VMEM((2, CX, CZ), f32), pltpu.VMEM((CY, 128), f32),
            pltpu.VMEM((CY, CZ), f32), pltpu.VMEM((CY, CZ), f32),
            pltpu.VMEM((CX, CZ), f32), pltpu.VMEM((CX, CZ), f32),
            pltpu.VMEM((CY, 128), f32), pltpu.VMEM((CY, 128), f32),
            pltpu.VMEM((2, 8, 4, 16, 128), f32), pltpu.VMEM((2, 8, 4, 16, 128), f32),
            pltpu.VMEM((7, 2, 4, 16, 128), f32), pltpu.VMEM((3, 2, 8, 16, 128), f32),
            pltpu.VMEM((2, 4, 16, 128), f32), pltpu.VMEM((2, 8, 16, 128), f32),
            pltpu.VMEM((7, 16, 128), f32), pltpu.VMEM((15, 16, 128), f32),
            pltpu.SemaphoreType.DMA((9,)), pltpu.SemaphoreType.DMA((39,)),
            pltpu.SemaphoreType.DMA((39,)),
        ],
        compiler_params=pltpu.CompilerParams(
            collective_id=1, has_side_effects=True, vmem_limit_bytes=62 << 20
        ),
    )(adj1, base, solid, vx, vy, vz, dense, ly, lz, cx, cy, cz)


PARTS = 8


def hand_on_kernel(start, grad, start_out, grad_out, buf, in_sem, out_sem):
    size = CX // PARTS
    small = pltpu.make_async_copy(grad, grad_out, in_sem.at[PARTS])
    small.start()
    parts = [pl.ds(size * q, size) for q in range(PARTS)]
    ins = [pltpu.make_async_copy(start.at[p], buf.at[p], in_sem.at[q]) for q, p in enumerate(parts)]
    outs = [
        pltpu.make_async_copy(buf.at[p], start_out.at[p], out_sem.at[q]) for q, p in enumerate(parts)
    ]
    for copy in ins:
        copy.start()
    for q in range(PARTS):
        ins[q].wait()
        outs[q].start()
    for copy in outs:
        copy.wait()
    small.wait()


def hand_on(start, grad):
    return pl.pallas_call(
        hand_on_kernel,
        out_shape=(jax.ShapeDtypeStruct(start.shape, f32), jax.ShapeDtypeStruct(grad.shape, f32)),
        in_specs=[ANY] * 2,
        out_specs=[ANY] * 2,
        scratch_shapes=[
            pltpu.VMEM((CX, CY, CZ), f32), pltpu.SemaphoreType.DMA((PARTS + 1,)),
            pltpu.SemaphoreType.DMA((PARTS,)),
        ],
        compiler_params=pltpu.CompilerParams(vmem_limit_bytes=62 << 20),
    )(start, grad)


def per_device(
    conc, load, adj_conc, adj_load, vel_x, vel_y, vel_z, solid, voxel_slot, slot_grain, grain_home, rates
):
    block = (lax.axis_index("gx") * 32 + lax.axis_index("gy") * 4 + lax.axis_index("gz")).astype(i32)
    faces = call_faces(conc, adj_conc, vel_x, vel_y, vel_z, solid, rates.reshape(16, 128))
    arrays = (conc, load, adj_conc, adj_load, vel_x, solid, voxel_slot)
    adj1, base, load_start, dense, ly, lz, cx, cy, cz = call_main(
        block.reshape(1), arrays, faces, grain_home.reshape(128, 16, 128), slot_grain.reshape(32, 128)
    )
    start, grad = call_finish(
        adj1, base, solid, vel_x, vel_y, vel_z, dense.reshape(2, 2, 8, 4, 16, 128), ly, lz, cx, cy, cz
    )
    start, grad = hand_on(start, grad)
    return start, load_start, grad.reshape(2048)


def solution(mesh):
    cells = P("gx", "gy", "gz")
    every = P(("gx", "gy", "gz"))
    return jax.shard_map(
        per_device,
        mesh=mesh,
        in_specs=(cells,) * 9 + (P(("gx", "gy", "gz"), None), P(), every),
        out_specs=(cells, cells, every),
        check_vma=False,
    )
```
